32 devices in a mesh: dp: 8 (over y, x, core), tensor: 4 (over z).
Axes of the slice: x: 2, y: 2, z: 4, core: 2. Of those that a mesh axis runs over, the one named last changes fastest.
Arguments:
- tokens: bfloat16 [8, 256, 768], P('dp', 'tensor'), may hold values from -6 to 6
- condition: bfloat16 [8, 768], P('dp'), may hold values from -6 to 6
- cotangent: bfloat16 [8, 256, 768], P('dp', 'tensor'), may hold values from -6 to 6
- mod_weight: bfloat16 [2, 768, 6, 768], P(None, 'dp', None, 'tensor'), may hold values from -1 to 1
- mod_bias: bfloat16 [2, 6, 12, 64], P(None, None, 'tensor', 'dp'), may hold values from -3 to 3
- qkv_weight: bfloat16 [2, 768, 3, 768], P(None, 'dp', None, 'tensor'), may hold values from -1 to 1
- qv_bias: bfloat16 [2, 2, 12, 64], P(None, None, 'tensor', 'dp'), may hold values from -3 to 3
- out_weight: bfloat16 [2, 768, 768], P(None, 'tensor', 'dp'), may hold values from -1 to 1
- out_bias: bfloat16 [2, 12, 64], P(None, 'tensor', 'dp'), may hold values from -2 to 2
- up_weight: bfloat16 [2, 768, 3072], P(None, 'dp', 'tensor'), may hold values from -1 to 1
- up_bias: bfloat16 [2, 4, 768], P(None, 'tensor', 'dp'), may hold values from -3 to 3
- down_weight: bfloat16 [2, 3072, 768], P(None, 'tensor', 'dp'), may hold values from -1 to 1
- down_bias: bfloat16 [2, 12, 64], P(None, 'tensor', 'dp'), may hold values from -2 to 2
Outputs:
- output: bfloat16 [8, 256, 768], P('dp', 'tensor')
- grad_tokens: float32 [8, 256, 768], P('dp', 'tensor')
- grad_condition: float32 [8, 768], P('dp')
- grad_mod_weight: float32 [2, 768, 6, 768], P(None, 'dp', None, 'tensor')
- grad_mod_bias: float32 [2, 6, 12, 64], P(None, None, 'tensor', 'dp')
- grad_qkv_weight: float32 [2, 768, 3, 768], P(None, 'dp', None, 'tensor')
- grad_qv_bias: float32 [2, 2, 12, 64], P(None, None, 'tensor', 'dp')
- grad_out_weight: float32 [2, 768, 768], P(None, 'tensor', 'dp')
- grad_out_bias: float32 [2, 12, 64], P(None, 'tensor', 'dp')
- grad_up_weight: float32 [2, 768, 3072], P(None, 'dp', 'tensor')
- grad_up_bias: float32 [2, 4, 768], P(None, 'tensor', 'dp')
- grad_down_weight: float32 [2, 3072, 768], P(None, 'tensor', 'dp')
- grad_down_bias: float32 [2, 12, 64], P(None, 'tensor', 'dp')
The draws below stay inside these ranges and needn't reach their ends.
All inputs are finite; a program needn't handle non-finite values.
Results may differ from the reference program's by a relative error of at most 0.018.
Values may be sent and summed in bfloat16 or wider, within the bound.
No kernel may reach another device: no remote copies, remote signals or barrier semaphores. Data moves between devices by JAX's collectives and lax.ppermute only.
A program may use at most 128 MiB of HBM per device.

```python
import math
import jax
import jax.numpy as jnp
from jax import lax

D = 768
HEADS = 12
HD = 64
FF = 3072
S = 256
LAYERS = 2
LATENTS = 8


def clipped_normal(key, shape, scale, bound):
    values = jax.random.normal(key, shape, jnp.float32)
    return (scale * jnp.clip(values, -bound, bound)).astype(jnp.bfloat16)


def draw_condition(key, part):
    key = jax.random.fold_in(key, 11)
    return clipped_normal(key, (LATENTS, D), 1.0, 6.0)


def draw_mod_weight(key, part):
    key = jax.random.fold_in(key, 12)
    return clipped_normal(key, (LAYERS, D, 6, D), D ** (-0.5), 3.0)


def draw_mod_bias(key, part):
    key = jax.random.fold_in(key, 13)
    return clipped_normal(key, (LAYERS, 6, HEADS, HD), 0.5, 6.0)


def draw_qkv_weight(key, part):
    key = jax.random.fold_in(key, 14)
    return clipped_normal(key, (LAYERS, D, 3, D), D ** (-0.5), 3.0)


def draw_qv_bias(key, part):
    key = jax.random.fold_in(key, 15)
    return clipped_normal(key, (LAYERS, 2, HEADS, HD), 0.5, 6.0)


def draw_out_weight(key, part):
    key = jax.random.fold_in(key, 16)
    return clipped_normal(key, (LAYERS, D, D), (D // 16) ** (-0.5), 3.0)


def draw_out_bias(key, part):
    key = jax.random.fold_in(key, 17)
    return clipped_normal(key, (LAYERS, HEADS, HD), 0.3, 6.0)


def draw_up_weight(key, part):
    key = jax.random.fold_in(key, 18)
    return clipped_normal(key, (LAYERS, D, FF), D ** (-0.5), 3.0)


def draw_up_bias(key, part):
    key = jax.random.fold_in(key, 19)
    return clipped_normal(key, (LAYERS, FF // D, D), 0.5, 6.0)


def draw_down_weight(key, part):
    key = jax.random.fold_in(key, 20)
    return clipped_normal(key, (LAYERS, FF, D), FF ** (-0.5), 3.0)


def draw_down_bias(key, part):
    key = jax.random.fold_in(key, 21)
    return clipped_normal(key, (LAYERS, HEADS, HD), 0.3, 6.0)


def shard_levels(key, dims, pieces, smallest, high):
    gain = 1.0
    for axis_at, blocks in pieces:
        draws = jax.random.uniform(jax.random.fold_in(jax.random.fold_in(key, 6), axis_at), (blocks,), jnp.float32, smallest / len(pieces), high / len(pieces))
        gain = gain * jnp.repeat(jnp.exp(draws), dims[axis_at] // blocks).reshape((-1,) + (1,) * (len(dims) - 1 - axis_at))
    return gain


def bell_draw(own_key, dims, scale, most, split=(), kind=jnp.bfloat16):
    level = shard_levels(own_key, dims, split, -0.22, 0.18) if split else 1.0
    values = jax.random.normal(own_key, dims, jnp.float32) * scale * level
    return jnp.minimum(jnp.maximum(values, -most), most).astype(kind)


def setup_inputs(seed: int = 0) -> dict:
    streams_of = jax.random.split(jax.random.key(seed), 14)
    return {
        "tokens": bell_draw(streams_of[0], (LATENTS, S, D), 1.0, 6.0, ((0, 8), (1, 4))),
        "condition": draw_condition(jax.random.fold_in(streams_of[13], 71), 0),
        "cotangent": bell_draw(streams_of[2], (LATENTS, S, D), 1.0, 6.0, ((0, 8), (1, 4))),
        "mod_weight": draw_mod_weight(jax.random.fold_in(streams_of[13], 71), 0),
        "mod_bias": draw_mod_bias(jax.random.fold_in(streams_of[13], 71), 0),
        "qkv_weight": draw_qkv_weight(jax.random.fold_in(streams_of[13], 71), 0),
        "qv_bias": draw_qv_bias(jax.random.fold_in(streams_of[13], 71), 0),
        "out_weight": draw_out_weight(jax.random.fold_in(streams_of[13], 71), 0),
        "out_bias": draw_out_bias(jax.random.fold_in(streams_of[13], 71), 0),
        "up_weight": draw_up_weight(jax.random.fold_in(streams_of[13], 71), 0),
        "up_bias": draw_up_bias(jax.random.fold_in(streams_of[13], 71), 0),
        "down_weight": draw_down_weight(jax.random.fold_in(streams_of[13], 71), 0),
        "down_bias": draw_down_bias(jax.random.fold_in(streams_of[13], 71), 0),
    }


@jax.custom_vjp
def low(v):
    return lax.optimization_barrier(v.astype(jnp.bfloat16)).astype(jnp.float32)

@jax.custom_vjp
def low_back(v):
    return v

def low_keep(v):
    return (low(v), None)

def low_pass(kept, grad):
    return (grad,)

def back_keep(v):
    return (v, None)

def back_low(kept, grad):
    return (low(grad),)
low.defvjp(low_keep, low_pass)
low_back.defvjp(back_keep, back_low)
highest = lax.Precision.HIGHEST

def project(values, matrix):
    return jnp.einsum('...d,de->...e', values, matrix, precision=highest)

def normalize(values):
    centered = values - lax.optimization_barrier(jnp.mean(values, axis=-1, keepdims=True))
    return centered * lax.rsqrt(lax.optimization_barrier(jnp.mean(centered * centered, axis=-1, keepdims=True)) + 1e-06)

def one_block(residual, cond_act, weights):
    mod_weight, mod_bias, qkv_weight, qv_bias, out_weight, out_bias, up_weight, up_bias, down_weight, down_bias = weights
    group = residual.shape[0]
    modulation = low_back(project(cond_act, mod_weight.reshape(D, 6 * D)) + mod_bias.reshape(1, 6 * D))
    modulation = modulation.reshape(group, 6, 1, D)
    shift_one = modulation[:, 0]
    scale_one = modulation[:, 1]
    gate_one = modulation[:, 2]
    shift_two = modulation[:, 3]
    scale_two = modulation[:, 4]
    gate_two = modulation[:, 5]
    attn_in = low(normalize(residual) * (1.0 + scale_one) + shift_one)
    mixed_heads = project(attn_in, qkv_weight.reshape(D, 3 * D)).reshape(group, S, 3, D)
    query = low_back(low(mixed_heads[:, :, 0] + qv_bias[0].reshape(D))).reshape(group, S, HEADS, HD)
    keys = low_back(low(mixed_heads[:, :, 1])).reshape(group, S, HEADS, HD)
    values = low_back(low(mixed_heads[:, :, 2] + qv_bias[1].reshape(D))).reshape(group, S, HEADS, HD)
    scores = jnp.einsum('gqhe,gkhe->ghqk', query, keys, precision=highest) * (1.0 / math.sqrt(HD))
    scores = low_back(scores)
    probs = low(jax.nn.softmax(scores, axis=-1))
    attention_result = jnp.einsum('ghqk,gkhe->gqhe', probs, values, precision=highest).reshape(group, S, D)
    attention_result = low_back(low(attention_result))
    branch = low_back(project(attention_result, out_weight) + out_bias.reshape(D))
    middle = residual + gate_one * branch
    mlp_in = low(normalize(middle) * (1.0 + scale_two) + shift_two)
    hidden = low_back(project(mlp_in, up_weight) + up_bias.reshape(FF))
    activated_hidden = low(jax.nn.gelu(hidden, approximate=False))
    mlp_out = low_back(project(activated_hidden, down_weight) + down_bias.reshape(D))
    return middle + gate_two * mlp_out

def forward(residual, condition, weights):
    cond_act = low(jax.nn.silu(condition))
    for layer in range(LAYERS):
        residual = one_block(residual, cond_act, tuple((member[layer] for member in weights)))
    return residual

def reference(tokens, condition, cotangent, mod_weight, mod_bias, qkv_weight, qv_bias, out_weight, out_bias, up_weight, up_bias, down_weight, down_bias):
    weights = tuple((member.astype(jnp.float32) for member in (mod_weight, mod_bias, qkv_weight, qv_bias, out_weight, out_bias, up_weight, up_bias, down_weight, down_bias)))
    group = math.gcd(LATENTS, 16)
    blocks = LATENTS // group
    token_groups = tokens.astype(jnp.float32).reshape(blocks, group, S, D)
    cond_groups = condition.astype(jnp.float32).reshape(blocks, group, D)
    grad_groups = cotangent.astype(jnp.float32).reshape(blocks, group, S, D)

    def step(totals, item):
        token_part, cond_part, grad_part = item
        result, pullback = jax.vjp(forward, token_part, cond_part, weights)
        grad_token, grad_cond, grad_weights = pullback(grad_part)
        totals = jax.tree.map(jnp.add, totals, grad_weights)
        return (totals, (result, grad_token, grad_cond))
    start_totals = jax.tree.map(jnp.zeros_like, weights)
    totals, (results, grad_token, grad_cond) = lax.scan(step, start_totals, (token_groups, cond_groups, grad_groups))
    return (results.reshape(LATENTS, S, D).astype(jnp.bfloat16), grad_token.reshape(LATENTS, S, D), grad_cond.reshape(LATENTS, D), totals[0], totals[1], totals[2], totals[3], totals[4], totals[5], totals[6], totals[7], totals[8], totals[9])
```

```python
import math

import jax
import jax.numpy as jnp
from jax import lax
from jax.experimental import pallas as pl
from jax.experimental.pallas import tpu as pltpu
from jax.sharding import PartitionSpec as P

D = 768
HD = 64
EPS = 1e-06
AXES = ("dp", "tensor")
F32 = jnp.float32
BF16 = jnp.bfloat16

PARITY = 1
HALF = 2
CORE = 4
CHIP = 8


def call(kernel, out_shape, *args, flops=0, name=None):
    size = sum(a.size * a.dtype.itemsize for a in args) + sum(math.prod(o.shape) * o.dtype.itemsize for o in out_shape)
    return pl.pallas_call(
        kernel,
        out_shape=out_shape,
        in_specs=[pl.BlockSpec(memory_space=pltpu.VMEM)] * len(args),
        out_specs=[pl.BlockSpec(memory_space=pltpu.VMEM)] * len(out_shape),
        compiler_params=pltpu.CompilerParams(vmem_limit_bytes=48 * 1024 * 1024),
        cost_estimate=pl.CostEstimate(flops=flops, bytes_accessed=size, transcendentals=0),
        name=name,
    )(*args)


def sds(shape, dtype):
    return jax.ShapeDtypeStruct(shape, dtype)


def dot(a, b, ca=1, cb=0):
    return lax.dot_general(a, b, (((ca,), (cb,)), ((), ())), preferred_element_type=F32)


def normalize(values):
    centered = values - jnp.mean(values, axis=-1, keepdims=True)
    inverse = lax.rsqrt(jnp.mean(centered * centered, axis=-1, keepdims=True) + EPS)
    return centered * inverse, inverse


def norm_back(incoming, normed, inverse):
    average = jnp.mean(incoming, axis=-1, keepdims=True)
    along = jnp.mean(incoming * normed, axis=-1, keepdims=True)
    return inverse * (incoming - average - normed * along)


def col_sum(values):
    return jnp.sum(values, axis=0, keepdims=True)


def modulate(values, mod, shift, scale):
    normed, _ = normalize(values)
    return (normed * (1.0 + mod[scale : scale + 1]) + mod[shift : shift + 1]).astype(BF16)


def rows_of(refs):
    return jnp.concatenate([ref[...] for ref in refs], axis=0)


def split_out(total, keep_ref, send_ref):
    half = total.shape[0] // 2
    keep_ref[...] = total[:half]
    send_ref[...] = total[half:].astype(BF16)


def enter_kernel(res_ref, mod_ref, in_ref):
    in_ref[...] = modulate(res_ref[...], mod_ref[...], 0, 1)


def attention_kernel(x0, x1, x2, x3, w_ref, bias_ref, bo_ref, qkv_ref, att_ref, keep_ref, send_ref):
    x = rows_of((x0, x1, x2, x3))
    cols = w_ref.shape[1] // 4
    w = w_ref[...]
    qkv = (dot(x, w[:, : 3 * cols]) + bias_ref[...]).astype(BF16)
    qkv_ref[...] = qkv
    parts = []
    for head in range(cols // HD):
        at = head * HD
        q = qkv[:, at : at + HD]
        k = qkv[:, cols + at : cols + at + HD]
        v = qkv[:, 2 * cols + at : 2 * cols + at + HD]
        scores = dot(q, k, 1, 1) * (1.0 / math.sqrt(HD))
        expo = jnp.exp(scores - jnp.max(scores, axis=-1, keepdims=True))
        probs = expo / jnp.sum(expo, axis=-1, keepdims=True)
        parts.append(dot(probs.astype(BF16), v))
    att = jnp.concatenate(parts, axis=1).astype(BF16)
    att_ref[...] = att
    split_out(dot(att, w[:, 3 * cols :], 1, 1) + bo_ref[...], keep_ref, send_ref)


def middle_kernel(res_ref, mod_ref, part_ref, recv_ref, branch_ref, mid_ref, in_ref):
    mod = mod_ref[...]
    branch = part_ref[...] + recv_ref[...].astype(F32)
    branch_ref[...] = branch
    middle = res_ref[...] + mod[2:3] * branch
    mid_ref[...] = middle
    in_ref[...] = modulate(middle, mod, 3, 4)


def mlp_kernel(x0, x1, x2, x3, w_ref, bu_ref, bd_ref, hid_ref, act_ref, keep_ref, send_ref):
    x = rows_of((x0, x1, x2, x3))
    units = w_ref.shape[1] // 2
    hidden = dot(x, w_ref[:, :units]) + bu_ref[...]
    hid_ref[...] = hidden
    act = (0.5 * hidden * (1.0 + lax.erf(hidden * 0.7071067811865476))).astype(BF16)
    act_ref[...] = act
    split_out(dot(act, w_ref[:, units:], 1, 1) + bd_ref[...], keep_ref, send_ref)


def next_kernel(mid_ref, mod_ref, part_ref, recv_ref, mod_next_ref, out_ref, res_ref, in_ref):
    mlp_out = part_ref[...] + recv_ref[...].astype(F32)
    out_ref[...] = mlp_out
    residual = mid_ref[...] + mod_ref[5:6] * mlp_out
    res_ref[...] = residual
    in_ref[...] = modulate(residual, mod_next_ref[...], 0, 1)


def last_kernel(mid_ref, mod_ref, part_ref, recv_ref, g_ref, out_ref, dmlp_ref, dgate_ref):
    mlp_out = part_ref[...] + recv_ref[...].astype(F32)
    out_ref[...] = (mid_ref[...] + mod_ref[5:6] * mlp_out).astype(BF16)
    g = g_ref[...].astype(F32)
    dmlp_ref[...] = (g * mod_ref[5:6]).astype(BF16)
    dgate_ref[...] = col_sum(g * mlp_out)


def mlp_back_kernel(x0, x1, x2, x3, w_ref, hid_ref, dhid_ref, keep_ref, send_ref):
    x = rows_of((x0, x1, x2, x3))
    units = w_ref.shape[1] // 2
    hidden = hid_ref[...]
    d_active = dot(x, w_ref[:, units:])
    cumulative = 0.5 * (1.0 + lax.erf(hidden * 0.7071067811865476))
    density = jnp.exp(-0.5 * hidden * hidden) * 0.3989422804014327
    d_hidden = (d_active * (cumulative + hidden * density)).astype(BF16)
    dhid_ref[...] = d_hidden
    split_out(dot(d_hidden, w_ref[:, :units], 1, 1), keep_ref, send_ref)


def mlp_grad_kernel(y0, y1, y2, y3, x0, x1, x2, x3, dhid_ref, act_ref, grad_ref, bu_ref, bd_ref):
    y = rows_of((y0, y1, y2, y3))
    x = rows_of((x0, x1, x2, x3))
    units = act_ref.shape[1]
    d_hidden = dhid_ref[...]
    grad_ref[:, :units] = dot(x, d_hidden, 0, 0).astype(BF16)
    grad_ref[:, units:] = dot(y, act_ref[...], 0, 0).astype(BF16)
    bu_ref[...] = col_sum(d_hidden.astype(F32))
    bd_ref[...] = col_sum(y.astype(F32))


def middle_back_kernel(g_ref, mod_ref, part_ref, recv_ref, mid_ref, branch_ref, dmid_ref, dbranch_ref, sums_ref):
    mod = mod_ref[...]
    incoming = part_ref[...] + recv_ref[...].astype(F32)
    normed, inverse = normalize(mid_ref[...])
    d_middle = g_ref[...].astype(F32) + norm_back(incoming * (1.0 + mod[4:5]), normed, inverse)
    dmid_ref[...] = d_middle
    dbranch_ref[...] = (d_middle * mod[2:3]).astype(BF16)
    sums_ref[...] = jnp.concatenate(
        [col_sum(d_middle * branch_ref[...]), col_sum(incoming), col_sum(incoming * normed)], axis=0
    )


def attention_back_kernel(x0, x1, x2, x3, w_ref, qkv_ref, dqkv_ref, keep_ref, send_ref):
    x = rows_of((x0, x1, x2, x3))
    cols = w_ref.shape[1] // 4
    w = w_ref[...]
    qkv = qkv_ref[...]
    scaling = 1.0 / math.sqrt(HD)
    d_att = dot(x, w[:, 3 * cols :]).astype(BF16)
    grads = ([], [], [])
    for head in range(cols // HD):
        at = head * HD
        q = qkv[:, at : at + HD]
        k = qkv[:, cols + at : cols + at + HD]
        v = qkv[:, 2 * cols + at : 2 * cols + at + HD]
        d_out = d_att[:, at : at + HD]
        scores = dot(q, k, 1, 1) * scaling
        expo = jnp.exp(scores - jnp.max(scores, axis=-1, keepdims=True))
        probs = expo / jnp.sum(expo, axis=-1, keepdims=True)
        d_probs = dot(d_out, v, 1, 1)
        d_scores = (probs * (d_probs - jnp.sum(probs * d_probs, axis=-1, keepdims=True))).astype(BF16)
        grads[0].append(dot(d_scores, k) * scaling)
        grads[1].append(dot(d_scores, q, 0, 0) * scaling)
        grads[2].append(dot(probs.astype(BF16), d_out, 0, 0))
    d_qkv = jnp.concatenate(grads[0] + grads[1] + grads[2], axis=1).astype(BF16)
    dqkv_ref[...] = d_qkv
    split_out(dot(d_qkv, w[:, : 3 * cols], 1, 1), keep_ref, send_ref)


def attention_grad_kernel(y0, y1, y2, y3, x0, x1, x2, x3, dqkv_ref, att_ref, grad_ref, bqkv_ref, bo_ref):
    y = rows_of((y0, y1, y2, y3))
    x = rows_of((x0, x1, x2, x3))
    cols = att_ref.shape[1]
    d_qkv = dqkv_ref[...]
    grad_ref[...] = jnp.concatenate([dot(x, d_qkv, 0, 0), dot(y, att_ref[...], 0, 0)], axis=1).astype(BF16)
    bqkv_ref[...] = col_sum(d_qkv.astype(F32))
    bo_ref[...] = col_sum(y.astype(F32))


def enter_back(dmid_ref, mod_ref, part_ref, recv_ref, res_ref):
    incoming = part_ref[...] + recv_ref[...].astype(F32)
    normed, inverse = normalize(res_ref[...])
    g = dmid_ref[...] + norm_back(incoming * (1.0 + mod_ref[1:2]), normed, inverse)
    return g, col_sum(incoming), col_sum(incoming * normed)


def enter_back_kernel(dmid_ref, mod_ref, part_ref, recv_ref, res_ref, g_ref, sums_ref):
    g, shift, scale = enter_back(dmid_ref, mod_ref, part_ref, recv_ref, res_ref)
    g_ref[...] = g
    sums_ref[...] = jnp.concatenate([shift, scale], axis=0)


def previous_kernel(
    dmid_ref, mod_ref, part_ref, recv_ref, res_ref, mod_prev_ref, out_prev_ref, g_ref, sums_ref, dmlp_ref, dgate_ref
):
    g, shift, scale = enter_back(dmid_ref, mod_ref, part_ref, recv_ref, res_ref)
    g_ref[...] = g
    sums_ref[...] = jnp.concatenate([shift, scale], axis=0)
    dmlp_ref[...] = (g * mod_prev_ref[5:6]).astype(BF16)
    dgate_ref[...] = col_sum(g * out_prev_ref[...])


def body(
    tokens,
    condition,
    cotangent,
    mod_weight,
    mod_bias,
    qkv_weight,
    qv_bias,
    out_weight,
    out_bias,
    up_weight,
    up_bias,
    down_weight,
    down_bias,
):
    layers = mod_weight.shape[0]
    n_dp = lax.axis_size("dp")
    n_chips = n_dp // 2
    n_all = n_dp * 4
    dp = lax.axis_index("dp")
    z = lax.axis_index("tensor")
    chip = dp // 2
    core = dp % 2
    half = z // 2
    quarter = 2 * (half ^ core) + z % 2
    cols = mod_weight.shape[3]
    rows = tokens.shape[1]
    shard = qkv_weight.shape[1]
    units = up_weight.shape[2]
    piece = qv_bias.shape[3]

    def move(values, target):
        return lax.ppermute(values, AXES, [(i, target(i)) for i in range(n_all)])

    def xor(values, mask):
        return move(values, lambda i: i ^ mask)

    def swap_core_half(i):
        return i & ~6 | (i & HALF) << 1 | (i & CORE) >> 1

    def to_other(i):
        return i ^ CORE if i & CORE else i ^ CORE ^ HALF

    def from_other(i):
        return i ^ CORE ^ HALF if i & CORE else i ^ CORE

    def to_same(i):
        return i ^ HALF if i & CORE else i

    def pick(values, index):
        return lax.dynamic_index_in_dim(values, index, 0, keepdims=False)

    def chip_gather(values):
        if n_chips > 8:
            groups = [[2 * i + c for i in range(n_chips)] for c in range(2)]
            return lax.all_gather(values, "dp", axis_index_groups=groups)
        out = jnp.zeros((n_chips,) + values.shape, values.dtype)
        for j in range(n_chips):
            got = xor(values, CHIP * j) if j else values
            out = lax.dynamic_update_index_in_dim(out, got, chip ^ j, 0)
        return out

    def chip_swap(values):
        if n_chips > 8:
            groups = [[2 * i + c for i in range(n_chips)] for c in range(2)]
            got = lax.all_to_all(values, "dp", 0, 0, axis_index_groups=groups, tiled=True)
            return [got[i] for i in range(n_chips)]
        return [xor(pick(values, chip ^ j), CHIP * j) if j else pick(values, chip) for j in range(n_chips)]

    def chip_sum(values):
        return sum(part.astype(F32) for part in chip_swap(values))

    def fetch(own):
        same = move(own, to_same)
        other = move(own, to_other)
        pair = jnp.where(core == 0, jnp.stack([same, other]), jnp.stack([other, same]))
        return chip_gather(pair)

    def give(total):
        low = chip_sum(total).astype(BF16)
        same = move(pick(low, core), to_same)
        other = move(pick(low, core ^ 1), from_other)
        return same.astype(F32) + other.astype(F32)

    def all_rows(values):
        other = xor(values, PARITY)
        return (values, other, xor(values, CORE), xor(other, CORE))

    def sum_rows(keep, send):
        total = keep + xor(send, CORE).astype(F32)
        return total[:rows], xor(total[rows:].astype(BF16), PARITY)

    cond_full = condition.astype(F32)
    cond_act = jax.nn.silu(cond_full).astype(BF16)
    cond_other = xor(cond_act, CORE)
    cond_pair = jnp.where(core == 0, jnp.stack([cond_act, cond_other]), jnp.stack([cond_other, cond_act]))
    cond_every = chip_gather(cond_pair).reshape(n_dp, D)
    cond_slice = lax.dynamic_slice_in_dim(cond_every, dp * shard, shard, 1)
    bias_at = lax.dynamic_update_slice(
        jnp.zeros((layers, 6, cols // HD, HD), F32), mod_bias.astype(F32), (0, 0, 0, dp * piece)
    ).reshape(layers, 6, cols)
    partial_mod = jnp.einsum("ld,ydkc->lykc", cond_slice, mod_weight, preferred_element_type=F32) + bias_at
    mod_sum = chip_sum(partial_mod.reshape((n_chips, 2) + partial_mod.shape[1:]))
    mod_sum = mod_sum + xor(mod_sum, CORE)
    mod_own = pick(mod_sum, half)
    mod_far = pick(mod_sum, half ^ 1)
    modulation = jnp.zeros((4,) + mod_own.shape, F32)
    for mask in range(4):
        got = xor(mod_far if mask & HALF else mod_own, mask) if mask else mod_own
        modulation = lax.dynamic_update_index_in_dim(modulation, got, z ^ mask, 0)
    modulation = jnp.transpose(modulation, (1, 2, 0, 3)).reshape(layers, 6, D)

    moved = move(jnp.concatenate([tokens[0], cotangent[0]]), swap_core_half)
    residual = moved[:rows].astype(F32)
    cotan = moved[rows:]

    bias_len = 12 * piece + up_bias.shape[2]
    bias_vec = jnp.concatenate(
        [
            qv_bias.reshape(layers, 6 * piece),
            out_bias.reshape(layers, 3 * piece),
            down_bias.reshape(layers, 3 * piece),
            up_bias.reshape(layers, -1),
        ],
        axis=1,
    )
    bias_block = lax.dynamic_update_slice(jnp.zeros((16, D), BF16), bias_vec, (0, 0))
    attention_weights = []
    mlp_weights = []
    for layer in range(layers):
        own = jnp.concatenate([qkv_weight[layer].reshape(shard, 3 * cols), out_weight[layer].T], axis=1)
        if layer == 0:
            got = fetch(jnp.concatenate([own, bias_block])).reshape(n_dp, shard + 16, 4 * cols)
            bias_every = got[:, shard : shard + layers, :bias_len].astype(F32)
            attention_weights.append(got[:, :shard].reshape(D, 4 * cols))
        else:
            attention_weights.append(fetch(own).reshape(D, 4 * cols))
        own = jnp.concatenate([up_weight[layer], down_weight[layer].T], axis=1)
        mlp_weights.append(fetch(own).reshape(D, 2 * units))

    def heads_of(values, count):
        return jnp.transpose(values.reshape(n_dp, layers, count, 3, piece), (1, 2, 3, 0, 4)).reshape(layers, count, cols)

    head_bias = heads_of(bias_every[:, :, : 12 * piece], 4)
    qkv_bias_all = jnp.concatenate([head_bias[:, :1], jnp.zeros_like(head_bias[:, :1]), head_bias[:, 1:2]], axis=1)
    qkv_bias_all = qkv_bias_all.reshape(layers, 1, 3 * cols)
    wide_bias = lax.dynamic_update_slice(jnp.zeros((layers, 2, D), F32), head_bias[:, 2:4], (0, 0, quarter * cols))
    up_bias_all = jnp.transpose(bias_every[:, :, 12 * piece :], (1, 0, 2)).reshape(layers, 1, units)

    full = 4 * rows
    keep_send = [sds((full // 2, D), F32), sds((full // 2, D), BF16)]
    row_f32 = sds((rows, D), F32)
    row_bf16 = sds((rows, D), BF16)
    line = sds((1, D), F32)
    attention_flops = 2 * full * D * 4 * cols + 4 * full * full * cols
    mlp_flops = 4 * full * D * units

    saved = []
    (attn_in,) = call(enter_kernel, [row_bf16], residual, modulation[0], name="enter")
    for layer in range(layers):
        mod = modulation[layer]
        attn_rows = all_rows(attn_in)
        qkv, att, keep, send = call(
            attention_kernel,
            [sds((full, 3 * cols), BF16), sds((full, cols), BF16)] + keep_send,
            *attn_rows,
            attention_weights[layer],
            qkv_bias_all[layer],
            wide_bias[layer, :1],
            flops=attention_flops,
            name="attention",
        )
        branch, middle, mlp_in = call(
            middle_kernel, [row_f32, row_f32, row_bf16], residual, mod, *sum_rows(keep, send), name="middle"
        )
        mlp_rows = all_rows(mlp_in)
        hidden, act, keep, send = call(
            mlp_kernel,
            [sds((full, units), F32), sds((full, units), BF16)] + keep_send,
            *mlp_rows,
            mlp_weights[layer],
            up_bias_all[layer],
            wide_bias[layer, 1:],
            flops=mlp_flops,
            name="mlp",
        )
        part, recv = sum_rows(keep, send)
        saved.append((residual, attn_rows, qkv, att, branch, middle, mlp_rows, hidden, act))
        if layer + 1 < layers:
            mlp_out, residual, attn_in = call(
                next_kernel,
                [row_f32, row_f32, row_bf16],
                middle,
                mod,
                part,
                recv,
                modulation[layer + 1],
                name="next",
            )
            saved[-1] += (mlp_out,)
        else:
            output, d_mlp, d_gate_two = call(
                last_kernel, [row_bf16, row_bf16, line], middle, mod, part, recv, cotan, name="last"
            )

    output = move(output, swap_core_half)[None]
    flow = cotan
    mod_lines = [None] * layers
    packs = [None] * layers
    for layer in reversed(range(layers)):
        residual, attn_rows, qkv, att, branch, middle, mlp_rows, hidden, act = saved[layer][:9]
        mod = modulation[layer]
        d_mlp_rows = all_rows(d_mlp)
        d_hidden, keep, send = call(
            mlp_back_kernel,
            [sds((full, units), BF16)] + keep_send,
            *d_mlp_rows,
            mlp_weights[layer],
            hidden,
            flops=mlp_flops,
            name="mlp_back",
        )
        part, recv = sum_rows(keep, send)
        grad_mlp, grad_up_b, grad_down_b = call(
            mlp_grad_kernel,
            [sds((D, 2 * units), BF16), sds((1, units), F32), line],
            *d_mlp_rows,
            *mlp_rows,
            d_hidden,
            act,
            flops=mlp_flops,
            name="mlp_grad",
        )
        d_middle, d_branch, sums_mid = call(
            middle_back_kernel,
            [row_f32, row_bf16, sds((3, D), F32)],
            flow,
            mod,
            part,
            recv,
            middle,
            branch,
            name="middle_back",
        )
        d_branch_rows = all_rows(d_branch)
        d_qkv, keep, send = call(
            attention_back_kernel,
            [sds((full, 3 * cols), BF16)] + keep_send,
            *d_branch_rows,
            attention_weights[layer],
            qkv,
            flops=attention_flops * 2,
            name="attention_back",
        )
        part, recv = sum_rows(keep, send)
        grad_att, grad_qkv_b, grad_out_b = call(
            attention_grad_kernel,
            [sds((D, 4 * cols), BF16), sds((1, 3 * cols), F32), line],
            *d_branch_rows,
            *attn_rows,
            d_qkv,
            att,
            flops=attention_flops,
            name="attention_grad",
        )
        if layer:
            flow, sums_in, d_mlp, gate_next = call(
                previous_kernel,
                [row_f32, sds((2, D), F32), row_bf16, line],
                d_middle,
                mod,
                part,
                recv,
                residual,
                modulation[layer - 1],
                saved[layer - 1][9],
                name="previous",
            )
        else:
            flow, sums_in = call(
                enter_back_kernel,
                [row_f32, sds((2, D), F32)],
                d_middle,
                mod,
                part,
                recv,
                residual,
                name="enter_back",
            )
            gate_next = None
        mod_lines[layer] = jnp.concatenate([sums_in, sums_mid, d_gate_two], axis=0)
        d_gate_two = gate_next

        wide = lax.dynamic_slice(jnp.concatenate([grad_out_b, grad_down_b]), (0, quarter * cols), (2, cols))
        grad_heads = jnp.concatenate([grad_qkv_b[:, :cols], grad_qkv_b[:, 2 * cols :], wide])
        grad_heads = jnp.transpose(grad_heads.reshape(4, 3, n_dp, piece), (2, 0, 1, 3)).reshape(n_dp, 12 * piece)
        grad_vec = jnp.concatenate([grad_heads, grad_up_b.reshape(n_dp, -1)], axis=1).astype(BF16)
        grad_vec = jnp.pad(grad_vec[:, None], ((0, 0), (0, 15), (0, D - bias_len)))
        pack = jnp.concatenate([grad_att.reshape(n_dp, shard, 4 * cols), grad_vec], axis=1)
        packs[layer] = (
            give(pack.reshape(n_chips, 2, shard + 16, 4 * cols)),
            give(grad_mlp.reshape(n_chips, 2, shard, 2 * units)),
        )

    d_mod = jnp.stack(mod_lines)
    d_mod = d_mod + xor(d_mod, CORE)
    d_mod = (d_mod + xor(d_mod, PARITY)).astype(BF16).reshape(layers * 6, 4, cols)
    d_mod = jnp.transpose(d_mod, (1, 0, 2))
    mine = pick(d_mod, z)
    far = xor(pick(d_mod, z ^ HALF), HALF)
    d_mod_pair = jnp.where(half == 0, jnp.stack([mine, far]), jnp.stack([far, mine]))
    d_mod_every = chip_gather(d_mod_pair).reshape(n_dp, layers, 6, cols)
    grad_mod_w = jnp.einsum("ld,lykc->ydkc", cond_slice, d_mod_every, preferred_element_type=F32)
    grad_mod_b = jnp.sum(d_mod_every.astype(F32), axis=0).reshape(layers, 6, cols // HD, HD)
    grad_mod_b = lax.dynamic_slice_in_dim(grad_mod_b, dp * piece, piece, 3)
    cond_pieces = jnp.einsum("lykc,ydkc->ld", d_mod_every, mod_weight, preferred_element_type=F32)
    cond_pieces = jnp.stack(chip_swap(cond_pieces.reshape(n_chips, 2, shard)), axis=1)
    if n_chips <= 8:
        source = chip ^ jnp.arange(n_chips)
        cond_pieces = jnp.take(cond_pieces, source, axis=1)
    cond_mine = pick(cond_pieces, core)
    cond_sent = xor(pick(cond_pieces, core ^ 1), CORE)
    cond_total = jnp.where(
        core == 0, jnp.stack([cond_mine, cond_sent], axis=1), jnp.stack([cond_sent, cond_mine], axis=1)
    ).reshape(1, D)
    cond_total = cond_total + xor(cond_total, PARITY)
    cond_total = cond_total + xor(cond_total, HALF)
    sigmoid_cond = jax.nn.sigmoid(cond_full)
    grad_condition = cond_total * sigmoid_cond * (1.0 + cond_full * (1.0 - sigmoid_cond))

    grad_tokens = move(flow, swap_core_half)[None]
    att_pack = jnp.stack([packs[layer][0] for layer in range(layers)])
    mlp_pack = jnp.stack([packs[layer][1] for layer in range(layers)])
    vec = att_pack[:, shard, :bias_len]
    vec_heads = vec[:, : 12 * piece].reshape(layers, 4, 3, piece)
    return (
        output,
        grad_tokens,
        grad_condition,
        grad_mod_w,
        grad_mod_b,
        att_pack[:, :shard, : 3 * cols].reshape(layers, shard, 3, cols),
        vec_heads[:, :2],
        jnp.transpose(att_pack[:, :shard, 3 * cols :], (0, 2, 1)),
        vec_heads[:, 2],
        mlp_pack[:, :, :units],
        vec[:, 12 * piece :].reshape(layers, 1, -1),
        jnp.transpose(mlp_pack[:, :, units:], (0, 2, 1)),
        vec_heads[:, 3],
    )


def solution(mesh):
    in_specs = (
        P("dp", "tensor", None),
        P("dp", None),
        P("dp", "tensor", None),
        P(None, "dp", None, "tensor"),
        P(None, None, "tensor", "dp"),
        P(None, "dp", None, "tensor"),
        P(None, None, "tensor", "dp"),
        P(None, "tensor", "dp"),
        P(None, "tensor", "dp"),
        P(None, "dp", "tensor"),
        P(None, "tensor", "dp"),
        P(None, "tensor", "dp"),
        P(None, "tensor", "dp"),
    )
    out_specs = (
        P("dp", "tensor", None),
        P("dp", "tensor", None),
        P("dp", None),
        P(None, "dp", None, "tensor"),
        P(None, None, "tensor", "dp"),
        P(None, "dp", None, "tensor"),
        P(None, None, "tensor", "dp"),
        P(None, "tensor", "dp"),
        P(None, "tensor", "dp"),
        P(None, "dp", "tensor"),
        P(None, "tensor", "dp"),
        P(None, "tensor", "dp"),
        P(None, "tensor", "dp"),
    )
    return jax.shard_map(body, mesh=mesh, in_specs=in_specs, out_specs=out_specs, check_vma=False)
```

```python
import functools
import math

import jax
import jax.numpy as jnp
from jax import lax
from jax.experimental import pallas as pl
from jax.experimental.pallas import tpu as pltpu
from jax.sharding import PartitionSpec as P

D = 768
HD = 64
EPS = 1e-06
AXES = ("dp", "tensor")
F32 = jnp.float32
BF16 = jnp.bfloat16
VMEM_LIMIT = 16 * 1024 * 1024

PARITY = 1
HALF = 2
CORE = 4
CHIP = 8


class Stored:
    def __init__(self, source, target, sem, local):
        self.copy = pltpu.make_async_copy(source, target, sem)
        self.local = local
        self.shape = local.shape
        self.busy = False
        self.dirty = False

    def start(self):
        self.copy.start()
        self.busy = True
        self.dirty = False

    def settle(self):
        if self.busy:
            self.copy.wait()
            self.busy = False

    def __getitem__(self, index):
        self.settle()
        return self.local[index]

    def __setitem__(self, index, value):
        self.local[index] = value
        self.dirty = True
        if index is Ellipsis:
            self.start()


def call(
    kernel, out_shape, *args, flops=0, name=None, scalars=None, after=(), scratch=(), stored=(), kept=(), window=()
):
    size = sum(a.size * a.dtype.itemsize for a in args) + sum(math.prod(o.shape) * o.dtype.itemsize for o in out_shape)
    hbm = pl.BlockSpec(memory_space=pltpu.HBM)
    vmem = pl.BlockSpec(memory_space=pltpu.VMEM)
    in_specs = [hbm if i in stored else vmem for i in range(len(args))]
    out_specs = [hbm if i in kept else vmem for i in range(len(out_shape))]
    window = dict(window)
    copies = [pltpu.VMEM((args[i].shape[0], window[i][1]) if i in window else args[i].shape, args[i].dtype) for i in stored]
    copies += [pltpu.VMEM(out_shape[i].shape, out_shape[i].dtype) for i in kept]
    lead = 0
    if after:
        args = (gate(args[0], *after),) + args[1:]
    if scalars is not None:
        args = (scalars,) + args
        in_specs = [pl.BlockSpec(memory_space=pltpu.SMEM)] + in_specs
        lead = 1

    def run(*refs):
        ins = list(refs[: len(args)])
        outs = list(refs[len(args) : len(args) + len(out_shape)])
        rest = refs[len(args) + len(out_shape) :]
        own, local = rest[: len(scratch)], rest[len(scratch) :]
        held = []
        for n, i in enumerate(stored):
            source = ins[lead + i].at[:, pl.ds(*window[i])] if i in window else ins[lead + i]
            held.append(Stored(source, local[n], local[-1].at[n], local[n]))
            held[-1].start()
            ins[lead + i] = held[-1]
        for n, i in enumerate(kept, len(stored)):
            held.append(Stored(local[n], outs[i], local[-1].at[n], local[n]))
            outs[i] = held[-1]
        kernel(*ins, *outs, *own)
        for item in held:
            if item.dirty:
                item.start()
        for item in held:
            item.settle()

    return pl.pallas_call(
        run,
        out_shape=out_shape,
        in_specs=in_specs,
        out_specs=out_specs,
        scratch_shapes=list(scratch) + copies + ([pltpu.SemaphoreType.DMA((len(copies),))] if copies else []),
        compiler_params=pltpu.CompilerParams(vmem_limit_bytes=VMEM_LIMIT),
        cost_estimate=pl.CostEstimate(flops=flops, bytes_accessed=size, transcendentals=0),
        name=name,
    )(*args)


def gate(value, *others):
    return lax.optimization_barrier((value,) + others)[0]


def place_parts(kernel, out_shape, *args, scalars, name, copies):
    count = len(args)

    def run(place_ref, *refs):
        outs = refs[count : count + len(out_shape)]
        sems = refs[-1]
        moves = [
            pltpu.make_async_copy(source, target, sems.at[n])
            for n, (source, target) in enumerate(kernel(place_ref, refs[:count], outs))
        ]
        for item in moves:
            item.start()
        for item in moves:
            item.wait()

    size = sum(a.size * a.dtype.itemsize for a in args)
    return pl.pallas_call(
        run,
        out_shape=out_shape,
        in_specs=[pl.BlockSpec(memory_space=pltpu.SMEM)]
        + [pl.BlockSpec(memory_space=pltpu.HBM)] * count,
        out_specs=[pl.BlockSpec(memory_space=pltpu.HBM)] * len(out_shape),
        scratch_shapes=[pltpu.SemaphoreType.DMA((copies,))],
        compiler_params=pltpu.CompilerParams(vmem_limit_bytes=VMEM_LIMIT),
        cost_estimate=pl.CostEstimate(flops=0, bytes_accessed=2 * size, transcendentals=0),
        name=name,
    )(scalars, *args)


def sds(shape, dtype):
    return jax.ShapeDtypeStruct(shape, dtype)


def dot(a, b, ca=1, cb=0):
    return lax.dot_general(a, b, (((ca,), (cb,)), ((), ())), preferred_element_type=F32)


def normalize(values):
    centered = values - jnp.mean(values, axis=-1, keepdims=True)
    inverse = lax.rsqrt(jnp.mean(centered * centered, axis=-1, keepdims=True) + EPS)
    return centered * inverse, inverse


def norm_back(incoming, normed, inverse):
    average = jnp.mean(incoming, axis=-1, keepdims=True)
    along = jnp.mean(incoming * normed, axis=-1, keepdims=True)
    return inverse * (incoming - average - normed * along)


def col_sum(values):
    return jnp.sum(values, axis=0, keepdims=True)


def modulate(values, mod, shift, scale):
    normed, _ = normalize(values)
    return (normed * (1.0 + mod[scale : scale + 1]) + mod[shift : shift + 1]).astype(BF16)


def rows_of(refs):
    return jnp.concatenate([ref[...] for ref in refs], axis=0)


def split_out(total, keep_ref, near_ref, send_ref):
    quarter = total.shape[0] // 4
    keep_ref[...] = total[:quarter]
    near_ref[...] = total[quarter : 2 * quarter]
    send_ref[...] = total[2 * quarter :].astype(BF16)


def summed(keep_ref, core_ref, far_ref):
    return keep_ref[...] + core_ref[: keep_ref.shape[0]].astype(F32) + far_ref[...].astype(F32)


def attention_pack(qkv_ref, out_ref):
    out = out_ref[...].astype(F32).T.astype(BF16)
    return jnp.concatenate([qkv_ref[0], qkv_ref[1], qkv_ref[2], out], axis=1)


def pack_block_kernel(qkv_ref, out_ref, up_ref, down_ref, pack_ref):
    wide = 4 * out_ref.shape[0]
    units = up_ref.shape[1]
    pack_ref[:, :wide] = attention_pack(qkv_ref, out_ref)
    pack_ref[:, wide : wide + units] = up_ref[...]
    pack_ref[:, wide + units :] = down_ref[...]


def pack_first_kernel(qkv_ref, out_ref, bias_ref, pack_ref):
    shard = out_ref.shape[1]
    pack_ref[:shard] = attention_pack(qkv_ref, out_ref)
    pack_ref[shard:] = bias_ref[...]


def pack_mlp_kernel(up_ref, down_ref, pack_ref):
    units = up_ref.shape[1]
    pack_ref[:, :units] = up_ref[...]
    pack_ref[:, units:] = down_ref[...]


def join_moves(place_ref, ins, outs):
    shard = outs[0].shape[2]
    moves = []
    for j, part in enumerate(ins):
        at = place_ref[0] ^ j
        moves.append((part.at[:, :shard], outs[0].at[at]))
        if len(outs) == 2:
            moves.append((part.at[:, shard:], outs[1].at[at]))
    return moves


def assemble_kernel(place_ref, *refs):
    parts, out_ref = refs[:-1], refs[-1]
    cols = parts[0].shape[2]
    for layer in range(out_ref.shape[0]):
        for at in range(4):
            quarter = sum(
                jnp.where(place_ref[3] ^ mask == at, part[layer], 0.0) for mask, part in enumerate(parts)
            )
            out_ref[layer, :, at * cols : (at + 1) * cols] = quarter


def spread_kernel(place_ref, *refs):
    parts, out_ref = refs[:-1], refs[-1]
    for j, part in enumerate(parts):
        out_ref[place_ref[0] ^ j] = part[...]


def couple_kernel(place_ref, own_ref, other_ref, *out_refs):
    first = place_ref[1] == 0
    at = 0
    for out_ref in out_refs:
        end = at + out_ref.shape[-1]
        own, other = own_ref[..., at:end], other_ref[..., at:end]
        out_ref[0] = jnp.where(first, own, other)
        out_ref[1] = jnp.where(first, other, own)
        at = end


def head_select(n_dp, piece, cols):
    row = lax.broadcasted_iota(jnp.int32, (3 * piece, cols), 0)
    col = lax.broadcasted_iota(jnp.int32, (3 * piece, cols), 1)
    return (row == col // HD * piece + col % piece).astype(F32)


def head_mask(n_dp, piece, cols):
    row = lax.broadcasted_iota(jnp.int32, (n_dp, cols), 0)
    col = lax.broadcasted_iota(jnp.int32, (n_dp, cols), 1)
    return (col % HD // piece == row).astype(F32)


def exact(a, b):
    return lax.dot_general(
        a, b, (((1,), (0,)), ((), ())), preferred_element_type=F32, precision=lax.Precision.HIGHEST
    )


def heads_back(line, at, n_dp, length):
    cols, piece = line.shape[1], HD // n_dp
    row = lax.broadcasted_iota(jnp.int32, (length, cols), 0) - at
    col = lax.broadcasted_iota(jnp.int32, (length, cols), 1)
    select = (row == col // HD * piece + col % piece).astype(F32)
    return lax.dot_general(
        head_mask(n_dp, piece, cols) * line,
        select,
        (((1,), (1,)), ((), ())),
        preferred_element_type=F32,
        precision=lax.Precision.HIGHEST,
    )


def units_back(line, at, n_dp, length):
    units = line.shape[1]
    width = units // n_dp
    row = lax.broadcasted_iota(jnp.int32, (length, units), 0) - at
    col = lax.broadcasted_iota(jnp.int32, (length, units), 1)
    mask = (
        lax.broadcasted_iota(jnp.int32, (n_dp, units), 1) // width
        == lax.broadcasted_iota(jnp.int32, (n_dp, units), 0)
    )
    return lax.dot_general(
        mask.astype(F32) * line,
        (col % width == row).astype(F32),
        (((1,), (1,)), ((), ())),
        preferred_element_type=F32,
        precision=lax.Precision.HIGHEST,
    )


def own_quarter(line, cols, place_ref):
    return sum(
        jnp.where(place_ref[2] == i, line[:, i * cols : (i + 1) * cols], 0.0) for i in range(line.shape[1] // cols)
    )


def bias_kernel(place_ref, vec_ref, qkv_ref, wide_ref, up_ref):
    n_dp, piece = vec_ref.shape[0] // 16, HD * 16 // vec_ref.shape[0]
    vec_row = lax.broadcasted_iota(jnp.int32, (n_dp, vec_ref.shape[0]), 0)
    vec_col = lax.broadcasted_iota(jnp.int32, (n_dp, vec_ref.shape[0]), 1)
    cols, units = qkv_ref.shape[2] // 3, up_ref.shape[2]
    select, mask = head_select(n_dp, piece, cols), head_mask(n_dp, piece, cols)
    width = units // n_dp
    row = lax.broadcasted_iota(jnp.int32, (width, units), 0)
    col = lax.broadcasted_iota(jnp.int32, (width, units), 1)
    up_select = (col % width == row).astype(F32)
    up_row = lax.broadcasted_iota(jnp.int32, (n_dp, units), 0)
    up_col = lax.broadcasted_iota(jnp.int32, (n_dp, units), 1)
    up_mask = (up_col // width == up_row).astype(F32)
    quarters = wide_ref.shape[2] // cols
    place = lax.broadcasted_iota(jnp.int32, (1, quarters * cols), 1) // cols == place_ref[2]
    for layer in range(qkv_ref.shape[0]):
        vec = dot((vec_col == 16 * vec_row + layer).astype(BF16), vec_ref[...])
        heads = [col_sum(exact(vec[:, 3 * t * piece : 3 * (t + 1) * piece], select) * mask) for t in range(4)]
        qkv_ref[layer] = jnp.concatenate([heads[0], jnp.zeros_like(heads[0]), heads[1]], axis=1)
        for t in range(2):
            wide_ref[layer, t : t + 1] = jnp.where(place, jnp.concatenate([heads[2 + t]] * quarters, axis=1), 0.0)
        up_ref[layer] = col_sum(exact(vec[:, 12 * piece : 12 * piece + width], up_select) * up_mask)


def sum_parts_kernel(count, shard, place_ref, *refs):
    parts, (same_ref, other_ref) = refs[:-2], refs[-2:]
    first = place_ref[1] == 0
    at = 0
    for start in range(0, len(parts), count):
        low = sum(part[...].astype(F32) for part in parts[start : start + count])
        end = at + low.shape[1]
        mine, far = low[:shard], low[shard : 2 * shard]
        same_ref[:shard, at:end] = jnp.where(first, mine, far).astype(BF16)
        other_ref[:shard, at:end] = jnp.where(first, far, mine).astype(BF16)
        if low.shape[0] > 2 * shard:
            mine, far = low[2 * shard : 2 * shard + 1], low[2 * shard + 1 : 2 * shard + 2]
            same_ref[shard:, at:end] = jnp.broadcast_to(jnp.where(first, mine, far), (16, end - at)).astype(BF16)
            other_ref[shard:, at:end] = jnp.broadcast_to(jnp.where(first, far, mine), (16, end - at)).astype(BF16)
            same_ref[shard:, end:] = jnp.zeros((16, same_ref.shape[1] - end), BF16)
            other_ref[shard:, end:] = jnp.zeros((16, same_ref.shape[1] - end), BF16)
        at = end


def finish_kernel(*refs):
    parts, (qkv_ref, out_ref, up_ref, down_ref, vec_ref) = refs[:-5], refs[-5:]
    shard, cols, units = up_ref.shape[1], out_ref.shape[1], up_ref.shape[2]
    for layer in range(qkv_ref.shape[0]):
        total = parts[2 * layer][...].astype(F32) + parts[2 * layer + 1][...].astype(F32)
        for i in range(3):
            qkv_ref[layer, i] = total[:shard, i * cols : (i + 1) * cols]
        out_ref[layer] = total[:shard, 3 * cols : 4 * cols].T
        up_ref[layer] = total[:shard, 4 * cols : 4 * cols + units]
        down_ref[layer] = total[:shard, 4 * cols + units :]
        if layer == 0:
            vec_ref[...] = total[shard : shard + 8, : 4 * cols]


def enter_kernel(moved_ref, mod_ref, res_ref, far_res_ref, in_ref):
    residual = moved_ref[: res_ref.shape[0]].astype(F32)
    far_res_ref[...] = residual
    res_ref[...] = residual
    in_ref[...] = modulate(residual, mod_ref[...], 0, 1)


def attention_kernel(x0, x1, x2, x3, w_ref, bias_ref, bo_ref, x_ref, qkv_ref, att_ref, keep_ref, near_ref, send_ref):
    x = rows_of((x0, x1, x2, x3))
    x_ref[...] = x
    cols = w_ref.shape[1] // 4
    qkv = (dot(x, w_ref[:, : 3 * cols]) + bias_ref[...]).astype(BF16)
    qkv_ref[...] = qkv
    parts = []
    for head in range(cols // HD):
        at = head * HD
        q = qkv[:, at : at + HD]
        k = qkv[:, cols + at : cols + at + HD]
        v = qkv[:, 2 * cols + at : 2 * cols + at + HD]
        scores = dot(q, k, 1, 1) * (1.0 / math.sqrt(HD))
        expo = jnp.exp(scores - jnp.max(scores, axis=-1, keepdims=True))
        probs = expo / jnp.sum(expo, axis=-1, keepdims=True)
        parts.append(dot(probs.astype(BF16), v))
    att = jnp.concatenate(parts, axis=1).astype(BF16)
    att_ref[...] = att
    split_out(dot(att, w_ref[:, 3 * cols :], 1, 1) + bo_ref[...], keep_ref, near_ref, send_ref)


def middle_kernel(res_ref, mod_ref, keep_ref, core_ref, far_ref, branch_ref, far_mid_ref, mid_ref, in_ref):
    mod = mod_ref[...]
    branch = summed(keep_ref, core_ref, far_ref)
    branch_ref[...] = branch
    middle = res_ref[...] + mod[2:3] * branch
    far_mid_ref[...] = middle
    mid_ref[...] = middle
    in_ref[...] = modulate(middle, mod, 3, 4)


def mlp_kernel(x0, x1, x2, x3, w_ref, bu_ref, bd_ref, x_ref, hid_ref, act_ref, keep_ref, near_ref, send_ref):
    x = rows_of((x0, x1, x2, x3))
    x_ref[...] = x
    units = w_ref.shape[1] // 2
    hidden = dot(x, w_ref[:, :units]) + bu_ref[...]
    hid_ref[...] = hidden
    act = (0.5 * hidden * (1.0 + lax.erf(hidden * 0.7071067811865476))).astype(BF16)
    act_ref[...] = act
    split_out(dot(act, w_ref[:, units:], 1, 1) + bd_ref[...], keep_ref, near_ref, send_ref)


def next_kernel(
    mid_ref, mod_ref, keep_ref, core_ref, far_ref, mod_next_ref, out_ref, far_res_ref, res_ref, in_ref
):
    mlp_out = summed(keep_ref, core_ref, far_ref)
    out_ref[...] = mlp_out
    residual = mid_ref[...] + mod_ref[5:6] * mlp_out
    far_res_ref[...] = residual
    res_ref[...] = residual
    in_ref[...] = modulate(residual, mod_next_ref[...], 0, 1)


def last_kernel(mid_ref, mod_ref, keep_ref, core_ref, far_ref, g_ref, out_ref, dgate_ref):
    mlp_out = summed(keep_ref, core_ref, far_ref)
    out_ref[...] = (mid_ref[...] + mod_ref[5:6] * mlp_out).astype(BF16)
    dgate_ref[...] = col_sum(g_ref[...] * mlp_out)


def turn_kernel(moved_ref, mod_ref, g_ref, dmlp_ref):
    g = moved_ref[dmlp_ref.shape[0] :].astype(F32)
    g_ref[...] = g
    dmlp_ref[...] = (g * mod_ref[5:6]).astype(BF16)


def mlp_back_kernel(x0, x1, x2, x3, w_ref, hid_ref, x_ref, dhid_ref, keep_ref, near_ref, send_ref):
    x = rows_of((x0, x1, x2, x3))
    x_ref[...] = x
    units = w_ref.shape[1] // 2
    hidden = hid_ref[...]
    d_active = dot(x, w_ref[:, units:])
    cumulative = 0.5 * (1.0 + lax.erf(hidden * 0.7071067811865476))
    density = jnp.exp(-0.5 * hidden * hidden) * 0.3989422804014327
    d_hidden = (d_active * (cumulative + hidden * density)).astype(BF16)
    dhid_ref[...] = d_hidden
    split_out(dot(d_hidden, w_ref[:, :units], 1, 1), keep_ref, near_ref, send_ref)


def give_parts(grad, place_ref, scratch_ref, part_refs):
    if len(part_refs) == 1:
        part_refs[0][...] = grad.astype(BF16)
        return
    scratch_ref[...] = grad.astype(BF16)
    rows = part_refs[0].shape[0]
    for j, part in enumerate(part_refs):
        start = pl.multiple_of((place_ref[0] ^ j) * rows, rows)
        part[...] = scratch_ref[pl.ds(start, rows), :]


def mlp_grad_kernel(place_ref, y_ref, x_ref, dhid_ref, act_ref, *refs):
    part_refs, (vec_ref, scratch_ref) = refs[:-2], refs[-2:]
    y = y_ref[...]
    d_hidden = dhid_ref[...]
    grad = jnp.concatenate([dot(x_ref[...], d_hidden, 0, 0), dot(y, act_ref[...], 0, 0)], axis=1)
    give_parts(grad, place_ref, scratch_ref, part_refs)
    n_dp, length = vec_ref.shape
    piece = HD // n_dp
    cols = y.shape[1] // 4
    down = own_quarter(col_sum(y.astype(F32)), cols, place_ref)
    up = col_sum(d_hidden.astype(F32))
    vec_ref[...] = heads_back(down, 9 * piece, n_dp, length) + units_back(up, 12 * piece, n_dp, length)


def middle_back_kernel(g_ref, mod_ref, keep_ref, core_ref, far_ref, mid_ref, branch_ref, dmid_ref, dbranch_ref, sums_ref):
    mod = mod_ref[...]
    incoming = summed(keep_ref, core_ref, far_ref)
    normed, inverse = normalize(mid_ref[...])
    d_middle = g_ref[...] + norm_back(incoming * (1.0 + mod[4:5]), normed, inverse)
    dmid_ref[...] = d_middle
    dbranch_ref[...] = (d_middle * mod[2:3]).astype(BF16)
    sums_ref[...] = jnp.concatenate(
        [col_sum(d_middle * branch_ref[...]), col_sum(incoming), col_sum(incoming * normed)], axis=0
    )


def attention_back_kernel(x0, x1, x2, x3, w_ref, qkv_ref, x_ref, dqkv_ref, keep_ref, near_ref, send_ref):
    x = rows_of((x0, x1, x2, x3))
    x_ref[...] = x
    cols = w_ref.shape[1] // 4
    qkv = qkv_ref[...]
    scaling = 1.0 / math.sqrt(HD)
    d_att = dot(x, w_ref[:, 3 * cols :]).astype(BF16)
    grads = ([], [], [])
    for head in range(cols // HD):
        at = head * HD
        q = qkv[:, at : at + HD]
        k = qkv[:, cols + at : cols + at + HD]
        v = qkv[:, 2 * cols + at : 2 * cols + at + HD]
        d_out = d_att[:, at : at + HD]
        scores = dot(q, k, 1, 1) * scaling
        expo = jnp.exp(scores - jnp.max(scores, axis=-1, keepdims=True))
        probs = expo / jnp.sum(expo, axis=-1, keepdims=True)
        d_probs = dot(d_out, v, 1, 1)
        d_scores = (probs * (d_probs - jnp.sum(probs * d_probs, axis=-1, keepdims=True))).astype(BF16)
        grads[0].append(dot(d_scores, k) * scaling)
        grads[1].append(dot(d_scores, q, 0, 0) * scaling)
        grads[2].append(dot(probs.astype(BF16), d_out, 0, 0))
    d_qkv = jnp.concatenate(grads[0] + grads[1] + grads[2], axis=1).astype(BF16)
    dqkv_ref[...] = d_qkv
    split_out(dot(d_qkv, w_ref[:, : 3 * cols], 1, 1), keep_ref, near_ref, send_ref)


def attention_grad_kernel(n_parts, place_ref, y_ref, x_ref, dqkv_ref, att_ref, vecs_ref, *refs):
    part_refs, (vec_ref, scratch_ref) = refs[:-2], refs[-2:]
    y = y_ref[...]
    d_qkv = dqkv_ref[...]
    cols = d_qkv.shape[1] // 3
    wide = 4 * cols
    grad = jnp.concatenate([dot(x_ref[...], d_qkv, 0, 0), dot(y, att_ref[...], 0, 0)], axis=1)
    scratch_ref[...] = grad.astype(BF16)
    n_dp, length = vec_ref.shape
    piece = HD // n_dp
    total = col_sum(d_qkv.astype(F32))
    out = own_quarter(col_sum(y.astype(F32)), cols, place_ref)
    vec = vecs_ref[...] + (
        heads_back(total[:, :cols], 0, n_dp, length)
        + heads_back(total[:, 2 * cols :], 3 * piece, n_dp, length)
        + heads_back(out, 6 * piece, n_dp, length)
    )
    vec_ref[...] = vec
    if n_parts == 1:
        part_refs[0][...] = scratch_ref[...]
        return
    rows = scratch_ref.shape[0] // n_parts
    for j, part in enumerate(part_refs):
        at = place_ref[0] ^ j
        part[:rows] = scratch_ref[pl.ds(pl.multiple_of(at * rows, rows), rows), :]


def attention_grad_last_kernel(n_parts, place_ref, y_ref, x_ref, dqkv_ref, att_ref, vecs_ref, high_ref, *refs):
    part_refs, (vec_ref, scratch_ref) = refs[:-2], refs[-2:]
    rows = scratch_ref.shape[0] // n_parts
    attention_grad_kernel(
        n_parts, place_ref, y_ref, x_ref, dqkv_ref, att_ref, vecs_ref, *part_refs, vec_ref, scratch_ref
    )
    low = vec_ref[...]
    n_dp, length = low.shape
    width = scratch_ref.shape[1]
    row = lax.broadcasted_iota(jnp.int32, (16, n_dp), 0)
    col = lax.broadcasted_iota(jnp.int32, (16, n_dp), 1)
    lane = lax.broadcasted_iota(jnp.int32, (length, width), 0)
    place = lax.broadcasted_iota(jnp.int32, (length, width), 1)
    spread = exact(low, (place == lane).astype(F32)) + exact(high_ref[...], (place == lane + length).astype(F32))
    for j, part in enumerate(part_refs):
        part[rows:] = exact((col == 2 * (place_ref[0] ^ j) + row).astype(F32), spread).astype(BF16)


def enter_back(dmid_ref, mod_ref, keep_ref, core_ref, far_ref, res_ref):
    incoming = summed(keep_ref, core_ref, far_ref)
    normed, inverse = normalize(res_ref[...])
    g = dmid_ref[...] + norm_back(incoming * (1.0 + mod_ref[1:2]), normed, inverse)
    return g, col_sum(incoming), col_sum(incoming * normed)


def enter_back_kernel(dmid_ref, mod_ref, keep_ref, core_ref, far_ref, res_ref, g_ref, sums_ref):
    g, shift, scale = enter_back(dmid_ref, mod_ref, keep_ref, core_ref, far_ref, res_ref)
    g_ref[...] = g
    sums_ref[...] = jnp.concatenate([shift, scale], axis=0)


def previous_kernel(
    dmid_ref, mod_ref, keep_ref, core_ref, far_ref, res_ref, mod_prev_ref, out_prev_ref, g_ref, sums_ref, dmlp_ref, dgate_ref
):
    g, shift, scale = enter_back(dmid_ref, mod_ref, keep_ref, core_ref, far_ref, res_ref)
    g_ref[...] = g
    sums_ref[...] = jnp.concatenate([shift, scale], axis=0)
    dmlp_ref[...] = (g * mod_prev_ref[5:6]).astype(BF16)
    dgate_ref[...] = col_sum(g * out_prev_ref[...])


def body(
    tokens,
    condition,
    cotangent,
    mod_weight,
    mod_bias,
    qkv_weight,
    qv_bias,
    out_weight,
    out_bias,
    up_weight,
    up_bias,
    down_weight,
    down_bias,
):
    layers = mod_weight.shape[0]
    n_dp = lax.axis_size("dp")
    n_chips = n_dp // 2
    n_all = n_dp * 4
    dp = lax.axis_index("dp")
    z = lax.axis_index("tensor")
    chip = dp // 2
    core = dp % 2
    half = z // 2
    quarter = 2 * (half ^ core) + z % 2
    cols = mod_weight.shape[3]
    rows = tokens.shape[1]
    shard = qkv_weight.shape[1]
    units = up_weight.shape[2]
    piece = qv_bias.shape[3]

    place = jnp.stack([chip, core, quarter, z]).astype(jnp.int32)

    def move(values, target):
        return lax.ppermute(values, AXES, [(i, target(i)) for i in range(n_all)])

    def xor(values, mask):
        return move(values, lambda i: i ^ mask)

    def swap_core_half(i):
        return i & ~6 | (i & HALF) << 1 | (i & CORE) >> 1

    def to_other(i):
        return i ^ CORE if i & CORE else i ^ CORE ^ HALF

    def from_other(i):
        return i ^ CORE ^ HALF if i & CORE else i ^ CORE

    def to_same(i):
        return i ^ HALF if i & CORE else i

    def pick(values, index):
        return lax.dynamic_index_in_dim(values, index, 0, keepdims=False)

    def chip_gather(values, after=()):
        if n_chips > 8:
            groups = [[2 * i + c for i in range(n_chips)] for c in range(2)]
            return lax.all_gather(values, "dp", axis_index_groups=groups)
        parts = [xor(values, CHIP * j) if j else values for j in range(n_chips)]
        out = sds((n_chips,) + values.shape, values.dtype)
        return call(spread_kernel, [out], *parts, scalars=place, after=after, name="spread")[0]

    def chip_swap(values):
        if n_chips > 8:
            groups = [[2 * i + c for i in range(n_chips)] for c in range(2)]
            got = lax.all_to_all(values, "dp", 0, 0, axis_index_groups=groups, tiled=True)
            return [got[i] for i in range(n_chips)]
        return [xor(pick(values, chip ^ j), CHIP * j) if j else pick(values, chip) for j in range(n_chips)]

    def chip_sum(values):
        return sum(part.astype(F32) for part in chip_swap(values))

    def fetch_near(own, *widths):
        widths = widths or (own.shape[1],)
        return call(
            couple_kernel,
            [sds((2, own.shape[0], width), BF16) for width in widths],
            move(own, to_same),
            move(own, to_other),
            scalars=place,
            kept=tuple(range(len(widths))),
            name="couple",
        )

    def fetch_chips(pair):
        if n_chips > 8:
            return [chip_gather(pair)]
        return send_chips([pair] * n_chips, pair.size < D * 4 * cols // 4 + 32 * D)

    def send_chips(parts, at_once=False):
        if at_once:
            return [parts[0]] + [xor(parts[j], CHIP * j) for j in range(1, n_chips)]
        out = [parts[0]] + [xor(parts[j], CHIP * j) for j in range(1, min(3, n_chips))]
        return out + [xor(gate(parts[j], *out[1:]), CHIP * j) for j in range(3, n_chips)]

    def join(parts):
        if n_chips > 8:
            joined, extra = parts[0][:, :, :shard], parts[0][:, :, shard:]
        else:
            height, width = parts[0].shape[1:]
            out = [sds((n_chips, 2, shard, width), BF16)]
            if height > shard:
                out.append(sds((n_chips, 2, height - shard, width), BF16))
            joined, *extra = place_parts(
                join_moves, out, *parts, scalars=place, name="join", copies=len(out) * n_chips
            )
            extra = extra[0] if extra else None
        return joined.reshape(D, joined.shape[3]), extra

    def give_chips(parts, at_once=False):
        if n_chips > 8:
            return chip_swap(parts[0].reshape(n_chips, -1, parts[0].shape[1]))
        return send_chips(parts, at_once)

    def sum_given(parts, height, *after):
        out = sds((height, 4 * cols + 2 * units), BF16)
        return call(
            functools.partial(sum_parts_kernel, n_chips, shard),
            [out, out],
            *parts,
            scalars=place,
            after=after,
            stored=tuple(range(len(parts))),
            kept=(0, 1),
            name="sum_parts",
        )

    def give_near(low):
        return [move(low[0], to_same), move(low[1], from_other)]

    def all_rows(values):
        other = xor(values, PARITY)
        return (values, other, xor(values, CORE), xor(other, CORE))

    def sum_rows(keep, near, send):
        got = xor(send, CORE)
        return keep, got, xor((near + got[rows:].astype(F32)).astype(BF16), PARITY)

    cond_full = condition.astype(F32)
    cond_act = jax.nn.silu(cond_full).astype(BF16)
    (cond_pair,) = call(
        couple_kernel, [sds((2, 1, D), BF16)], cond_act, xor(cond_act, CORE), scalars=place, name="couple"
    )
    moved = move(jnp.concatenate([tokens[0], cotangent[0]]), swap_core_half)
    qkv_own = jnp.transpose(qkv_weight, (0, 2, 1, 3))
    down_own = jnp.transpose(down_weight, (0, 2, 1))

    bias_len = 12 * piece + up_bias.shape[2]
    bias_vec = jnp.concatenate(
        [
            qv_bias.reshape(layers, 6 * piece),
            out_bias.reshape(layers, 3 * piece),
            down_bias.reshape(layers, 3 * piece),
            up_bias.reshape(layers, -1),
        ],
        axis=1,
    )
    bias_block = lax.dynamic_update_slice(jnp.zeros((16, D), BF16), bias_vec, (0, 0))
    def pack_block(layer):
        return call(
            pack_block_kernel,
            [sds((shard, 4 * cols + 2 * units), BF16)],
            qkv_own[layer],
            out_weight[layer],
            up_weight[layer],
            down_own[layer],
            name="pack_block",
        )[0]

    (own_attention,) = call(
        pack_first_kernel, [sds((shard + 16, 4 * cols), BF16)], qkv_own[0], out_weight[0], bias_block, name="pack_first"
    )
    (own_mlp,) = call(pack_mlp_kernel, [sds((shard, 2 * units), BF16)], up_weight[0], down_own[0], name="pack_mlp")
    (pair_mlp,) = fetch_near(own_mlp)
    attention_weights = [None] * layers
    mlp_weights = [None] * layers
    (pair_attention,) = fetch_near(own_attention)

    cond_every = chip_gather(cond_pair, (pair_attention,)).reshape(n_dp, D)
    cond_slice = lax.dynamic_slice_in_dim(cond_every, dp * shard, shard, 1)
    bias_at = lax.dynamic_update_slice(
        jnp.zeros((layers, 6, cols // HD, HD), F32), mod_bias.astype(F32), (0, 0, 0, dp * piece)
    ).reshape(layers, 6, cols)
    partial_mod = jnp.einsum("ld,ydkc->lykc", cond_slice, mod_weight, preferred_element_type=F32) + bias_at
    mod_sum = chip_sum(partial_mod.reshape((n_chips, 2) + partial_mod.shape[1:]))
    mod_sum = gate(mod_sum, pair_mlp)
    attention_weights[0], bias_every = join(fetch_chips(gate(pair_attention, mod_sum)))
    mod_sum = mod_sum + xor(mod_sum, CORE)
    mod_own = pick(mod_sum, half)
    mod_far = pick(mod_sum, half ^ 1)
    quarters = [xor(mod_far if mask & HALF else mod_own, mask) if mask else mod_own for mask in range(4)]
    (modulation,) = call(
        assemble_kernel,
        [sds((layers, 6, D), F32)],
        *quarters,
        scalars=place,
        name="assemble",
    )

    parts_attention = [None] * layers
    parts_mlp = [None] * layers
    parts_mlp[0] = fetch_chips(gate(pair_mlp, attention_weights[0]))
    qkv_bias_all, wide_bias, up_bias_all = call(
        bias_kernel,
        [sds((layers, 1, 3 * cols), F32), sds((layers, 2, D), F32), sds((layers, 1, units), F32)],
        bias_every.reshape(n_dp * 16, D),
        scalars=place,
        name="bias",
    )
    cotan, d_mlp = call(
        turn_kernel, [sds((rows, D), F32), sds((rows, D), BF16)], moved, modulation[layers - 1], kept=(0,), name="turn"
    )
    d_mlp_rows = all_rows(d_mlp)

    full = 4 * rows
    keep_send = [sds((rows, D), F32), sds((rows, D), F32), sds((full // 2, D), BF16)]
    row_f32 = sds((rows, D), F32)
    row_bf16 = sds((rows, D), BF16)
    line = sds((1, D), F32)
    attention_flops = 2 * full * D * 4 * cols + 4 * full * full * cols
    mlp_flops = 4 * full * D * units

    def parts_of(width, extra=0):
        if n_chips > 8:
            return [sds((D, width), BF16)]
        return [sds((D // n_chips + extra, width), BF16)] * n_chips

    saved = []
    residual, far_residual, attn_in = call(
        enter_kernel,
        [row_f32, row_f32, row_bf16],
        moved,
        modulation[0],
        kept=(1,),
        after=(attention_weights[0],),
        name="enter",
    )
    for layer in range(layers):
        mod = modulation[layer]
        more = layer + 1 < layers
        attn_rows = all_rows(attn_in)
        if more:
            own_block = gate(pack_block(layer + 1), attn_rows[3])
            pair_attention, pair_mlp = fetch_near(own_block, 4 * cols, 2 * units)
            parts_attention[layer + 1] = fetch_chips(gate(pair_attention, parts_mlp[layer][-1]))
            parts_mlp[layer + 1] = fetch_chips(gate(pair_mlp, parts_attention[layer + 1][-1]))
        if layer:
            attention_weights[layer] = join(parts_attention[layer])[0]
        attn_x, qkv, att, *partial = call(
            attention_kernel,
            [sds((full, D), BF16), sds((full, 3 * cols), BF16), sds((full, cols), BF16)] + keep_send,
            *attn_rows,
            attention_weights[layer],
            qkv_bias_all[layer],
            wide_bias[layer, :1],
            flops=attention_flops,
            stored=(4,),
            kept=(0, 1, 2),
            name="attention",
        )
        partial[2] = gate(partial[2], *parts_mlp[layer][1:3])
        branch, far_middle, middle, mlp_in = call(
            middle_kernel,
            [row_f32, row_f32, row_f32, row_bf16],
            residual,
            mod,
            *sum_rows(*partial),
            kept=(0, 1),
            name="middle",
        )
        mlp_in = gate(mlp_in, parts_mlp[layer][-1])
        mlp_rows = all_rows(mlp_in)
        mlp_weights[layer] = join(parts_mlp[layer])[0]
        mlp_x, hidden, act, *partial = call(
            mlp_kernel,
            [sds((full, D), BF16), sds((full, units), F32), sds((full, units), BF16)] + keep_send,
            *mlp_rows,
            mlp_weights[layer],
            up_bias_all[layer],
            wide_bias[layer, 1:],
            flops=mlp_flops,
            stored=(4,),
            kept=(0, 1, 2),
            name="mlp",
        )
        if more:
            partial[2] = gate(partial[2], *parts_attention[layer + 1][1:3])
        arrived = sum_rows(*partial)
        saved.append((far_residual, attn_x, qkv, att, branch, far_middle, mlp_x, hidden, act))
        if more:
            arrived = (gate(arrived[0], parts_attention[layer + 1][-1]),) + arrived[1:]
            mlp_out, far_residual, residual, attn_in = call(
                next_kernel,
                [row_f32, row_f32, row_f32, row_bf16],
                middle,
                mod,
                *arrived,
                modulation[layer + 1],
                kept=(0, 1),
                name="next",
            )
            saved[-1] += (mlp_out,)
        else:
            output, d_gate_two = call(
                last_kernel, [row_bf16, line], middle, mod, *arrived, cotan, stored=(5,), name="last"
            )

    output = move(output, swap_core_half)[None]
    flow = cotan
    mod_lines = [None] * layers
    vecs = [None] * layers
    low = [None] * layers
    near_packs = [None] * layers
    given_attention = [None] * layers
    given_mlp = [None] * layers
    vec_shape = sds((n_dp, bias_len), F32)
    for layer in reversed(range(layers)):
        far_residual, attn_x, qkv, att, branch, far_middle, mlp_x, hidden, act = saved[layer][:9]
        mod = modulation[layer]
        more = layer + 1 < layers
        if more:
            d_mlp_rows = all_rows(d_mlp)
        mlp_y, d_hidden, *partial = call(
            mlp_back_kernel,
            [sds((full, D), BF16), sds((full, units), BF16)] + keep_send,
            *d_mlp_rows,
            mlp_weights[layer],
            hidden,
            flops=mlp_flops,
            stored=(4, 5),
            kept=(0, 1),
            name="mlp_back",
        )
        if more:
            partial[2] = gate(partial[2], *given_mlp[layer + 1][1:3])
        arrived = sum_rows(*partial)
        *grad_mlp, vec_mlp = call(
            mlp_grad_kernel,
            parts_of(2 * units) + [vec_shape],
            mlp_y,
            mlp_x,
            d_hidden,
            act,
            flops=mlp_flops,
            scalars=place,
            scratch=[pltpu.VMEM((D, 2 * units), BF16)],
            stored=(0, 1, 2, 3),
            kept=(0,),
            name="mlp_grad",
        )
        arrived = (gate(arrived[0], grad_mlp[0], *(given_mlp[layer + 1][3:] if more else ())),) + arrived[1:]
        if more:
            grad_mlp = [gate(part, *given_attention[layer + 1][1:]) for part in grad_mlp]
        given_mlp[layer] = give_chips(grad_mlp)
        d_middle, d_branch, sums_mid = call(
            middle_back_kernel,
            [row_f32, row_bf16, sds((3, D), F32)],
            flow,
            mod,
            *arrived,
            far_middle,
            branch,
            stored=(5, 6) if more else (0, 5, 6),
            name="middle_back",
        )
        if more:
            d_branch = gate(d_branch, *given_attention[layer + 1][1:])
            low[layer + 1] = sum_given(list(given_attention[layer + 1]) + list(given_mlp[layer + 1]), shard)
            near_packs[layer + 1] = give_near(low[layer + 1])
        d_branch_rows = all_rows(d_branch)
        attn_y, d_qkv, *partial = call(
            attention_back_kernel,
            [sds((full, D), BF16), sds((full, 3 * cols), BF16)] + keep_send,
            *d_branch_rows,
            attention_weights[layer],
            qkv,
            flops=attention_flops * 2,
            stored=(4, 5),
            kept=(0, 1),
            name="attention_back",
        )
        if more:
            partial[2] = gate(partial[2], *given_mlp[layer][1:3], near_packs[layer + 1][0])
        arrived = sum_rows(*partial)
        *grad_attention, vecs[layer] = call(
            functools.partial(
                attention_grad_kernel if layer or n_chips > 8 else attention_grad_last_kernel,
                1 if n_chips > 8 else n_chips,
            ),
            parts_of(4 * cols, 0 if layer else 16) + [vec_shape],
            attn_y,
            attn_x,
            d_qkv,
            att,
            vec_mlp,
            *(() if layer or n_chips > 8 else (vecs[1],)),
            flops=attention_flops,
            scalars=place,
            scratch=[pltpu.VMEM((D, 4 * cols), BF16)],
            stored=(0, 1, 2, 3),
            kept=(0,),
            name="attention_grad",
        )
        after = (grad_attention[0],)
        if layer == 0:
            after = after + tuple(given_mlp[0][3:]) + tuple(near_packs[upper][1] for upper in range(1, layers))
        if layer == 0:
            height = 2 * shard + 16
            if n_chips > 8:
                rows_bias = jnp.concatenate([vecs[i] for i in range(layers)], axis=1).astype(BF16)
                rows_bias = jnp.pad(
                    rows_bias.reshape(n_chips, 2, -1), ((0, 0), (0, 14), (0, 4 * cols - layers * bias_len))
                )
                rows_all = jnp.concatenate(
                    [grad_attention[0].reshape(n_chips, 2 * shard, 4 * cols), rows_bias], axis=1
                )
                grad_attention = [rows_all.reshape(n_chips * height, 4 * cols)]
        given_attention[layer] = give_chips([gate(part, *given_mlp[layer][1:]) for part in grad_attention], True)
        if layer:
            flow, sums_in, d_mlp, gate_next = call(
                previous_kernel,
                [row_f32, sds((2, D), F32), row_bf16, line],
                d_middle,
                mod,
                *arrived,
                far_residual,
                modulation[layer - 1],
                saved[layer - 1][9],
                stored=(5, 7),
                after=after,
                name="previous",
            )
        else:
            flow, sums_in = call(
                enter_back_kernel,
                [row_f32, sds((2, D), F32)],
                d_middle,
                mod,
                *arrived,
                far_residual,
                stored=(5,),
                after=after,
                name="enter_back",
            )
            gate_next = None
        mod_lines[layer] = jnp.concatenate([sums_in, sums_mid, d_gate_two], axis=0)
        d_gate_two = gate_next

    d_mod = jnp.stack(mod_lines)
    d_mod = d_mod + xor(d_mod, CORE)
    d_mod = (d_mod + xor(d_mod, PARITY)).astype(BF16).reshape(layers * 6, 4, cols)
    d_mod = jnp.transpose(d_mod, (1, 0, 2))
    mine = pick(d_mod, z)
    far = xor(pick(d_mod, z ^ HALF), HALF)
    d_mod_pair = jnp.where(half == 0, jnp.stack([mine, far]), jnp.stack([far, mine]))
    low[0] = sum_given(list(given_attention[0]) + list(given_mlp[0]), shard + 16)
    near_packs[0] = give_near(low[0])
    d_mod_every = chip_gather(d_mod_pair).reshape(n_dp, layers, 6, cols)
    grad_mod_w = jnp.einsum("ld,lykc->ydkc", cond_slice, d_mod_every, preferred_element_type=F32)
    grad_mod_b = jnp.sum(d_mod_every.astype(F32), axis=0).reshape(layers, 6, cols // HD, HD)
    grad_mod_b = lax.dynamic_slice_in_dim(grad_mod_b, dp * piece, piece, 3)
    cond_pieces = jnp.einsum("lykc,ydkc->ld", d_mod_every, mod_weight, preferred_element_type=F32)
    cond_pieces = gate(cond_pieces, *given_attention[0][1:])
    mixed = jnp.stack(chip_swap(cond_pieces.reshape(n_chips, 2, shard)))
    if n_chips <= 8:
        mixed = jnp.take(mixed, chip ^ jnp.arange(n_chips), axis=0)
    cond_pieces = jnp.transpose(mixed, (1, 0, 2))
    cond_pieces = gate(cond_pieces, *low[0])
    cond_mine = pick(cond_pieces, core)
    cond_sent = xor(pick(cond_pieces, core ^ 1), CORE)
    cond_total = jnp.where(
        core == 0, jnp.stack([cond_mine, cond_sent], axis=1), jnp.stack([cond_sent, cond_mine], axis=1)
    ).reshape(1, D)
    cond_total = cond_total + xor(cond_total, PARITY)
    cond_total = cond_total + xor(cond_total, HALF)
    sigmoid_cond = jax.nn.sigmoid(cond_full)
    grad_condition = cond_total * sigmoid_cond * (1.0 + cond_full * (1.0 - sigmoid_cond))

    grad_tokens = move(flow, swap_core_half)[None]
    grad_qkv, grad_out, grad_up, grad_down, vec = call(
        finish_kernel,
        [
            sds((layers, 3, shard, cols), F32),
            sds((layers, cols, shard), F32),
            sds((layers, shard, units), F32),
            sds((layers, shard, units), F32),
            sds((8, 4 * cols), F32),
        ],
        *[part for layer in range(layers) for part in near_packs[layer]],
        kept=(0, 1, 2, 3),
        name="finish",
    )
    vec = vec[0, : layers * bias_len].reshape(layers, bias_len)
    vec_heads = vec[:, : 12 * piece].reshape(layers, 4, 3, piece)
    return (
        output,
        grad_tokens,
        grad_condition,
        grad_mod_w,
        grad_mod_b,
        jnp.transpose(grad_qkv, (0, 2, 1, 3)),
        vec_heads[:, :2],
        grad_out,
        vec_heads[:, 2],
        grad_up,
        vec[:, 12 * piece :].reshape(layers, 1, -1),
        jnp.transpose(grad_down, (0, 2, 1)),
        vec_heads[:, 3],
    )


def solution(mesh):
    in_specs = (
        P("dp", "tensor", None),
        P("dp", None),
        P("dp", "tensor", None),
        P(None, "dp", None, "tensor"),
        P(None, None, "tensor", "dp"),
        P(None, "dp", None, "tensor"),
        P(None, None, "tensor", "dp"),
        P(None, "tensor", "dp"),
        P(None, "tensor", "dp"),
        P(None, "dp", "tensor"),
        P(None, "tensor", "dp"),
        P(None, "tensor", "dp"),
        P(None, "tensor", "dp"),
    )
    out_specs = (
        P("dp", "tensor", None),
        P("dp", "tensor", None),
        P("dp", None),
        P(None, "dp", None, "tensor"),
        P(None, None, "tensor", "dp"),
        P(None, "dp", None, "tensor"),
        P(None, None, "tensor", "dp"),
        P(None, "tensor", "dp"),
        P(None, "tensor", "dp"),
        P(None, "dp", "tensor"),
        P(None, "tensor", "dp"),
        P(None, "tensor", "dp"),
        P(None, "tensor", "dp"),
    )
    return jax.shard_map(body, mesh=mesh, in_specs=in_specs, out_specs=out_specs, check_vma=False)
```

```python
import functools
import math

import jax
import jax.numpy as jnp
from jax import lax
from jax.experimental import pallas as pl
from jax.experimental.pallas import tpu as pltpu
from jax.sharding import PartitionSpec as P

D = 768
HD = 64
EPS = 1e-06
AXES = ("dp", "tensor")
F32 = jnp.float32
BF16 = jnp.bfloat16
VMEM_LIMIT = 16 * 1024 * 1024

PARITY = 1
HALF = 2
CORE = 4
CHIP = 8


class Stored:
    def __init__(self, source, target, sem, local):
        self.copy = pltpu.make_async_copy(source, target, sem)
        self.local = local
        self.shape = local.shape
        self.busy = False
        self.dirty = False

    def start(self):
        self.copy.start()
        self.busy = True
        self.dirty = False

    def settle(self):
        if self.busy:
            self.copy.wait()
            self.busy = False

    def __getitem__(self, index):
        self.settle()
        return self.local[index]

    def __setitem__(self, index, value):
        self.local[index] = value
        self.dirty = True
        if index is Ellipsis:
            self.start()


def call(
    kernel, out_shape, *args, flops=0, name=None, scalars=None, after=(), scratch=(), stored=(), kept=(), window=()
):
    size = sum(a.size * a.dtype.itemsize for a in args) + sum(math.prod(o.shape) * o.dtype.itemsize for o in out_shape)
    hbm = pl.BlockSpec(memory_space=pltpu.HBM)
    vmem = pl.BlockSpec(memory_space=pltpu.VMEM)
    in_specs = [hbm if i in stored else vmem for i in range(len(args))]
    out_specs = [hbm if i in kept else vmem for i in range(len(out_shape))]
    window = dict(window)
    copies = [pltpu.VMEM((args[i].shape[0], window[i][1]) if i in window else args[i].shape, args[i].dtype) for i in stored]
    copies += [pltpu.VMEM(out_shape[i].shape, out_shape[i].dtype) for i in kept]
    lead = 0
    if after:
        args = (gate(args[0], *after),) + args[1:]
    if scalars is not None:
        args = (scalars,) + args
        in_specs = [pl.BlockSpec(memory_space=pltpu.SMEM)] + in_specs
        lead = 1

    def run(*refs):
        ins = list(refs[: len(args)])
        outs = list(refs[len(args) : len(args) + len(out_shape)])
        rest = refs[len(args) + len(out_shape) :]
        own, local = rest[: len(scratch)], rest[len(scratch) :]
        held = []
        for n, i in enumerate(stored):
            source = ins[lead + i].at[:, pl.ds(*window[i])] if i in window else ins[lead + i]
            held.append(Stored(source, local[n], local[-1].at[n], local[n]))
            held[-1].start()
            ins[lead + i] = held[-1]
        for n, i in enumerate(kept, len(stored)):
            held.append(Stored(local[n], outs[i], local[-1].at[n], local[n]))
            outs[i] = held[-1]
        kernel(*ins, *outs, *own)
        for item in held:
            if item.dirty:
                item.start()
        for item in held:
            item.settle()

    return pl.pallas_call(
        run,
        out_shape=out_shape,
        in_specs=in_specs,
        out_specs=out_specs,
        scratch_shapes=list(scratch) + copies + ([pltpu.SemaphoreType.DMA((len(copies),))] if copies else []),
        compiler_params=pltpu.CompilerParams(vmem_limit_bytes=VMEM_LIMIT),
        cost_estimate=pl.CostEstimate(flops=flops, bytes_accessed=size, transcendentals=0),
        name=name,
    )(*args)


def gate(value, *others):
    return lax.optimization_barrier((value,) + others)[0]


def place_parts(kernel, out_shape, *args, scalars, name, copies):
    count = len(args)

    def run(place_ref, *refs):
        outs = refs[count : count + len(out_shape)]
        sems = refs[-1]
        moves = [
            pltpu.make_async_copy(source, target, sems.at[n])
            for n, (source, target) in enumerate(kernel(place_ref, refs[:count], outs))
        ]
        for item in moves:
            item.start()
        for item in moves:
            item.wait()

    size = sum(a.size * a.dtype.itemsize for a in args)
    return pl.pallas_call(
        run,
        out_shape=out_shape,
        in_specs=[pl.BlockSpec(memory_space=pltpu.SMEM)]
        + [pl.BlockSpec(memory_space=pltpu.HBM)] * count,
        out_specs=[pl.BlockSpec(memory_space=pltpu.HBM)] * len(out_shape),
        scratch_shapes=[pltpu.SemaphoreType.DMA((copies,))],
        compiler_params=pltpu.CompilerParams(vmem_limit_bytes=VMEM_LIMIT),
        cost_estimate=pl.CostEstimate(flops=0, bytes_accessed=2 * size, transcendentals=0),
        name=name,
    )(scalars, *args)


def sds(shape, dtype):
    return jax.ShapeDtypeStruct(shape, dtype)


def dot(a, b, ca=1, cb=0):
    return lax.dot_general(a, b, (((ca,), (cb,)), ((), ())), preferred_element_type=F32)


def normalize(values):
    centered = values - jnp.mean(values, axis=-1, keepdims=True)
    inverse = lax.rsqrt(jnp.mean(centered * centered, axis=-1, keepdims=True) + EPS)
    return centered * inverse, inverse


def norm_back(incoming, normed, inverse):
    average = jnp.mean(incoming, axis=-1, keepdims=True)
    along = jnp.mean(incoming * normed, axis=-1, keepdims=True)
    return inverse * (incoming - average - normed * along)


def col_sum(values):
    return jnp.sum(values, axis=0, keepdims=True)


def modulate(values, mod, shift, scale):
    normed, _ = normalize(values)
    return (normed * (1.0 + mod[scale : scale + 1]) + mod[shift : shift + 1]).astype(BF16)


def rows_of(refs):
    return jnp.concatenate([ref[...] for ref in refs], axis=0)


def split_out(total, keep_ref, near_ref, send_ref):
    quarter = total.shape[0] // 4
    keep_ref[...] = total[:quarter]
    near_ref[...] = total[quarter : 2 * quarter]
    send_ref[...] = total[2 * quarter :].astype(BF16)


def summed(keep_ref, core_ref, far_ref):
    return keep_ref[...] + core_ref[: keep_ref.shape[0]].astype(F32) + far_ref[...].astype(F32)


def attention_pack(layer, qkv_ref, out_ref):
    out = out_ref[layer].astype(F32).T.astype(BF16)
    return jnp.concatenate([qkv_ref[layer, 0], qkv_ref[layer, 1], qkv_ref[layer, 2], out], axis=1)


def pack_block_kernel(layer, qkv_ref, out_ref, up_ref, down_ref, pack_ref):
    wide = 4 * out_ref.shape[1]
    units = up_ref.shape[2]
    pack_ref[:, :wide] = attention_pack(layer, qkv_ref, out_ref)
    pack_ref[:, wide : wide + units] = up_ref[layer]
    pack_ref[:, wide + units :] = down_ref[layer]


def pack_first_kernel(qkv_ref, out_ref, bias_ref, pack_ref):
    shard = out_ref.shape[2]
    pack_ref[:shard] = attention_pack(0, qkv_ref, out_ref)
    pack_ref[shard:] = bias_ref[...]


def pack_mlp_kernel(up_ref, down_ref, pack_ref):
    units = up_ref.shape[2]
    pack_ref[:, :units] = up_ref[0]
    pack_ref[:, units:] = down_ref[0]


def join_moves(place_ref, ins, outs):
    shard = outs[0].shape[2]
    moves = []
    for j, part in enumerate(ins):
        at = place_ref[0] ^ j
        moves.append((part.at[:, :shard], outs[0].at[at]))
        if len(outs) == 2:
            moves.append((part.at[:, shard:], outs[1].at[at]))
    return moves


def assemble_kernel(place_ref, *refs):
    parts, out_ref = refs[:-1], refs[-1]
    cols = parts[0].shape[2]
    for layer in range(out_ref.shape[0]):
        for at in range(4):
            quarter = sum(
                jnp.where(place_ref[3] ^ mask == at, part[layer], 0.0) for mask, part in enumerate(parts)
            )
            out_ref[layer, :, at * cols : (at + 1) * cols] = quarter


def spread_kernel(place_ref, *refs):
    parts, out_ref = refs[:-1], refs[-1]
    for j, part in enumerate(parts):
        out_ref[place_ref[0] ^ j] = part[...]


def couple_kernel(place_ref, own_ref, other_ref, *out_refs):
    first = place_ref[1] == 0
    at = 0
    for out_ref in out_refs:
        end = at + out_ref.shape[-1]
        own, other = own_ref[..., at:end], other_ref[..., at:end]
        out_ref[0] = jnp.where(first, own, other)
        out_ref[1] = jnp.where(first, other, own)
        at = end


def head_select(n_dp, piece, cols):
    row = lax.broadcasted_iota(jnp.int32, (3 * piece, cols), 0)
    col = lax.broadcasted_iota(jnp.int32, (3 * piece, cols), 1)
    return (row == col // HD * piece + col % piece).astype(F32)


def head_mask(n_dp, piece, cols):
    row = lax.broadcasted_iota(jnp.int32, (n_dp, cols), 0)
    col = lax.broadcasted_iota(jnp.int32, (n_dp, cols), 1)
    return (col % HD // piece == row).astype(F32)


def exact(a, b):
    return lax.dot_general(
        a, b, (((1,), (0,)), ((), ())), preferred_element_type=F32, precision=lax.Precision.HIGHEST
    )


def heads_back(line, at, n_dp, length):
    cols, piece = line.shape[1], HD // n_dp
    row = lax.broadcasted_iota(jnp.int32, (length, cols), 0) - at
    col = lax.broadcasted_iota(jnp.int32, (length, cols), 1)
    select = (row == col // HD * piece + col % piece).astype(F32)
    return lax.dot_general(
        head_mask(n_dp, piece, cols) * line,
        select,
        (((1,), (1,)), ((), ())),
        preferred_element_type=F32,
        precision=lax.Precision.HIGHEST,
    )


def units_back(line, at, n_dp, length):
    units = line.shape[1]
    width = units // n_dp
    row = lax.broadcasted_iota(jnp.int32, (length, units), 0) - at
    col = lax.broadcasted_iota(jnp.int32, (length, units), 1)
    mask = (
        lax.broadcasted_iota(jnp.int32, (n_dp, units), 1) // width
        == lax.broadcasted_iota(jnp.int32, (n_dp, units), 0)
    )
    return lax.dot_general(
        mask.astype(F32) * line,
        (col % width == row).astype(F32),
        (((1,), (1,)), ((), ())),
        preferred_element_type=F32,
        precision=lax.Precision.HIGHEST,
    )


def own_quarter(line, cols, place_ref):
    return sum(
        jnp.where(place_ref[2] == i, line[:, i * cols : (i + 1) * cols], 0.0) for i in range(line.shape[1] // cols)
    )


def bias_kernel(place_ref, vec_ref, qkv_ref, wide_ref, up_ref):
    n_dp, piece = vec_ref.shape[0] // 16, HD * 16 // vec_ref.shape[0]
    vec_row = lax.broadcasted_iota(jnp.int32, (n_dp, vec_ref.shape[0]), 0)
    vec_col = lax.broadcasted_iota(jnp.int32, (n_dp, vec_ref.shape[0]), 1)
    cols, units = qkv_ref.shape[2] // 3, up_ref.shape[2]
    select, mask = head_select(n_dp, piece, cols), head_mask(n_dp, piece, cols)
    width = units // n_dp
    row = lax.broadcasted_iota(jnp.int32, (width, units), 0)
    col = lax.broadcasted_iota(jnp.int32, (width, units), 1)
    up_select = (col % width == row).astype(F32)
    up_row = lax.broadcasted_iota(jnp.int32, (n_dp, units), 0)
    up_col = lax.broadcasted_iota(jnp.int32, (n_dp, units), 1)
    up_mask = (up_col // width == up_row).astype(F32)
    quarters = wide_ref.shape[2] // cols
    place = lax.broadcasted_iota(jnp.int32, (1, quarters * cols), 1) // cols == place_ref[2]
    for layer in range(qkv_ref.shape[0]):
        vec = dot((vec_col == 16 * vec_row + layer).astype(BF16), vec_ref[...])
        heads = [col_sum(exact(vec[:, 3 * t * piece : 3 * (t + 1) * piece], select) * mask) for t in range(4)]
        qkv_ref[layer] = jnp.concatenate([heads[0], jnp.zeros_like(heads[0]), heads[1]], axis=1)
        for t in range(2):
            wide_ref[layer, t : t + 1] = jnp.where(place, jnp.concatenate([heads[2 + t]] * quarters, axis=1), 0.0)
        up_ref[layer] = col_sum(exact(vec[:, 12 * piece : 12 * piece + width], up_select) * up_mask)


def sum_parts_kernel(count, shard, place_ref, *refs):
    parts, (same_ref, other_ref) = refs[:-2], refs[-2:]
    first = place_ref[1] == 0
    at = 0
    for start in range(0, len(parts), count):
        low = sum(part[...].astype(F32) for part in parts[start : start + count])
        end = at + low.shape[1]
        mine, far = low[:shard], low[shard : 2 * shard]
        same_ref[:shard, at:end] = jnp.where(first, mine, far).astype(BF16)
        other_ref[:shard, at:end] = jnp.where(first, far, mine).astype(BF16)
        if low.shape[0] > 2 * shard:
            mine, far = low[2 * shard : 2 * shard + 1], low[2 * shard + 1 : 2 * shard + 2]
            same_ref[shard:, at:end] = jnp.broadcast_to(jnp.where(first, mine, far), (16, end - at)).astype(BF16)
            other_ref[shard:, at:end] = jnp.broadcast_to(jnp.where(first, far, mine), (16, end - at)).astype(BF16)
        at = end


def finish_kernel(last_ref, flow_ref, *refs):
    parts, (last_out_ref, flow_out_ref, qkv_ref, out_ref, up_ref, down_ref, vec_ref) = refs[:-7], refs[-7:]
    last_out_ref[...] = last_ref[...]
    flow_out_ref[...] = flow_ref[...]
    shard, cols, units = up_ref.shape[1], out_ref.shape[1], up_ref.shape[2]
    for layer in range(qkv_ref.shape[0]):
        if layer == 0:
            total = parts[0][...].astype(F32) + parts[1][...].astype(F32)
            vec_ref[...] = total[shard : shard + 8]
            mlp = parts[2][...].astype(F32) + parts[3][...].astype(F32)
        else:
            total = parts[2 * layer + 2][...].astype(F32) + parts[2 * layer + 3][...].astype(F32)
            mlp = total[:, 4 * cols :]
        for i in range(3):
            qkv_ref[layer, i] = total[:shard, i * cols : (i + 1) * cols]
        out_ref[layer] = total[:shard, 3 * cols : 4 * cols].T
        up_ref[layer] = mlp[:, :units]
        down_ref[layer] = mlp[:, units:]


def enter_kernel(moved_ref, mod_ref, res_ref, far_res_ref, in_ref):
    residual = moved_ref[: res_ref.shape[0]].astype(F32)
    far_res_ref[...] = residual
    res_ref[...] = residual
    in_ref[...] = modulate(residual, mod_ref[...], 0, 1)


def attention_kernel(x0, x1, x2, x3, w_ref, bias_ref, bo_ref, x_ref, qkv_ref, att_ref, keep_ref, near_ref, send_ref):
    x = rows_of((x0, x1, x2, x3))
    x_ref[...] = x
    cols = w_ref.shape[1] // 4
    qkv = (dot(x, w_ref[:, : 3 * cols]) + bias_ref[...]).astype(BF16)
    qkv_ref[...] = qkv
    parts = []
    for head in range(cols // HD):
        at = head * HD
        q = qkv[:, at : at + HD]
        k = qkv[:, cols + at : cols + at + HD]
        v = qkv[:, 2 * cols + at : 2 * cols + at + HD]
        scores = dot(q, k, 1, 1) * (1.0 / math.sqrt(HD))
        expo = jnp.exp(scores - jnp.max(scores, axis=-1, keepdims=True))
        probs = expo / jnp.sum(expo, axis=-1, keepdims=True)
        parts.append(dot(probs.astype(BF16), v))
    att = jnp.concatenate(parts, axis=1).astype(BF16)
    att_ref[...] = att
    split_out(dot(att, w_ref[:, 3 * cols :], 1, 1) + bo_ref[...], keep_ref, near_ref, send_ref)


def middle_kernel(res_ref, mod_ref, keep_ref, core_ref, far_ref, branch_ref, far_mid_ref, mid_ref, in_ref):
    mod = mod_ref[...]
    branch = summed(keep_ref, core_ref, far_ref)
    branch_ref[...] = branch
    middle = res_ref[...] + mod[2:3] * branch
    far_mid_ref[...] = middle
    mid_ref[...] = middle
    in_ref[...] = modulate(middle, mod, 3, 4)


def mlp_kernel(x0, x1, x2, x3, w_ref, bu_ref, bd_ref, x_ref, hid_ref, act_ref, keep_ref, near_ref, send_ref):
    x = rows_of((x0, x1, x2, x3))
    x_ref[...] = x
    units = w_ref.shape[1] // 2
    hidden = dot(x, w_ref[:, :units]) + bu_ref[...]
    hid_ref[...] = hidden
    act = (0.5 * hidden * (1.0 + lax.erf(hidden * 0.7071067811865476))).astype(BF16)
    act_ref[...] = act
    split_out(dot(act, w_ref[:, units:], 1, 1) + bd_ref[...], keep_ref, near_ref, send_ref)


def next_kernel(
    mid_ref, mod_ref, keep_ref, core_ref, far_ref, mod_next_ref, out_ref, far_res_ref, res_ref, in_ref
):
    mlp_out = summed(keep_ref, core_ref, far_ref)
    out_ref[...] = mlp_out
    residual = mid_ref[...] + mod_ref[5:6] * mlp_out
    far_res_ref[...] = residual
    res_ref[...] = residual
    in_ref[...] = modulate(residual, mod_next_ref[...], 0, 1)


def last_kernel(mid_ref, mod_ref, keep_ref, core_ref, far_ref, g_ref, out_ref, dgate_ref):
    mlp_out = summed(keep_ref, core_ref, far_ref)
    out_ref[...] = (mid_ref[...] + mod_ref[5:6] * mlp_out).astype(BF16)
    dgate_ref[...] = col_sum(g_ref[...] * mlp_out)


def turn_kernel(moved_ref, mod_ref, g_ref, dmlp_ref):
    g = moved_ref[dmlp_ref.shape[0] :].astype(F32)
    g_ref[...] = g
    dmlp_ref[...] = (g * mod_ref[5:6]).astype(BF16)


def mlp_back_kernel(x0, x1, x2, x3, w_ref, hid_ref, x_ref, dhid_ref, keep_ref, near_ref, send_ref):
    x = rows_of((x0, x1, x2, x3))
    x_ref[...] = x
    units = w_ref.shape[1] // 2
    hidden = hid_ref[...]
    d_active = dot(x, w_ref[:, units:])
    cumulative = 0.5 * (1.0 + lax.erf(hidden * 0.7071067811865476))
    density = jnp.exp(-0.5 * hidden * hidden) * 0.3989422804014327
    d_hidden = (d_active * (cumulative + hidden * density)).astype(BF16)
    dhid_ref[...] = d_hidden
    split_out(dot(d_hidden, w_ref[:, :units], 1, 1), keep_ref, near_ref, send_ref)


def give_parts(grad, place_ref, scratch_ref, part_refs):
    if len(part_refs) == 1:
        part_refs[0][...] = grad.astype(BF16)
        return
    scratch_ref[...] = grad.astype(BF16)
    rows = part_refs[0].shape[0]
    for j, part in enumerate(part_refs):
        start = pl.multiple_of((place_ref[0] ^ j) * rows, rows)
        part[...] = scratch_ref[pl.ds(start, rows), :]


def mlp_grad_kernel(place_ref, y_ref, x_ref, dhid_ref, act_ref, *refs):
    part_refs, (vec_ref, scratch_ref) = refs[:-2], refs[-2:]
    y = y_ref[...]
    d_hidden = dhid_ref[...]
    grad = jnp.concatenate([dot(x_ref[...], d_hidden, 0, 0), dot(y, act_ref[...], 0, 0)], axis=1)
    give_parts(grad, place_ref, scratch_ref, part_refs)
    n_dp, length = vec_ref.shape
    piece = HD // n_dp
    cols = y.shape[1] // 4
    down = own_quarter(col_sum(y.astype(F32)), cols, place_ref)
    up = col_sum(d_hidden.astype(F32))
    vec_ref[...] = heads_back(down, 9 * piece, n_dp, length) + units_back(up, 12 * piece, n_dp, length)


def middle_back_kernel(g_ref, mod_ref, keep_ref, core_ref, far_ref, mid_ref, branch_ref, dmid_ref, dbranch_ref, sums_ref):
    mod = mod_ref[...]
    incoming = summed(keep_ref, core_ref, far_ref)
    normed, inverse = normalize(mid_ref[...])
    d_middle = g_ref[...] + norm_back(incoming * (1.0 + mod[4:5]), normed, inverse)
    dmid_ref[...] = d_middle
    dbranch_ref[...] = (d_middle * mod[2:3]).astype(BF16)
    sums_ref[...] = jnp.concatenate(
        [col_sum(d_middle * branch_ref[...]), col_sum(incoming), col_sum(incoming * normed)], axis=0
    )


def attention_back_kernel(x0, x1, x2, x3, w_ref, qkv_ref, x_ref, dqkv_ref, keep_ref, near_ref, send_ref):
    x = rows_of((x0, x1, x2, x3))
    x_ref[...] = x
    cols = w_ref.shape[1] // 4
    qkv = qkv_ref[...]
    scaling = 1.0 / math.sqrt(HD)
    d_att = dot(x, w_ref[:, 3 * cols :]).astype(BF16)
    grads = ([], [], [])
    for head in range(cols // HD):
        at = head * HD
        q = qkv[:, at : at + HD]
        k = qkv[:, cols + at : cols + at + HD]
        v = qkv[:, 2 * cols + at : 2 * cols + at + HD]
        d_out = d_att[:, at : at + HD]
        scores = dot(q, k, 1, 1) * scaling
        expo = jnp.exp(scores - jnp.max(scores, axis=-1, keepdims=True))
        probs = expo / jnp.sum(expo, axis=-1, keepdims=True)
        d_probs = dot(d_out, v, 1, 1)
        d_scores = (probs * (d_probs - jnp.sum(probs * d_probs, axis=-1, keepdims=True))).astype(BF16)
        grads[0].append(dot(d_scores, k) * scaling)
        grads[1].append(dot(d_scores, q, 0, 0) * scaling)
        grads[2].append(dot(probs.astype(BF16), d_out, 0, 0))
    d_qkv = jnp.concatenate(grads[0] + grads[1] + grads[2], axis=1).astype(BF16)
    dqkv_ref[...] = d_qkv
    split_out(dot(d_qkv, w_ref[:, : 3 * cols], 1, 1), keep_ref, near_ref, send_ref)


def attention_grad_kernel(n_parts, place_ref, y_ref, x_ref, dqkv_ref, att_ref, vecs_ref, *refs):
    part_refs, (vec_ref, scratch_ref) = refs[:-2], refs[-2:]
    y = y_ref[...]
    d_qkv = dqkv_ref[...]
    cols = d_qkv.shape[1] // 3
    wide = 4 * cols
    grad = jnp.concatenate([dot(x_ref[...], d_qkv, 0, 0), dot(y, att_ref[...], 0, 0)], axis=1)
    scratch_ref[...] = grad.astype(BF16)
    n_dp, length = vec_ref.shape
    piece = HD // n_dp
    total = col_sum(d_qkv.astype(F32))
    out = own_quarter(col_sum(y.astype(F32)), cols, place_ref)
    vec = vecs_ref[...] + (
        heads_back(total[:, :cols], 0, n_dp, length)
        + heads_back(total[:, 2 * cols :], 3 * piece, n_dp, length)
        + heads_back(out, 6 * piece, n_dp, length)
    )
    vec_ref[...] = vec
    if n_parts == 1:
        part_refs[0][...] = scratch_ref[...]
        return
    rows = scratch_ref.shape[0] // n_parts
    for j, part in enumerate(part_refs):
        at = place_ref[0] ^ j
        part[:rows] = scratch_ref[pl.ds(pl.multiple_of(at * rows, rows), rows), :]


def attention_grad_last_kernel(n_parts, place_ref, y_ref, x_ref, dqkv_ref, att_ref, vecs_ref, high_ref, *refs):
    part_refs, (vec_ref, scratch_ref) = refs[:-2], refs[-2:]
    rows = scratch_ref.shape[0] // n_parts
    attention_grad_kernel(
        n_parts, place_ref, y_ref, x_ref, dqkv_ref, att_ref, vecs_ref, *part_refs, vec_ref, scratch_ref
    )
    low = vec_ref[...]
    n_dp, length = low.shape
    width = scratch_ref.shape[1]
    row = lax.broadcasted_iota(jnp.int32, (16, n_dp), 0)
    col = lax.broadcasted_iota(jnp.int32, (16, n_dp), 1)
    lane = lax.broadcasted_iota(jnp.int32, (length, width), 0)
    place = lax.broadcasted_iota(jnp.int32, (length, width), 1)
    spread = exact(low, (place == lane).astype(F32)) + exact(high_ref[...], (place == lane + length).astype(F32))
    for j, part in enumerate(part_refs):
        part[rows:] = exact((col == 2 * (place_ref[0] ^ j) + row).astype(F32), spread).astype(BF16)


def enter_back(dmid_ref, mod_ref, keep_ref, core_ref, far_ref, res_ref):
    incoming = summed(keep_ref, core_ref, far_ref)
    normed, inverse = normalize(res_ref[...])
    g = dmid_ref[...] + norm_back(incoming * (1.0 + mod_ref[1:2]), normed, inverse)
    return g, col_sum(incoming), col_sum(incoming * normed)


def enter_back_kernel(dmid_ref, mod_ref, keep_ref, core_ref, far_ref, res_ref, g_ref, sums_ref):
    g, shift, scale = enter_back(dmid_ref, mod_ref, keep_ref, core_ref, far_ref, res_ref)
    g_ref[...] = g
    sums_ref[...] = jnp.concatenate([shift, scale], axis=0)


def previous_kernel(
    dmid_ref, mod_ref, keep_ref, core_ref, far_ref, res_ref, mod_prev_ref, out_prev_ref, g_ref, sums_ref, dmlp_ref, dgate_ref
):
    g, shift, scale = enter_back(dmid_ref, mod_ref, keep_ref, core_ref, far_ref, res_ref)
    g_ref[...] = g
    sums_ref[...] = jnp.concatenate([shift, scale], axis=0)
    dmlp_ref[...] = (g * mod_prev_ref[5:6]).astype(BF16)
    dgate_ref[...] = col_sum(g * out_prev_ref[...])


def body(
    tokens,
    condition,
    cotangent,
    mod_weight,
    mod_bias,
    qkv_weight,
    qv_bias,
    out_weight,
    out_bias,
    up_weight,
    up_bias,
    down_weight,
    down_bias,
):
    layers = mod_weight.shape[0]
    n_dp = lax.axis_size("dp")
    n_chips = n_dp // 2
    n_all = n_dp * 4
    dp = lax.axis_index("dp")
    z = lax.axis_index("tensor")
    chip = dp // 2
    core = dp % 2
    half = z // 2
    quarter = 2 * (half ^ core) + z % 2
    cols = mod_weight.shape[3]
    rows = tokens.shape[1]
    shard = qkv_weight.shape[1]
    units = up_weight.shape[2]
    piece = qv_bias.shape[3]

    place = jnp.stack([chip, core, quarter, z]).astype(jnp.int32)

    def move(values, target):
        return lax.ppermute(values, AXES, [(i, target(i)) for i in range(n_all)])

    def xor(values, mask):
        return move(values, lambda i: i ^ mask)

    def swap_core_half(i):
        return i & ~6 | (i & HALF) << 1 | (i & CORE) >> 1

    def to_other(i):
        return i ^ CORE if i & CORE else i ^ CORE ^ HALF

    def from_other(i):
        return i ^ CORE ^ HALF if i & CORE else i ^ CORE

    def to_same(i):
        return i ^ HALF if i & CORE else i

    def pick(values, index):
        return lax.dynamic_index_in_dim(values, index, 0, keepdims=False)

    def chip_gather(values, after=()):
        if n_chips > 8:
            groups = [[2 * i + c for i in range(n_chips)] for c in range(2)]
            return lax.all_gather(values, "dp", axis_index_groups=groups)
        parts = [xor(values, CHIP * j) if j else values for j in range(n_chips)]
        out = sds((n_chips,) + values.shape, values.dtype)
        return call(spread_kernel, [out], *parts, scalars=place, after=after, name="spread")[0]

    def chip_swap(values):
        if n_chips > 8:
            groups = [[2 * i + c for i in range(n_chips)] for c in range(2)]
            got = lax.all_to_all(values, "dp", 0, 0, axis_index_groups=groups, tiled=True)
            return [got[i] for i in range(n_chips)]
        return [xor(pick(values, chip ^ j), CHIP * j) if j else pick(values, chip) for j in range(n_chips)]

    def chip_sum(values):
        return sum(part.astype(F32) for part in chip_swap(values))

    def fetch_near(own, *widths):
        widths = widths or (own.shape[1],)
        return call(
            couple_kernel,
            [sds((2, own.shape[0], width), BF16) for width in widths],
            move(own, to_same),
            move(own, to_other),
            scalars=place,
            kept=tuple(range(len(widths))),
            name="couple",
        )

    def fetch_chips(pair):
        if n_chips > 8:
            return [chip_gather(pair)]
        return send_chips([pair] * n_chips, pair.shape[2] < 2 * units)

    def send_chips(parts, at_once=False):
        if at_once:
            return [parts[0]] + [xor(parts[j], CHIP * j) for j in range(1, n_chips)]
        out = [parts[0]] + [xor(parts[j], CHIP * j) for j in range(1, min(3, n_chips))]
        return out + [xor(gate(parts[j], *out[1:]), CHIP * j) for j in range(3, n_chips)]

    def join(parts):
        if n_chips > 8:
            joined, extra = parts[0][:, :, :shard], parts[0][:, :, shard:]
        else:
            height, width = parts[0].shape[1:]
            out = [sds((n_chips, 2, shard, width), BF16)]
            if height > shard:
                out.append(sds((n_chips, 2, height - shard, width), BF16))
            joined, *extra = place_parts(
                join_moves, out, *parts, scalars=place, name="join", copies=len(out) * n_chips
            )
            extra = extra[0] if extra else None
        return joined.reshape(D, joined.shape[3]), extra

    def give_chips(parts, at_once=False):
        if n_chips > 8:
            return chip_swap(parts[0].reshape(n_chips, -1, parts[0].shape[1]))
        return send_chips(parts, at_once)

    def sum_given(parts, height, *after):
        width = sum(part.shape[1] for part in parts) // n_chips
        out = sds((height, width), BF16)
        return call(
            functools.partial(sum_parts_kernel, n_chips, shard),
            [out, out],
            *parts,
            scalars=place,
            after=after,
            stored=tuple(range(len(parts))),
            kept=(0, 1),
            name="sum_parts",
        )

    def give_near(low):
        return [move(low[0], to_same), move(low[1], from_other)]

    def all_rows(values):
        other = xor(values, PARITY)
        return (values, other, xor(values, CORE), xor(other, CORE))

    def sum_rows(keep, near, send):
        got = xor(send, CORE)
        return keep, got, xor((near + got[rows:].astype(F32)).astype(BF16), PARITY)

    cond_full = condition.astype(F32)
    cond_act = jax.nn.silu(cond_full).astype(BF16)
    (cond_pair,) = call(
        couple_kernel, [sds((2, 1, D), BF16)], cond_act, xor(cond_act, CORE), scalars=place, name="couple"
    )
    cond_every = chip_gather(cond_pair).reshape(n_dp, D)
    qv_bias, out_bias, down_bias, up_bias, up_weight, _ = lax.optimization_barrier(
        (qv_bias, out_bias, down_bias, up_bias, up_weight, cond_every)
    )
    moved = move(jnp.concatenate([tokens[0], cotangent[0]]), swap_core_half)
    qkv_own = jnp.transpose(qkv_weight, (0, 2, 1, 3))
    down_own = jnp.transpose(down_weight, (0, 2, 1))

    bias_len = 12 * piece + up_bias.shape[2]
    bias_vec = jnp.concatenate(
        [
            qv_bias.reshape(layers, 6 * piece),
            out_bias.reshape(layers, 3 * piece),
            down_bias.reshape(layers, 3 * piece),
            up_bias.reshape(layers, -1),
        ],
        axis=1,
    )
    bias_block = lax.dynamic_update_slice(jnp.zeros((16, D), BF16), bias_vec, (0, 0))
    def pack_block(layer):
        return call(
            functools.partial(pack_block_kernel, layer),
            [sds((shard, 4 * cols + 2 * units), BF16)],
            qkv_own,
            out_weight,
            up_weight,
            down_own,
            name="pack_block",
        )[0]

    (own_attention,) = call(
        pack_first_kernel, [sds((shard + 16, 4 * cols), BF16)], qkv_own, out_weight, bias_block, name="pack_first"
    )
    (own_mlp,) = call(pack_mlp_kernel, [sds((shard, 2 * units), BF16)], up_weight, down_own, name="pack_mlp")
    (pair_mlp,) = fetch_near(own_mlp)
    attention_weights = [None] * layers
    mlp_weights = [None] * layers
    (pair_attention,) = fetch_near(own_attention)

    cond_slice = lax.dynamic_slice_in_dim(cond_every, dp * shard, shard, 1)
    bias_at = lax.dynamic_update_slice(
        jnp.zeros((layers, 6, cols // HD, HD), F32), mod_bias.astype(F32), (0, 0, 0, dp * piece)
    ).reshape(layers, 6, cols)
    partial_mod = jnp.einsum("ld,ydkc->lykc", cond_slice, mod_weight, preferred_element_type=F32) + bias_at
    mod_sum = chip_sum(partial_mod.reshape((n_chips, 2) + partial_mod.shape[1:]))
    parts_first = fetch_chips(gate(pair_attention, partial_mod))
    mod_sum = gate(mod_sum, pair_mlp)
    attention_weights[0], bias_every = join(parts_first)
    mod_sum = mod_sum + xor(mod_sum, CORE)
    mod_own = pick(mod_sum, half)
    mod_far = pick(mod_sum, half ^ 1)
    quarters = [xor(mod_far if mask & HALF else mod_own, mask) if mask else mod_own for mask in range(4)]
    (modulation,) = call(
        assemble_kernel,
        [sds((layers, 6, D), F32)],
        *quarters,
        scalars=place,
        after=(pair_mlp,) + tuple(parts_first[1:]),
        name="assemble",
    )

    parts_attention = [None] * layers
    parts_mlp = [None] * layers
    parts_mlp[0] = fetch_chips(gate(pair_mlp, modulation))
    qkv_bias_all, wide_bias, up_bias_all = call(
        bias_kernel,
        [sds((layers, 1, 3 * cols), F32), sds((layers, 2, D), F32), sds((layers, 1, units), F32)],
        bias_every.reshape(n_dp * 16, D),
        scalars=place,
        name="bias",
    )
    cotan, d_mlp = call(
        turn_kernel, [sds((rows, D), F32), sds((rows, D), BF16)], moved, modulation[layers - 1], kept=(0,), name="turn"
    )
    d_mlp_rows = all_rows(d_mlp)

    full = 4 * rows
    keep_send = [sds((rows, D), F32), sds((rows, D), F32), sds((full // 2, D), BF16)]
    row_f32 = sds((rows, D), F32)
    row_bf16 = sds((rows, D), BF16)
    line = sds((1, D), F32)
    attention_flops = 2 * full * D * 4 * cols + 4 * full * full * cols
    mlp_flops = 4 * full * D * units

    def parts_of(width, extra=0):
        if n_chips > 8:
            return [sds((D, width), BF16)]
        return [sds((D // n_chips + extra, width), BF16)] * n_chips

    saved = []
    residual, far_residual, attn_in = call(
        enter_kernel,
        [row_f32, row_f32, row_bf16],
        moved,
        modulation[0],
        kept=(1,),
        after=(attention_weights[0],),
        name="enter",
    )
    for layer in range(layers):
        mod = modulation[layer]
        more = layer + 1 < layers
        attn_rows = all_rows(attn_in)
        if more:
            own_block = gate(pack_block(layer + 1), attn_rows[3])
            pair_attention, pair_mlp = fetch_near(own_block, 4 * cols, 2 * units)
            parts_attention[layer + 1] = fetch_chips(gate(pair_attention, parts_mlp[layer][-1]))
            parts_mlp[layer + 1] = fetch_chips(gate(pair_mlp, parts_attention[layer + 1][-1]))
        if layer:
            attention_weights[layer] = join(parts_attention[layer])[0]
        attn_x, qkv, att, *partial = call(
            attention_kernel,
            [sds((full, D), BF16), sds((full, 3 * cols), BF16), sds((full, cols), BF16)] + keep_send,
            *attn_rows,
            attention_weights[layer],
            qkv_bias_all[layer],
            wide_bias[layer, :1],
            flops=attention_flops,
            stored=(4,),
            kept=(0, 1, 2),
            name="attention",
        )
        partial[2] = gate(partial[2], *parts_mlp[layer][1:3])
        branch, far_middle, middle, mlp_in = call(
            middle_kernel,
            [row_f32, row_f32, row_f32, row_bf16],
            residual,
            mod,
            *sum_rows(*partial),
            kept=(0, 1),
            name="middle",
        )
        mlp_rows = all_rows(mlp_in)
        mlp_weights[layer] = join(parts_mlp[layer])[0]
        mlp_x, hidden, act, *partial = call(
            mlp_kernel,
            [sds((full, D), BF16), sds((full, units), F32), sds((full, units), BF16)] + keep_send,
            *mlp_rows,
            mlp_weights[layer],
            up_bias_all[layer],
            wide_bias[layer, 1:],
            flops=mlp_flops,
            stored=(4,),
            kept=(0, 1, 2),
            name="mlp",
        )
        if more:
            partial[2] = gate(partial[2], *parts_attention[layer + 1][1:3])
        arrived = sum_rows(*partial)
        saved.append((far_residual, attn_x, qkv, att, branch, far_middle, mlp_x, hidden, act))
        if more:
            arrived = (gate(arrived[0], parts_attention[layer + 1][-1]),) + arrived[1:]
            mlp_out, far_residual, residual, attn_in = call(
                next_kernel,
                [row_f32, row_f32, row_f32, row_bf16],
                middle,
                mod,
                *arrived,
                modulation[layer + 1],
                kept=(0, 1),
                name="next",
            )
            saved[-1] += (mlp_out,)
        else:
            output, d_gate_two = call(
                last_kernel, [row_bf16, line], middle, mod, *arrived, cotan, stored=(5,), name="last"
            )

    output = move(output, swap_core_half)
    flow = cotan
    mod_lines = [None] * layers
    vecs = [None] * layers
    low = [None] * layers
    near_packs = [None] * layers
    given_attention = [None] * layers
    given_mlp = [None] * layers
    vec_shape = sds((n_dp, bias_len), F32)
    for layer in reversed(range(layers)):
        far_residual, attn_x, qkv, att, branch, far_middle, mlp_x, hidden, act = saved[layer][:9]
        mod = modulation[layer]
        more = layer + 1 < layers
        if more:
            d_mlp_rows = all_rows(d_mlp)
        mlp_y, d_hidden, *partial = call(
            mlp_back_kernel,
            [sds((full, D), BF16), sds((full, units), BF16)] + keep_send,
            *d_mlp_rows,
            mlp_weights[layer],
            hidden,
            flops=mlp_flops,
            stored=(4, 5),
            kept=(0, 1),
            name="mlp_back",
        )
        if more:
            partial[2] = gate(partial[2], *given_mlp[layer + 1][1:3])
        arrived = sum_rows(*partial)
        *grad_mlp, vec_mlp = call(
            mlp_grad_kernel,
            parts_of(2 * units) + [vec_shape],
            mlp_y,
            mlp_x,
            d_hidden,
            act,
            flops=mlp_flops,
            scalars=place,
            scratch=[pltpu.VMEM((D, 2 * units), BF16)],
            stored=(0, 1, 2, 3),
            kept=(0,),
            name="mlp_grad",
        )
        arrived = (gate(arrived[0], grad_mlp[0], *(given_mlp[layer + 1][3:] if more else ())),) + arrived[1:]
        if more:
            grad_mlp = [gate(part, *given_attention[layer + 1][1:]) for part in grad_mlp]
        given_mlp[layer] = give_chips(grad_mlp)
        d_middle, d_branch, sums_mid = call(
            middle_back_kernel,
            [row_f32, row_bf16, sds((3, D), F32)],
            flow,
            mod,
            *arrived,
            far_middle,
            branch,
            stored=(5, 6) if more else (0, 5, 6),
            name="middle_back",
        )
        if more:
            d_branch = gate(d_branch, *given_attention[layer + 1][1:])
            low[layer + 1] = sum_given(list(given_attention[layer + 1]) + list(given_mlp[layer + 1]), shard)
            near_packs[layer + 1] = give_near(low[layer + 1])
        d_branch_rows = all_rows(d_branch)
        attn_y, d_qkv, *partial = call(
            attention_back_kernel,
            [sds((full, D), BF16), sds((full, 3 * cols), BF16)] + keep_send,
            *d_branch_rows,
            attention_weights[layer],
            qkv,
            flops=attention_flops * 2,
            stored=(4, 5),
            kept=(0, 1),
            name="attention_back",
        )
        if more:
            partial[2] = gate(partial[2], *given_mlp[layer][1:3], near_packs[layer + 1][0])
        arrived = sum_rows(*partial)
        *grad_attention, vecs[layer] = call(
            functools.partial(
                attention_grad_kernel if layer or n_chips > 8 else attention_grad_last_kernel,
                1 if n_chips > 8 else n_chips,
            ),
            parts_of(4 * cols, 0 if layer else 16) + [vec_shape],
            attn_y,
            attn_x,
            d_qkv,
            att,
            vec_mlp,
            *(() if layer or n_chips > 8 else (vecs[1],)),
            flops=attention_flops,
            scalars=place,
            scratch=[pltpu.VMEM((D, 4 * cols), BF16)],
            stored=(0, 1, 2, 3),
            kept=(0,),
            name="attention_grad",
        )
        after = (grad_attention[0],)
        if layer == 0:
            after = after + tuple(given_mlp[0][3:]) + tuple(near_packs[upper][1] for upper in range(1, layers))
        if layer == 0:
            height = 2 * shard + 16
            if n_chips > 8:
                rows_bias = jnp.concatenate([vecs[i] for i in range(layers)], axis=1).astype(BF16)
                rows_bias = jnp.pad(
                    rows_bias.reshape(n_chips, 2, -1), ((0, 0), (0, 14), (0, 4 * cols - layers * bias_len))
                )
                rows_all = jnp.concatenate(
                    [grad_attention[0].reshape(n_chips, 2 * shard, 4 * cols), rows_bias], axis=1
                )
                grad_attention = [rows_all.reshape(n_chips * height, 4 * cols)]
        given_attention[layer] = give_chips([gate(part, *given_mlp[layer][1:]) for part in grad_attention], True)
        if layer:
            flow, sums_in, d_mlp, gate_next = call(
                previous_kernel,
                [row_f32, sds((2, D), F32), row_bf16, line],
                d_middle,
                mod,
                *arrived,
                far_residual,
                modulation[layer - 1],
                saved[layer - 1][9],
                stored=(5, 7),
                after=after,
                name="previous",
            )
        else:
            flow, sums_in = call(
                enter_back_kernel,
                [row_f32, sds((2, D), F32)],
                d_middle,
                mod,
                *arrived,
                far_residual,
                stored=(5,),
                after=after,
                name="enter_back",
            )
            gate_next = None
        mod_lines[layer] = jnp.concatenate([sums_in, sums_mid, d_gate_two], axis=0)
        d_gate_two = gate_next

    d_mod = jnp.stack(mod_lines)
    d_mod = d_mod + xor(d_mod, CORE)
    d_mod = (d_mod + xor(d_mod, PARITY)).astype(BF16).reshape(layers * 6, 4, cols)
    d_mod = jnp.transpose(d_mod, (1, 0, 2))
    mine = pick(d_mod, z)
    far = xor(pick(d_mod, z ^ HALF), HALF)
    d_mod_pair = jnp.where(half == 0, jnp.stack([mine, far]), jnp.stack([far, mine]))
    low_attention = sum_given(list(given_attention[0]), shard + 16)
    near_attention = give_near(low_attention)
    near_mlp = give_near(sum_given(list(given_mlp[0]), shard))
    near_packs[0] = near_attention + near_mlp
    d_mod_pair = gate(d_mod_pair, *given_attention[0][1:])
    d_mod_every = gate(chip_gather(d_mod_pair), *near_mlp).reshape(n_dp, layers, 6, cols)
    grad_mod_w = jnp.einsum("ld,lykc->ykdc", cond_slice, d_mod_every, preferred_element_type=F32)
    grad_mod_w = jnp.transpose(grad_mod_w, (0, 2, 1, 3))
    grad_mod_b = jnp.sum(d_mod_every.astype(F32), axis=0).reshape(layers, 6, cols // HD, HD)
    grad_mod_b = lax.dynamic_slice_in_dim(grad_mod_b, dp * piece, piece, 3)
    cond_pieces = jnp.einsum("lykc,ydkc->ld", d_mod_every, mod_weight, preferred_element_type=F32)
    mixed = jnp.stack(chip_swap(cond_pieces.reshape(n_chips, 2, shard)))
    if n_chips <= 8:
        mixed = jnp.take(mixed, chip ^ jnp.arange(n_chips), axis=0)
    cond_pieces = jnp.transpose(mixed, (1, 0, 2))
    cond_pieces = gate(cond_pieces, *low_attention)
    cond_mine = pick(cond_pieces, core)
    cond_sent = xor(pick(cond_pieces, core ^ 1), CORE)
    cond_total = jnp.where(
        core == 0, jnp.stack([cond_mine, cond_sent], axis=1), jnp.stack([cond_sent, cond_mine], axis=1)
    ).reshape(1, D)
    cond_total = gate(cond_total, *near_attention)
    cond_total = cond_total + xor(cond_total, PARITY)
    cond_total = cond_total + xor(cond_total, HALF)
    sigmoid_cond = jax.nn.sigmoid(cond_full)
    grad_condition = cond_total * sigmoid_cond * (1.0 + cond_full * (1.0 - sigmoid_cond))

    grad_tokens = move(flow, swap_core_half)
    output, grad_tokens, grad_qkv, grad_out, grad_up, grad_down, vec = call(
        finish_kernel,
        [
            row_bf16,
            row_f32,
            sds((layers, 3, shard, cols), F32),
            sds((layers, cols, shard), F32),
            sds((layers, shard, units), F32),
            sds((layers, shard, units), F32),
            sds((8, 4 * cols), F32),
        ],
        output,
        grad_tokens,
        *[part for layer in range(layers) for part in near_packs[layer]],
        kept=(0, 1, 2, 3, 4, 5),
        name="finish",
    )
    vec = vec[0, : layers * bias_len].reshape(layers, bias_len)
    vec_heads = vec[:, : 12 * piece].reshape(layers, 4, 3, piece)
    return (
        output[None],
        grad_tokens[None],
        grad_condition,
        grad_mod_w,
        grad_mod_b,
        jnp.transpose(grad_qkv, (0, 2, 1, 3)),
        vec_heads[:, :2],
        grad_out,
        vec_heads[:, 2],
        grad_up,
        vec[:, 12 * piece :].reshape(layers, 1, -1),
        jnp.transpose(grad_down, (0, 2, 1)),
        vec_heads[:, 3],
    )


def solution(mesh):
    in_specs = (
        P("dp", "tensor", None),
        P("dp", None),
        P("dp", "tensor", None),
        P(None, "dp", None, "tensor"),
        P(None, None, "tensor", "dp"),
        P(None, "dp", None, "tensor"),
        P(None, None, "tensor", "dp"),
        P(None, "tensor", "dp"),
        P(None, "tensor", "dp"),
        P(None, "dp", "tensor"),
        P(None, "tensor", "dp"),
        P(None, "tensor", "dp"),
        P(None, "tensor", "dp"),
    )
    out_specs = (
        P("dp", "tensor", None),
        P("dp", "tensor", None),
        P("dp", None),
        P(None, "dp", None, "tensor"),
        P(None, None, "tensor", "dp"),
        P(None, "dp", None, "tensor"),
        P(None, None, "tensor", "dp"),
        P(None, "tensor", "dp"),
        P(None, "tensor", "dp"),
        P(None, "dp", "tensor"),
        P(None, "tensor", "dp"),
        P(None, "tensor", "dp"),
        P(None, "tensor", "dp"),
    )
    return jax.shard_map(body, mesh=mesh, in_specs=in_specs, out_specs=out_specs, check_vma=False)
```

```python
import functools
import math

import jax
import jax.numpy as jnp
from jax import lax
from jax.experimental import pallas as pl
from jax.experimental.pallas import tpu as pltpu
from jax.sharding import PartitionSpec as P

D = 768
HD = 64
EPS = 1e-06
AXES = ("dp", "tensor")
F32 = jnp.float32
BF16 = jnp.bfloat16
VMEM_LIMIT = 16 * 1024 * 1024

PARITY = 1
HALF = 2
CORE = 4
CHIP = 8


class Stored:
    def __init__(self, source, target, sem, local):
        self.copy = pltpu.make_async_copy(source, target, sem)
        self.local = local
        self.shape = local.shape
        self.busy = False
        self.dirty = False

    def start(self):
        self.copy.start()
        self.busy = True
        self.dirty = False

    def settle(self):
        if self.busy:
            self.copy.wait()
            self.busy = False

    def __getitem__(self, index):
        self.settle()
        return self.local[index]

    def __setitem__(self, index, value):
        self.local[index] = value
        self.dirty = True
        if index is Ellipsis:
            self.start()


def call(
    kernel, out_shape, *args, flops=0, name=None, scalars=None, after=(), scratch=(), stored=(), kept=(), window=()
):
    size = sum(a.size * a.dtype.itemsize for a in args) + sum(math.prod(o.shape) * o.dtype.itemsize for o in out_shape)
    hbm = pl.BlockSpec(memory_space=pltpu.HBM)
    vmem = pl.BlockSpec(memory_space=pltpu.VMEM)
    in_specs = [hbm if i in stored else vmem for i in range(len(args))]
    out_specs = [hbm if i in kept else vmem for i in range(len(out_shape))]
    window = dict(window)
    copies = [pltpu.VMEM((args[i].shape[0], window[i][1]) if i in window else args[i].shape, args[i].dtype) for i in stored]
    copies += [pltpu.VMEM(out_shape[i].shape, out_shape[i].dtype) for i in kept]
    lead = 0
    if after:
        args = (gate(args[0], *after),) + args[1:]
    if scalars is not None:
        args = (scalars,) + args
        in_specs = [pl.BlockSpec(memory_space=pltpu.SMEM)] + in_specs
        lead = 1

    def run(*refs):
        ins = list(refs[: len(args)])
        outs = list(refs[len(args) : len(args) + len(out_shape)])
        rest = refs[len(args) + len(out_shape) :]
        own, local = rest[: len(scratch)], rest[len(scratch) :]
        held = []
        for n, i in enumerate(stored):
            source = ins[lead + i].at[:, pl.ds(*window[i])] if i in window else ins[lead + i]
            held.append(Stored(source, local[n], local[-1].at[n], local[n]))
            held[-1].start()
            ins[lead + i] = held[-1]
        for n, i in enumerate(kept, len(stored)):
            held.append(Stored(local[n], outs[i], local[-1].at[n], local[n]))
            outs[i] = held[-1]
        kernel(*ins, *outs, *own)
        for item in held:
            if item.dirty:
                item.start()
        for item in held:
            item.settle()

    return pl.pallas_call(
        run,
        out_shape=out_shape,
        in_specs=in_specs,
        out_specs=out_specs,
        scratch_shapes=list(scratch) + copies + ([pltpu.SemaphoreType.DMA((len(copies),))] if copies else []),
        compiler_params=pltpu.CompilerParams(vmem_limit_bytes=VMEM_LIMIT),
        cost_estimate=pl.CostEstimate(flops=flops, bytes_accessed=size, transcendentals=0),
        name=name,
    )(*args)


def gate(value, *others):
    return lax.optimization_barrier((value,) + others)[0]


def place_parts(kernel, out_shape, *args, scalars, name, copies):
    count = len(args)

    def run(place_ref, *refs):
        outs = refs[count : count + len(out_shape)]
        sems = refs[-1]
        moves = [
            pltpu.make_async_copy(source, target, sems.at[n])
            for n, (source, target) in enumerate(kernel(place_ref, refs[:count], outs))
        ]
        for item in moves:
            item.start()
        for item in moves:
            item.wait()

    size = sum(a.size * a.dtype.itemsize for a in args)
    return pl.pallas_call(
        run,
        out_shape=out_shape,
        in_specs=[pl.BlockSpec(memory_space=pltpu.SMEM)]
        + [pl.BlockSpec(memory_space=pltpu.HBM)] * count,
        out_specs=[pl.BlockSpec(memory_space=pltpu.HBM)] * len(out_shape),
        scratch_shapes=[pltpu.SemaphoreType.DMA((copies,))],
        compiler_params=pltpu.CompilerParams(vmem_limit_bytes=VMEM_LIMIT),
        cost_estimate=pl.CostEstimate(flops=0, bytes_accessed=2 * size, transcendentals=0),
        name=name,
    )(scalars, *args)


def sds(shape, dtype):
    return jax.ShapeDtypeStruct(shape, dtype)


def dot(a, b, ca=1, cb=0):
    return lax.dot_general(a, b, (((ca,), (cb,)), ((), ())), preferred_element_type=F32)


def normalize(values):
    centered = values - jnp.mean(values, axis=-1, keepdims=True)
    inverse = lax.rsqrt(jnp.mean(centered * centered, axis=-1, keepdims=True) + EPS)
    return centered * inverse, inverse


def norm_back(incoming, normed, inverse):
    average = jnp.mean(incoming, axis=-1, keepdims=True)
    along = jnp.mean(incoming * normed, axis=-1, keepdims=True)
    return inverse * (incoming - average - normed * along)


def col_sum(values):
    return jnp.sum(values, axis=0, keepdims=True)


def modulate(values, mod, shift, scale):
    normed, _ = normalize(values)
    return (normed * (1.0 + mod[scale : scale + 1]) + mod[shift : shift + 1]).astype(BF16)


def rows_of(refs):
    return jnp.concatenate([ref[...] for ref in refs], axis=0)


def split_out(total, keep_ref, near_ref, send_ref):
    quarter = total.shape[0] // 4
    keep_ref[...] = total[:quarter]
    near_ref[...] = total[quarter : 2 * quarter]
    send_ref[...] = total[2 * quarter :].astype(BF16)


def summed(keep_ref, core_ref, far_ref):
    return keep_ref[...] + core_ref[: keep_ref.shape[0]].astype(F32) + far_ref[...].astype(F32)


def attention_pack(layer, qkv_ref, out_ref):
    out = out_ref[layer].astype(F32).T.astype(BF16)
    return jnp.concatenate([qkv_ref[layer, 0], qkv_ref[layer, 1], qkv_ref[layer, 2], out], axis=1)


def pack_block_kernel(layer, qkv_ref, out_ref, up_ref, down_ref, pack_ref):
    wide = 4 * out_ref.shape[1]
    units = up_ref.shape[2]
    pack_ref[:, :wide] = attention_pack(layer, qkv_ref, out_ref)
    pack_ref[:, wide : wide + units] = up_ref[layer]
    pack_ref[:, wide + units :] = down_ref[layer]


def pack_first_kernel(qkv_ref, out_ref, bias_ref, pack_ref):
    shard = out_ref.shape[2]
    pack_ref[:shard] = attention_pack(0, qkv_ref, out_ref)
    pack_ref[shard:] = bias_ref[...]


def pack_mlp_kernel(up_ref, down_ref, pack_ref):
    units = up_ref.shape[2]
    pack_ref[:, :units] = up_ref[0]
    pack_ref[:, units:] = down_ref[0]


def join_moves(place_ref, ins, outs):
    shard = outs[0].shape[2]
    moves = []
    for j, part in enumerate(ins):
        at = place_ref[0] ^ j
        moves.append((part.at[:, :shard], outs[0].at[at]))
        if len(outs) == 2:
            moves.append((part.at[:, shard:], outs[1].at[at]))
    return moves


def assemble_kernel(place_ref, *refs):
    parts, out_ref = refs[:-1], refs[-1]
    cols = parts[0].shape[2]
    for layer in range(out_ref.shape[0]):
        for at in range(4):
            quarter = sum(
                jnp.where(place_ref[3] ^ mask == at, part[layer], 0.0) for mask, part in enumerate(parts)
            )
            out_ref[layer, :, at * cols : (at + 1) * cols] = quarter


def spread_kernel(place_ref, *refs):
    parts, out_ref = refs[:-1], refs[-1]
    for j, part in enumerate(parts):
        out_ref[place_ref[0] ^ j] = part[...]


def couple_kernel(place_ref, own_ref, other_ref, *out_refs):
    first = place_ref[1] == 0
    at = 0
    for out_ref in out_refs:
        end = at + out_ref.shape[-1]
        own, other = own_ref[..., at:end], other_ref[..., at:end]
        out_ref[0] = jnp.where(first, own, other)
        out_ref[1] = jnp.where(first, other, own)
        at = end


def head_select(n_dp, piece, cols):
    row = lax.broadcasted_iota(jnp.int32, (3 * piece, cols), 0)
    col = lax.broadcasted_iota(jnp.int32, (3 * piece, cols), 1)
    return (row == col // HD * piece + col % piece).astype(F32)


def head_mask(n_dp, piece, cols):
    row = lax.broadcasted_iota(jnp.int32, (n_dp, cols), 0)
    col = lax.broadcasted_iota(jnp.int32, (n_dp, cols), 1)
    return (col % HD // piece == row).astype(F32)


def exact(a, b):
    return lax.dot_general(
        a, b, (((1,), (0,)), ((), ())), preferred_element_type=F32, precision=lax.Precision.HIGHEST
    )


def heads_back(line, at, n_dp, length):
    cols, piece = line.shape[1], HD // n_dp
    row = lax.broadcasted_iota(jnp.int32, (length, cols), 0) - at
    col = lax.broadcasted_iota(jnp.int32, (length, cols), 1)
    select = (row == col // HD * piece + col % piece).astype(F32)
    return lax.dot_general(
        head_mask(n_dp, piece, cols) * line,
        select,
        (((1,), (1,)), ((), ())),
        preferred_element_type=F32,
        precision=lax.Precision.HIGHEST,
    )


def units_back(line, at, n_dp, length):
    units = line.shape[1]
    width = units // n_dp
    row = lax.broadcasted_iota(jnp.int32, (length, units), 0) - at
    col = lax.broadcasted_iota(jnp.int32, (length, units), 1)
    mask = (
        lax.broadcasted_iota(jnp.int32, (n_dp, units), 1) // width
        == lax.broadcasted_iota(jnp.int32, (n_dp, units), 0)
    )
    return lax.dot_general(
        mask.astype(F32) * line,
        (col % width == row).astype(F32),
        (((1,), (1,)), ((), ())),
        preferred_element_type=F32,
        precision=lax.Precision.HIGHEST,
    )


def own_quarter(line, cols, place_ref):
    return sum(
        jnp.where(place_ref[2] == i, line[:, i * cols : (i + 1) * cols], 0.0) for i in range(line.shape[1] // cols)
    )


def bias_kernel(place_ref, vec_ref, qkv_ref, wide_ref, up_ref):
    n_dp, piece = vec_ref.shape[0] // 16, HD * 16 // vec_ref.shape[0]
    vec_row = lax.broadcasted_iota(jnp.int32, (n_dp, vec_ref.shape[0]), 0)
    vec_col = lax.broadcasted_iota(jnp.int32, (n_dp, vec_ref.shape[0]), 1)
    cols, units = qkv_ref.shape[2] // 3, up_ref.shape[2]
    select, mask = head_select(n_dp, piece, cols), head_mask(n_dp, piece, cols)
    width = units // n_dp
    row = lax.broadcasted_iota(jnp.int32, (width, units), 0)
    col = lax.broadcasted_iota(jnp.int32, (width, units), 1)
    up_select = (col % width == row).astype(F32)
    up_row = lax.broadcasted_iota(jnp.int32, (n_dp, units), 0)
    up_col = lax.broadcasted_iota(jnp.int32, (n_dp, units), 1)
    up_mask = (up_col // width == up_row).astype(F32)
    quarters = wide_ref.shape[2] // cols
    place = lax.broadcasted_iota(jnp.int32, (1, quarters * cols), 1) // cols == place_ref[2]
    for layer in range(qkv_ref.shape[0]):
        vec = dot((vec_col == 16 * vec_row + layer).astype(BF16), vec_ref[...])
        heads = [col_sum(exact(vec[:, 3 * t * piece : 3 * (t + 1) * piece], select) * mask) for t in range(4)]
        qkv_ref[layer] = jnp.concatenate([heads[0], jnp.zeros_like(heads[0]), heads[1]], axis=1)
        for t in range(2):
            wide_ref[layer, t : t + 1] = jnp.where(place, jnp.concatenate([heads[2 + t]] * quarters, axis=1), 0.0)
        up_ref[layer] = col_sum(exact(vec[:, 12 * piece : 12 * piece + width], up_select) * up_mask)


def sum_parts_kernel(count, shard, place_ref, *refs):
    parts, (same_ref, other_ref) = refs[:-2], refs[-2:]
    first = place_ref[1] == 0
    at = 0
    for start in range(0, len(parts), count):
        low = sum(part[...].astype(F32) for part in parts[start : start + count])
        end = at + low.shape[1]
        mine, far = low[:shard], low[shard : 2 * shard]
        same_ref[:shard, at:end] = jnp.where(first, mine, far).astype(BF16)
        other_ref[:shard, at:end] = jnp.where(first, far, mine).astype(BF16)
        if low.shape[0] > 2 * shard:
            mine, far = low[2 * shard : 2 * shard + 1], low[2 * shard + 1 : 2 * shard + 2]
            same_ref[shard:, at:end] = jnp.broadcast_to(jnp.where(first, mine, far), (16, end - at)).astype(BF16)
            other_ref[shard:, at:end] = jnp.broadcast_to(jnp.where(first, far, mine), (16, end - at)).astype(BF16)
        at = end


def finish_kernel(last_ref, flow_ref, *refs):
    parts, (last_out_ref, flow_out_ref, qkv_ref, out_ref, up_ref, down_ref, vec_ref) = refs[:-7], refs[-7:]
    last_out_ref[...] = last_ref[...]
    flow_out_ref[...] = flow_ref[...]
    shard, cols, units = up_ref.shape[1], out_ref.shape[1], up_ref.shape[2]
    for layer in range(qkv_ref.shape[0]):
        if layer == 0:
            total = parts[0][...].astype(F32) + parts[1][...].astype(F32)
            vec_ref[...] = total[shard : shard + 8]
            mlp = parts[2][...].astype(F32) + parts[3][...].astype(F32)
        else:
            total = parts[2 * layer + 2][...].astype(F32) + parts[2 * layer + 3][...].astype(F32)
            mlp = total[:, 4 * cols :]
        for i in range(3):
            qkv_ref[layer, i] = total[:shard, i * cols : (i + 1) * cols]
        out_ref[layer] = total[:shard, 3 * cols : 4 * cols].T
        up_ref[layer] = mlp[:, :units]
        down_ref[layer] = mlp[:, units:]


def enter_kernel(moved_ref, mod_ref, res_ref, far_res_ref, in_ref):
    residual = moved_ref[: res_ref.shape[0]].astype(F32)
    far_res_ref[...] = residual
    res_ref[...] = residual
    in_ref[...] = modulate(residual, mod_ref[...], 0, 1)


def attention_kernel(x0, x1, x2, x3, w_ref, bias_ref, bo_ref, x_ref, qkv_ref, att_ref, keep_ref, near_ref, send_ref):
    x = rows_of((x0, x1, x2, x3))
    x_ref[...] = x
    cols = w_ref.shape[1] // 4
    qkv = (dot(x, w_ref[:, : 3 * cols]) + bias_ref[...]).astype(BF16)
    qkv_ref[...] = qkv
    parts = []
    for head in range(cols // HD):
        at = head * HD
        q = qkv[:, at : at + HD]
        k = qkv[:, cols + at : cols + at + HD]
        v = qkv[:, 2 * cols + at : 2 * cols + at + HD]
        scores = dot(q, k, 1, 1) * (1.0 / math.sqrt(HD))
        expo = jnp.exp(scores - jnp.max(scores, axis=-1, keepdims=True))
        probs = expo / jnp.sum(expo, axis=-1, keepdims=True)
        parts.append(dot(probs.astype(BF16), v))
    att = jnp.concatenate(parts, axis=1).astype(BF16)
    att_ref[...] = att
    split_out(dot(att, w_ref[:, 3 * cols :], 1, 1) + bo_ref[...], keep_ref, near_ref, send_ref)


def middle_kernel(res_ref, mod_ref, keep_ref, core_ref, far_ref, branch_ref, far_mid_ref, mid_ref, in_ref):
    mod = mod_ref[...]
    branch = summed(keep_ref, core_ref, far_ref)
    branch_ref[...] = branch
    middle = res_ref[...] + mod[2:3] * branch
    far_mid_ref[...] = middle
    mid_ref[...] = middle
    in_ref[...] = modulate(middle, mod, 3, 4)


def mlp_kernel(x0, x1, x2, x3, w_ref, bu_ref, bd_ref, x_ref, hid_ref, act_ref, keep_ref, near_ref, send_ref):
    x = rows_of((x0, x1, x2, x3))
    x_ref[...] = x
    units = w_ref.shape[1] // 2
    hidden = dot(x, w_ref[:, :units]) + bu_ref[...]
    hid_ref[...] = hidden
    act = (0.5 * hidden * (1.0 + lax.erf(hidden * 0.7071067811865476))).astype(BF16)
    act_ref[...] = act
    split_out(dot(act, w_ref[:, units:], 1, 1) + bd_ref[...], keep_ref, near_ref, send_ref)


def next_kernel(
    mid_ref, mod_ref, keep_ref, core_ref, far_ref, mod_next_ref, out_ref, far_res_ref, res_ref, in_ref
):
    mlp_out = summed(keep_ref, core_ref, far_ref)
    out_ref[...] = mlp_out
    residual = mid_ref[...] + mod_ref[5:6] * mlp_out
    far_res_ref[...] = residual
    res_ref[...] = residual
    in_ref[...] = modulate(residual, mod_next_ref[...], 0, 1)


def last_kernel(mid_ref, mod_ref, keep_ref, core_ref, far_ref, g_ref, out_ref, dgate_ref):
    mlp_out = summed(keep_ref, core_ref, far_ref)
    out_ref[...] = (mid_ref[...] + mod_ref[5:6] * mlp_out).astype(BF16)
    dgate_ref[...] = col_sum(g_ref[...] * mlp_out)


def turn_kernel(moved_ref, mod_ref, g_ref, dmlp_ref):
    g = moved_ref[dmlp_ref.shape[0] :].astype(F32)
    g_ref[...] = g
    dmlp_ref[...] = (g * mod_ref[5:6]).astype(BF16)


def mlp_back_kernel(x0, x1, x2, x3, w_ref, hid_ref, x_ref, dhid_ref, keep_ref, near_ref, send_ref):
    x = rows_of((x0, x1, x2, x3))
    x_ref[...] = x
    units = w_ref.shape[1] // 2
    hidden = hid_ref[...]
    d_active = dot(x, w_ref[:, units:])
    cumulative = 0.5 * (1.0 + lax.erf(hidden * 0.7071067811865476))
    density = jnp.exp(-0.5 * hidden * hidden) * 0.3989422804014327
    d_hidden = (d_active * (cumulative + hidden * density)).astype(BF16)
    dhid_ref[...] = d_hidden
    split_out(dot(d_hidden, w_ref[:, :units], 1, 1), keep_ref, near_ref, send_ref)


def give_parts(grad, place_ref, scratch_ref, part_refs):
    if len(part_refs) == 1:
        part_refs[0][...] = grad.astype(BF16)
        return
    scratch_ref[...] = grad.astype(BF16)
    rows = part_refs[0].shape[0]
    for j, part in enumerate(part_refs):
        start = pl.multiple_of((place_ref[0] ^ j) * rows, rows)
        part[...] = scratch_ref[pl.ds(start, rows), :]


def mlp_grad_kernel(place_ref, y_ref, x_ref, dhid_ref, act_ref, *refs):
    part_refs, (vec_ref, scratch_ref) = refs[:-2], refs[-2:]
    y = y_ref[...]
    d_hidden = dhid_ref[...]
    grad = jnp.concatenate([dot(x_ref[...], d_hidden, 0, 0), dot(y, act_ref[...], 0, 0)], axis=1)
    give_parts(grad, place_ref, scratch_ref, part_refs)
    n_dp, length = vec_ref.shape
    piece = HD // n_dp
    cols = y.shape[1] // 4
    down = own_quarter(col_sum(y.astype(F32)), cols, place_ref)
    up = col_sum(d_hidden.astype(F32))
    vec_ref[...] = heads_back(down, 9 * piece, n_dp, length) + units_back(up, 12 * piece, n_dp, length)


def middle_back_kernel(g_ref, mod_ref, keep_ref, core_ref, far_ref, mid_ref, branch_ref, dmid_ref, dbranch_ref, sums_ref):
    mod = mod_ref[...]
    incoming = summed(keep_ref, core_ref, far_ref)
    normed, inverse = normalize(mid_ref[...])
    d_middle = g_ref[...] + norm_back(incoming * (1.0 + mod[4:5]), normed, inverse)
    dmid_ref[...] = d_middle
    dbranch_ref[...] = (d_middle * mod[2:3]).astype(BF16)
    sums_ref[...] = jnp.concatenate(
        [col_sum(d_middle * branch_ref[...]), col_sum(incoming), col_sum(incoming * normed)], axis=0
    )


def attention_back_kernel(x0, x1, x2, x3, w_ref, qkv_ref, x_ref, dqkv_ref, keep_ref, near_ref, send_ref):
    x = rows_of((x0, x1, x2, x3))
    x_ref[...] = x
    cols = w_ref.shape[1] // 4
    qkv = qkv_ref[...]
    scaling = 1.0 / math.sqrt(HD)
    d_att = dot(x, w_ref[:, 3 * cols :]).astype(BF16)
    grads = ([], [], [])
    for head in range(cols // HD):
        at = head * HD
        q = qkv[:, at : at + HD]
        k = qkv[:, cols + at : cols + at + HD]
        v = qkv[:, 2 * cols + at : 2 * cols + at + HD]
        d_out = d_att[:, at : at + HD]
        scores = dot(q, k, 1, 1) * scaling
        expo = jnp.exp(scores - jnp.max(scores, axis=-1, keepdims=True))
        probs = expo / jnp.sum(expo, axis=-1, keepdims=True)
        d_probs = dot(d_out, v, 1, 1)
        d_scores = (probs * (d_probs - jnp.sum(probs * d_probs, axis=-1, keepdims=True))).astype(BF16)
        grads[0].append(dot(d_scores, k) * scaling)
        grads[1].append(dot(d_scores, q, 0, 0) * scaling)
        grads[2].append(dot(probs.astype(BF16), d_out, 0, 0))
    d_qkv = jnp.concatenate(grads[0] + grads[1] + grads[2], axis=1).astype(BF16)
    dqkv_ref[...] = d_qkv
    split_out(dot(d_qkv, w_ref[:, : 3 * cols], 1, 1), keep_ref, near_ref, send_ref)


def attention_grad_kernel(n_parts, place_ref, y_ref, x_ref, dqkv_ref, att_ref, vecs_ref, *refs):
    part_refs, (vec_ref, scratch_ref) = refs[:-2], refs[-2:]
    y = y_ref[...]
    d_qkv = dqkv_ref[...]
    cols = d_qkv.shape[1] // 3
    wide = 4 * cols
    grad = jnp.concatenate([dot(x_ref[...], d_qkv, 0, 0), dot(y, att_ref[...], 0, 0)], axis=1)
    scratch_ref[...] = grad.astype(BF16)
    n_dp, length = vec_ref.shape
    piece = HD // n_dp
    total = col_sum(d_qkv.astype(F32))
    out = own_quarter(col_sum(y.astype(F32)), cols, place_ref)
    vec = vecs_ref[...] + (
        heads_back(total[:, :cols], 0, n_dp, length)
        + heads_back(total[:, 2 * cols :], 3 * piece, n_dp, length)
        + heads_back(out, 6 * piece, n_dp, length)
    )
    vec_ref[...] = vec
    if n_parts == 1:
        part_refs[0][...] = scratch_ref[...]
        return
    rows = scratch_ref.shape[0] // n_parts
    for j, part in enumerate(part_refs):
        at = place_ref[0] ^ j
        part[:rows] = scratch_ref[pl.ds(pl.multiple_of(at * rows, rows), rows), :]


def attention_grad_last_kernel(n_parts, place_ref, y_ref, x_ref, dqkv_ref, att_ref, vecs_ref, high_ref, *refs):
    part_refs, (vec_ref, scratch_ref) = refs[:-2], refs[-2:]
    rows = scratch_ref.shape[0] // n_parts
    attention_grad_kernel(
        n_parts, place_ref, y_ref, x_ref, dqkv_ref, att_ref, vecs_ref, *part_refs, vec_ref, scratch_ref
    )
    low = vec_ref[...]
    n_dp, length = low.shape
    width = scratch_ref.shape[1]
    row = lax.broadcasted_iota(jnp.int32, (16, n_dp), 0)
    col = lax.broadcasted_iota(jnp.int32, (16, n_dp), 1)
    lane = lax.broadcasted_iota(jnp.int32, (length, width), 0)
    place = lax.broadcasted_iota(jnp.int32, (length, width), 1)
    spread = exact(low, (place == lane).astype(F32)) + exact(high_ref[...], (place == lane + length).astype(F32))
    for j, part in enumerate(part_refs):
        part[rows:] = exact((col == 2 * (place_ref[0] ^ j) + row).astype(F32), spread).astype(BF16)


def enter_back(dmid_ref, mod_ref, keep_ref, core_ref, far_ref, res_ref):
    incoming = summed(keep_ref, core_ref, far_ref)
    normed, inverse = normalize(res_ref[...])
    g = dmid_ref[...] + norm_back(incoming * (1.0 + mod_ref[1:2]), normed, inverse)
    return g, col_sum(incoming), col_sum(incoming * normed)


def enter_back_kernel(dmid_ref, mod_ref, keep_ref, core_ref, far_ref, res_ref, g_ref, sums_ref):
    g, shift, scale = enter_back(dmid_ref, mod_ref, keep_ref, core_ref, far_ref, res_ref)
    g_ref[...] = g
    sums_ref[...] = jnp.concatenate([shift, scale], axis=0)


def previous_kernel(
    dmid_ref, mod_ref, keep_ref, core_ref, far_ref, res_ref, mod_prev_ref, out_prev_ref, g_ref, sums_ref, dmlp_ref, dgate_ref
):
    g, shift, scale = enter_back(dmid_ref, mod_ref, keep_ref, core_ref, far_ref, res_ref)
    g_ref[...] = g
    sums_ref[...] = jnp.concatenate([shift, scale], axis=0)
    dmlp_ref[...] = (g * mod_prev_ref[5:6]).astype(BF16)
    dgate_ref[...] = col_sum(g * out_prev_ref[...])


def body(
    tokens,
    condition,
    cotangent,
    mod_weight,
    mod_bias,
    qkv_weight,
    qv_bias,
    out_weight,
    out_bias,
    up_weight,
    up_bias,
    down_weight,
    down_bias,
):
    layers = mod_weight.shape[0]
    n_dp = lax.axis_size("dp")
    n_chips = n_dp // 2
    n_all = n_dp * 4
    dp = lax.axis_index("dp")
    z = lax.axis_index("tensor")
    chip = dp // 2
    core = dp % 2
    half = z // 2
    quarter = 2 * (half ^ core) + z % 2
    cols = mod_weight.shape[3]
    rows = tokens.shape[1]
    shard = qkv_weight.shape[1]
    units = up_weight.shape[2]
    piece = qv_bias.shape[3]

    place = jnp.stack([chip, core, quarter, z]).astype(jnp.int32)

    def move(values, target):
        return lax.ppermute(values, AXES, [(i, target(i)) for i in range(n_all)])

    def xor(values, mask):
        return move(values, lambda i: i ^ mask)

    def swap_core_half(i):
        return i & ~6 | (i & HALF) << 1 | (i & CORE) >> 1

    def to_other(i):
        return i ^ CORE if i & CORE else i ^ CORE ^ HALF

    def from_other(i):
        return i ^ CORE ^ HALF if i & CORE else i ^ CORE

    def to_same(i):
        return i ^ HALF if i & CORE else i

    def pick(values, index):
        return lax.dynamic_index_in_dim(values, index, 0, keepdims=False)

    def chip_gather(values, after=()):
        if n_chips > 8:
            groups = [[2 * i + c for i in range(n_chips)] for c in range(2)]
            return lax.all_gather(values, "dp", axis_index_groups=groups)
        parts = [xor(values, CHIP * j) if j else values for j in range(n_chips)]
        out = sds((n_chips,) + values.shape, values.dtype)
        return call(spread_kernel, [out], *parts, scalars=place, after=after, name="spread")[0]

    def chip_swap(values):
        if n_chips > 8:
            groups = [[2 * i + c for i in range(n_chips)] for c in range(2)]
            got = lax.all_to_all(values, "dp", 0, 0, axis_index_groups=groups, tiled=True)
            return [got[i] for i in range(n_chips)]
        return [xor(pick(values, chip ^ j), CHIP * j) if j else pick(values, chip) for j in range(n_chips)]

    def chip_sum(values):
        return sum(part.astype(F32) for part in chip_swap(values))

    def fetch_near(own, *widths):
        widths = widths or (own.shape[1],)
        return call(
            couple_kernel,
            [sds((2, own.shape[0], width), BF16) for width in widths],
            move(own, to_same),
            move(own, to_other),
            scalars=place,
            kept=tuple(range(len(widths))),
            name="couple",
        )

    def fetch_chips(pair):
        if n_chips > 8:
            return [chip_gather(pair)]
        return send_chips([pair] * n_chips, pair.shape[2] < 2 * units)

    def send_chips(parts, at_once=False):
        if at_once:
            return [parts[0]] + [xor(parts[j], CHIP * j) for j in range(1, n_chips)]
        out = [parts[0]] + [xor(parts[j], CHIP * j) for j in range(1, min(3, n_chips))]
        return out + [xor(gate(parts[j], *out[1:]), CHIP * j) for j in range(3, n_chips)]

    def join(parts):
        if n_chips > 8:
            joined, extra = parts[0][:, :, :shard], parts[0][:, :, shard:]
        else:
            height, width = parts[0].shape[1:]
            out = [sds((n_chips, 2, shard, width), BF16)]
            if height > shard:
                out.append(sds((n_chips, 2, height - shard, width), BF16))
            joined, *extra = place_parts(
                join_moves, out, *parts, scalars=place, name="join", copies=len(out) * n_chips
            )
            extra = extra[0] if extra else None
        return joined.reshape(D, joined.shape[3]), extra

    def give_chips(parts, at_once=False):
        if n_chips > 8:
            return chip_swap(parts[0].reshape(n_chips, -1, parts[0].shape[1]))
        return send_chips(parts, at_once)

    def sum_given(parts, height, *after):
        width = sum(part.shape[1] for part in parts) // n_chips
        out = sds((height, width), BF16)
        return call(
            functools.partial(sum_parts_kernel, n_chips, shard),
            [out, out],
            *parts,
            scalars=place,
            after=after,
            stored=tuple(range(len(parts))),
            kept=(0, 1),
            name="sum_parts",
        )

    def give_near(low):
        return [move(low[0], to_same), move(low[1], from_other)]

    def all_rows(values):
        other = xor(values, PARITY)
        return (values, other, xor(values, CORE), xor(other, CORE))

    def sum_rows(keep, near, send):
        got = xor(send, CORE)
        return keep, got, xor((near + got[rows:].astype(F32)).astype(BF16), PARITY)

    cond_full = condition.astype(F32)
    cond_act = jax.nn.silu(cond_full).astype(BF16)
    (cond_pair,) = call(
        couple_kernel, [sds((2, 1, D), BF16)], cond_act, xor(cond_act, CORE), scalars=place, name="couple"
    )
    cond_every = chip_gather(cond_pair).reshape(n_dp, D)
    qv_bias, out_bias, down_bias, up_bias, up_weight, _ = lax.optimization_barrier(
        (qv_bias, out_bias, down_bias, up_bias, up_weight, cond_every)
    )
    moved = move(jnp.concatenate([tokens[0], cotangent[0]]), swap_core_half)
    qkv_own = jnp.transpose(qkv_weight, (0, 2, 1, 3))
    down_own = jnp.transpose(down_weight, (0, 2, 1))

    bias_len = 12 * piece + up_bias.shape[2]
    bias_vec = jnp.concatenate(
        [
            qv_bias.reshape(layers, 6 * piece),
            out_bias.reshape(layers, 3 * piece),
            down_bias.reshape(layers, 3 * piece),
            up_bias.reshape(layers, -1),
        ],
        axis=1,
    )
    bias_block = lax.dynamic_update_slice(jnp.zeros((16, D), BF16), bias_vec, (0, 0))
    def pack_block(layer):
        return call(
            functools.partial(pack_block_kernel, layer),
            [sds((shard, 4 * cols + 2 * units), BF16)],
            qkv_own,
            out_weight,
            up_weight,
            down_own,
            name="pack_block",
        )[0]

    (own_attention,) = call(
        pack_first_kernel, [sds((shard + 16, 4 * cols), BF16)], qkv_own, out_weight, bias_block, name="pack_first"
    )
    (own_mlp,) = call(pack_mlp_kernel, [sds((shard, 2 * units), BF16)], up_weight, down_own, name="pack_mlp")
    (pair_mlp,) = fetch_near(own_mlp)
    attention_weights = [None] * layers
    mlp_weights = [None] * layers
    (pair_attention,) = fetch_near(own_attention)

    cond_slice = lax.dynamic_slice_in_dim(cond_every, dp * shard, shard, 1)
    bias_at = lax.dynamic_update_slice(
        jnp.zeros((layers, 6, cols // HD, HD), F32), mod_bias.astype(F32), (0, 0, 0, dp * piece)
    ).reshape(layers, 6, cols)
    partial_mod = jnp.einsum("ld,ydkc->lykc", cond_slice, mod_weight, preferred_element_type=F32) + bias_at
    mod_sum = chip_sum(partial_mod.reshape((n_chips, 2) + partial_mod.shape[1:]))
    parts_first = fetch_chips(gate(pair_attention, partial_mod))
    mod_sum = gate(mod_sum, pair_mlp)
    attention_weights[0], bias_every = join(parts_first)
    mod_sum = mod_sum + xor(mod_sum, CORE)
    mod_own = pick(mod_sum, half)
    mod_far = pick(mod_sum, half ^ 1)
    quarters = [xor(mod_far if mask & HALF else mod_own, mask) if mask else mod_own for mask in range(4)]
    (modulation,) = call(
        assemble_kernel,
        [sds((layers, 6, D), F32)],
        *quarters,
        scalars=place,
        after=(pair_mlp,) + tuple(parts_first[1:]),
        name="assemble",
    )

    parts_attention = [None] * layers
    parts_mlp = [None] * layers
    parts_mlp[0] = fetch_chips(gate(pair_mlp, modulation))
    qkv_bias_all, wide_bias, up_bias_all = call(
        bias_kernel,
        [sds((layers, 1, 3 * cols), F32), sds((layers, 2, D), F32), sds((layers, 1, units), F32)],
        bias_every.reshape(n_dp * 16, D),
        scalars=place,
        name="bias",
    )
    cotan, d_mlp = call(
        turn_kernel, [sds((rows, D), F32), sds((rows, D), BF16)], moved, modulation[layers - 1], kept=(0,), name="turn"
    )
    d_mlp_rows = all_rows(d_mlp)

    full = 4 * rows
    keep_send = [sds((rows, D), F32), sds((rows, D), F32), sds((full // 2, D), BF16)]
    row_f32 = sds((rows, D), F32)
    row_bf16 = sds((rows, D), BF16)
    line = sds((1, D), F32)
    attention_flops = 2 * full * D * 4 * cols + 4 * full * full * cols
    mlp_flops = 4 * full * D * units

    def parts_of(width, extra=0):
        if n_chips > 8:
            return [sds((D, width), BF16)]
        return [sds((D // n_chips + extra, width), BF16)] * n_chips

    saved = []
    residual, far_residual, attn_in = call(
        enter_kernel,
        [row_f32, row_f32, row_bf16],
        moved,
        modulation[0],
        kept=(1,),
        after=(attention_weights[0],),
        name="enter",
    )
    for layer in range(layers):
        mod = modulation[layer]
        more = layer + 1 < layers
        attn_rows = all_rows(attn_in)
        if more:
            own_block = gate(pack_block(layer + 1), attn_rows[3])
            pair_attention, pair_mlp = fetch_near(own_block, 4 * cols, 2 * units)
            parts_attention[layer + 1] = fetch_chips(gate(pair_attention, parts_mlp[layer][-1]))
            parts_mlp[layer + 1] = fetch_chips(gate(pair_mlp, parts_attention[layer + 1][-1]))
        if layer:
            attention_weights[layer] = join(parts_attention[layer])[0]
        attn_x, qkv, att, *partial = call(
            attention_kernel,
            [sds((full, D), BF16), sds((full, 3 * cols), BF16), sds((full, cols), BF16)] + keep_send,
            *attn_rows,
            attention_weights[layer],
            qkv_bias_all[layer],
            wide_bias[layer, :1],
            flops=attention_flops,
            stored=(4,),
            kept=(0, 1, 2),
            name="attention",
        )
        partial[2] = gate(partial[2], *parts_mlp[layer][1:3])
        branch, far_middle, middle, mlp_in = call(
            middle_kernel,
            [row_f32, row_f32, row_f32, row_bf16],
            residual,
            mod,
            *sum_rows(*partial),
            kept=(0, 1),
            name="middle",
        )
        mlp_rows = all_rows(mlp_in)
        mlp_weights[layer] = join(parts_mlp[layer])[0]
        mlp_x, hidden, act, *partial = call(
            mlp_kernel,
            [sds((full, D), BF16), sds((full, units), F32), sds((full, units), BF16)] + keep_send,
            *mlp_rows,
            mlp_weights[layer],
            up_bias_all[layer],
            wide_bias[layer, 1:],
            flops=mlp_flops,
            stored=(4,),
            kept=(0, 1, 2),
            name="mlp",
        )
        if more:
            partial[2] = gate(partial[2], *parts_attention[layer + 1][1:3])
        arrived = sum_rows(*partial)
        saved.append((far_residual, attn_x, qkv, att, branch, far_middle, mlp_x, hidden, act))
        if more:
            arrived = (gate(arrived[0], parts_attention[layer + 1][-1]),) + arrived[1:]
            mlp_out, far_residual, residual, attn_in = call(
                next_kernel,
                [row_f32, row_f32, row_f32, row_bf16],
                middle,
                mod,
                *arrived,
                modulation[layer + 1],
                kept=(0, 1),
                name="next",
            )
            saved[-1] += (mlp_out,)
        else:
            output, d_gate_two = call(
                last_kernel, [row_bf16, line], middle, mod, *arrived, cotan, stored=(5,), name="last"
            )

    output = move(output, swap_core_half)
    flow = cotan
    mod_lines = [None] * layers
    vecs = [None] * layers
    low = [None] * layers
    near_packs = [None] * layers
    given_attention = [None] * layers
    given_mlp = [None] * layers
    vec_shape = sds((n_dp, bias_len), F32)
    for layer in reversed(range(layers)):
        far_residual, attn_x, qkv, att, branch, far_middle, mlp_x, hidden, act = saved[layer][:9]
        mod = modulation[layer]
        more = layer + 1 < layers
        if more:
            d_mlp_rows = all_rows(d_mlp)
        mlp_y, d_hidden, *partial = call(
            mlp_back_kernel,
            [sds((full, D), BF16), sds((full, units), BF16)] + keep_send,
            *d_mlp_rows,
            mlp_weights[layer],
            hidden,
            flops=mlp_flops,
            stored=(4, 5),
            kept=(0, 1),
            name="mlp_back",
        )
        if more:
            partial[2] = gate(partial[2], *given_mlp[layer + 1][1:3])
        arrived = sum_rows(*partial)
        *grad_mlp, vec_mlp = call(
            mlp_grad_kernel,
            parts_of(2 * units) + [vec_shape],
            mlp_y,
            mlp_x,
            d_hidden,
            act,
            flops=mlp_flops,
            scalars=place,
            scratch=[pltpu.VMEM((D, 2 * units), BF16)],
            stored=(0, 1, 2, 3),
            kept=(0,),
            name="mlp_grad",
        )
        arrived = (gate(arrived[0], grad_mlp[0], *(given_mlp[layer + 1][3:] if more else ())),) + arrived[1:]
        if more:
            grad_mlp = [gate(part, *given_attention[layer + 1][1:]) for part in grad_mlp]
        given_mlp[layer] = give_chips(grad_mlp)
        d_middle, d_branch, sums_mid = call(
            middle_back_kernel,
            [row_f32, row_bf16, sds((3, D), F32)],
            flow,
            mod,
            *arrived,
            far_middle,
            branch,
            stored=(5, 6) if more else (0, 5, 6),
            name="middle_back",
        )
        if more:
            d_branch = gate(d_branch, *given_attention[layer + 1][1:])
            low[layer + 1] = sum_given(list(given_attention[layer + 1]) + list(given_mlp[layer + 1]), shard)
            near_packs[layer + 1] = give_near(low[layer + 1])
        d_branch_rows = all_rows(d_branch)
        attn_y, d_qkv, *partial = call(
            attention_back_kernel,
            [sds((full, D), BF16), sds((full, 3 * cols), BF16)] + keep_send,
            *d_branch_rows,
            attention_weights[layer],
            qkv,
            flops=attention_flops * 2,
            stored=(4, 5),
            kept=(0, 1),
            name="attention_back",
        )
        if more:
            partial[2] = gate(partial[2], *given_mlp[layer][1:3], near_packs[layer + 1][0])
        arrived = sum_rows(*partial)
        *grad_attention, vecs[layer] = call(
            functools.partial(
                attention_grad_kernel if layer or n_chips > 8 else attention_grad_last_kernel,
                1 if n_chips > 8 else n_chips,
            ),
            parts_of(4 * cols, 0 if layer else 16) + [vec_shape],
            attn_y,
            attn_x,
            d_qkv,
            att,
            vec_mlp,
            *(() if layer or n_chips > 8 else (vecs[1],)),
            flops=attention_flops,
            scalars=place,
            scratch=[pltpu.VMEM((D, 4 * cols), BF16)],
            stored=(0, 1, 2, 3),
            kept=(0,),
            name="attention_grad",
        )
        after = (grad_attention[0],)
        if layer == 0:
            after = after + (output,) + tuple(given_mlp[0][3:]) + tuple(near_packs[upper][1] for upper in range(1, layers))
        if layer == 0:
            height = 2 * shard + 16
            if n_chips > 8:
                rows_bias = jnp.concatenate([vecs[i] for i in range(layers)], axis=1).astype(BF16)
                rows_bias = jnp.pad(
                    rows_bias.reshape(n_chips, 2, -1), ((0, 0), (0, 14), (0, 4 * cols - layers * bias_len))
                )
                rows_all = jnp.concatenate(
                    [grad_attention[0].reshape(n_chips, 2 * shard, 4 * cols), rows_bias], axis=1
                )
                grad_attention = [rows_all.reshape(n_chips * height, 4 * cols)]
        given_attention[layer] = give_chips([gate(part, *given_mlp[layer][1:]) for part in grad_attention], True)
        if layer:
            flow, sums_in, d_mlp, gate_next = call(
                previous_kernel,
                [row_f32, sds((2, D), F32), row_bf16, line],
                d_middle,
                mod,
                *arrived,
                far_residual,
                modulation[layer - 1],
                saved[layer - 1][9],
                stored=(5, 7),
                after=after,
                name="previous",
            )
        else:
            flow, sums_in = call(
                enter_back_kernel,
                [row_f32, sds((2, D), F32)],
                d_middle,
                mod,
                *arrived,
                far_residual,
                stored=(5,),
                after=after,
                name="enter_back",
            )
            gate_next = None
        mod_lines[layer] = jnp.concatenate([sums_in, sums_mid, d_gate_two], axis=0)
        d_gate_two = gate_next

    d_mod = jnp.stack(mod_lines)
    d_mod = d_mod + xor(d_mod, CORE)
    d_mod = (d_mod + xor(d_mod, PARITY)).astype(BF16).reshape(layers * 6, 4, cols)
    d_mod = jnp.transpose(d_mod, (1, 0, 2))
    mine = pick(d_mod, z)
    far = xor(pick(d_mod, z ^ HALF), HALF)
    d_mod_pair = jnp.where(half == 0, jnp.stack([mine, far]), jnp.stack([far, mine]))
    low_attention = sum_given(list(given_attention[0]), shard + 16)
    near_attention = give_near(low_attention)
    near_mlp = give_near(sum_given(list(given_mlp[0]), shard))
    near_packs[0] = near_attention + near_mlp
    d_mod_pair = gate(d_mod_pair, *given_attention[0][1:])
    d_mod_every = gate(chip_gather(d_mod_pair), *near_mlp).reshape(n_dp, layers, 6, cols)
    grad_mod_w = jnp.einsum("ld,lykc->ykdc", cond_slice, d_mod_every, preferred_element_type=F32)
    grad_mod_w = jnp.transpose(grad_mod_w, (0, 2, 1, 3))
    grad_mod_b = jnp.sum(d_mod_every.astype(F32), axis=0).reshape(layers, 6, cols // HD, HD)
    grad_mod_b = lax.dynamic_slice_in_dim(grad_mod_b, dp * piece, piece, 3)
    cond_pieces = jnp.einsum("lykc,ydkc->ld", d_mod_every, mod_weight, preferred_element_type=F32)
    mixed = jnp.stack(chip_swap(cond_pieces.reshape(n_chips, 2, shard)))
    if n_chips <= 8:
        mixed = jnp.take(mixed, chip ^ jnp.arange(n_chips), axis=0)
    cond_pieces = jnp.transpose(mixed, (1, 0, 2))
    cond_pieces = gate(cond_pieces, *low_attention)
    cond_mine = pick(cond_pieces, core)
    cond_sent = xor(pick(cond_pieces, core ^ 1), CORE)
    cond_total = jnp.where(
        core == 0, jnp.stack([cond_mine, cond_sent], axis=1), jnp.stack([cond_sent, cond_mine], axis=1)
    ).reshape(1, D)
    cond_total = gate(cond_total, *near_attention)
    cond_total = cond_total + xor(cond_total, PARITY)
    cond_total = cond_total + xor(cond_total, HALF)
    sigmoid_cond = jax.nn.sigmoid(cond_full)
    grad_condition = cond_total * sigmoid_cond * (1.0 + cond_full * (1.0 - sigmoid_cond))

    grad_tokens = move(gate(flow, cond_mine), swap_core_half)
    output, grad_tokens, grad_qkv, grad_out, grad_up, grad_down, vec = call(
        finish_kernel,
        [
            row_bf16,
            row_f32,
            sds((layers, 3, shard, cols), F32),
            sds((layers, cols, shard), F32),
            sds((layers, shard, units), F32),
            sds((layers, shard, units), F32),
            sds((8, 4 * cols), F32),
        ],
        output,
        grad_tokens,
        *[part for layer in range(layers) for part in near_packs[layer]],
        kept=(0, 1, 2, 3, 4, 5),
        name="finish",
    )
    vec = vec[0, : layers * bias_len].reshape(layers, bias_len)
    vec_heads = vec[:, : 12 * piece].reshape(layers, 4, 3, piece)
    return (
        output[None],
        grad_tokens[None],
        grad_condition,
        grad_mod_w,
        grad_mod_b,
        jnp.transpose(grad_qkv, (0, 2, 1, 3)),
        vec_heads[:, :2],
        grad_out,
        vec_heads[:, 2],
        grad_up,
        vec[:, 12 * piece :].reshape(layers, 1, -1),
        jnp.transpose(grad_down, (0, 2, 1)),
        vec_heads[:, 3],
    )


def solution(mesh):
    in_specs = (
        P("dp", "tensor", None),
        P("dp", None),
        P("dp", "tensor", None),
        P(None, "dp", None, "tensor"),
        P(None, None, "tensor", "dp"),
        P(None, "dp", None, "tensor"),
        P(None, None, "tensor", "dp"),
        P(None, "tensor", "dp"),
        P(None, "tensor", "dp"),
        P(None, "dp", "tensor"),
        P(None, "tensor", "dp"),
        P(None, "tensor", "dp"),
        P(None, "tensor", "dp"),
    )
    out_specs = (
        P("dp", "tensor", None),
        P("dp", "tensor", None),
        P("dp", None),
        P(None, "dp", None, "tensor"),
        P(None, None, "tensor", "dp"),
        P(None, "dp", None, "tensor"),
        P(None, None, "tensor", "dp"),
        P(None, "tensor", "dp"),
        P(None, "tensor", "dp"),
        P(None, "dp", "tensor"),
        P(None, "tensor", "dp"),
        P(None, "tensor", "dp"),
        P(None, "tensor", "dp"),
    )
    return jax.shard_map(body, mesh=mesh, in_specs=in_specs, out_specs=out_specs, check_vma=False)
```

```python
import functools
import math

import jax
import jax.numpy as jnp
from jax import lax
from jax.experimental import pallas as pl
from jax.experimental.pallas import tpu as pltpu
from jax.sharding import PartitionSpec as P

D = 768
HD = 64
EPS = 1e-06
AXES = ("dp", "tensor")
F32 = jnp.float32
BF16 = jnp.bfloat16
VMEM_LIMIT = 16 * 1024 * 1024

PARITY = 1
HALF = 2
CORE = 4
CHIP = 8


class Stored:
    def __init__(self, source, target, sem, local):
        self.copy = pltpu.make_async_copy(source, target, sem)
        self.local = local
        self.shape = local.shape
        self.busy = False
        self.dirty = False

    def start(self):
        self.copy.start()
        self.busy = True
        self.dirty = False

    def settle(self):
        if self.busy:
            self.copy.wait()
            self.busy = False

    def __getitem__(self, index):
        self.settle()
        return self.local[index]

    def __setitem__(self, index, value):
        self.local[index] = value
        self.dirty = True
        if index is Ellipsis:
            self.start()


def call(
    kernel, out_shape, *args, flops=0, name=None, scalars=None, after=(), scratch=(), stored=(), kept=(), window=()
):
    size = sum(a.size * a.dtype.itemsize for a in args) + sum(math.prod(o.shape) * o.dtype.itemsize for o in out_shape)
    hbm = pl.BlockSpec(memory_space=pltpu.HBM)
    vmem = pl.BlockSpec(memory_space=pltpu.VMEM)
    in_specs = [hbm if i in stored else vmem for i in range(len(args))]
    out_specs = [hbm if i in kept else vmem for i in range(len(out_shape))]
    window = dict(window)
    copies = [pltpu.VMEM((args[i].shape[0], window[i][1]) if i in window else args[i].shape, args[i].dtype) for i in stored]
    copies += [pltpu.VMEM(out_shape[i].shape, out_shape[i].dtype) for i in kept]
    lead = 0
    if after:
        args = (gate(args[0], *after),) + args[1:]
    if scalars is not None:
        args = (scalars,) + args
        in_specs = [pl.BlockSpec(memory_space=pltpu.SMEM)] + in_specs
        lead = 1

    def run(*refs):
        ins = list(refs[: len(args)])
        outs = list(refs[len(args) : len(args) + len(out_shape)])
        rest = refs[len(args) + len(out_shape) :]
        own, local = rest[: len(scratch)], rest[len(scratch) :]
        held = []
        for n, i in enumerate(stored):
            source = ins[lead + i].at[:, pl.ds(*window[i])] if i in window else ins[lead + i]
            held.append(Stored(source, local[n], local[-1].at[n], local[n]))
            held[-1].start()
            ins[lead + i] = held[-1]
        for n, i in enumerate(kept, len(stored)):
            held.append(Stored(local[n], outs[i], local[-1].at[n], local[n]))
            outs[i] = held[-1]
        kernel(*ins, *outs, *own)
        for item in held:
            if item.dirty:
                item.start()
        for item in held:
            item.settle()

    return pl.pallas_call(
        run,
        out_shape=out_shape,
        in_specs=in_specs,
        out_specs=out_specs,
        scratch_shapes=list(scratch) + copies + ([pltpu.SemaphoreType.DMA((len(copies),))] if copies else []),
        compiler_params=pltpu.CompilerParams(vmem_limit_bytes=VMEM_LIMIT),
        cost_estimate=pl.CostEstimate(flops=flops, bytes_accessed=size, transcendentals=0),
        name=name,
    )(*args)


def gate(value, *others):
    return lax.optimization_barrier((value,) + others)[0]


def place_parts(kernel, out_shape, *args, scalars, name, copies):
    count = len(args)

    def run(place_ref, *refs):
        outs = refs[count : count + len(out_shape)]
        sems = refs[-1]
        moves = [
            pltpu.make_async_copy(source, target, sems.at[n])
            for n, (source, target) in enumerate(kernel(place_ref, refs[:count], outs))
        ]
        for item in moves:
            item.start()
        for item in moves:
            item.wait()

    size = sum(a.size * a.dtype.itemsize for a in args)
    return pl.pallas_call(
        run,
        out_shape=out_shape,
        in_specs=[pl.BlockSpec(memory_space=pltpu.SMEM)]
        + [pl.BlockSpec(memory_space=pltpu.HBM)] * count,
        out_specs=[pl.BlockSpec(memory_space=pltpu.HBM)] * len(out_shape),
        scratch_shapes=[pltpu.SemaphoreType.DMA((copies,))],
        compiler_params=pltpu.CompilerParams(vmem_limit_bytes=VMEM_LIMIT),
        cost_estimate=pl.CostEstimate(flops=0, bytes_accessed=2 * size, transcendentals=0),
        name=name,
    )(scalars, *args)


def sds(shape, dtype):
    return jax.ShapeDtypeStruct(shape, dtype)


def dot(a, b, ca=1, cb=0):
    return lax.dot_general(a, b, (((ca,), (cb,)), ((), ())), preferred_element_type=F32)


def normalize(values):
    centered = values - jnp.mean(values, axis=-1, keepdims=True)
    inverse = lax.rsqrt(jnp.mean(centered * centered, axis=-1, keepdims=True) + EPS)
    return centered * inverse, inverse


def norm_back(incoming, normed, inverse):
    average = jnp.mean(incoming, axis=-1, keepdims=True)
    along = jnp.mean(incoming * normed, axis=-1, keepdims=True)
    return inverse * (incoming - average - normed * along)


def col_sum(values):
    return jnp.sum(values, axis=0, keepdims=True)


def modulate(values, mod, shift, scale):
    normed, _ = normalize(values)
    return (normed * (1.0 + mod[scale : scale + 1]) + mod[shift : shift + 1]).astype(BF16)


def rows_of(refs):
    return jnp.concatenate([ref[...] for ref in refs], axis=0)


def split_out(total, keep_ref, near_ref, send_ref):
    quarter = total.shape[0] // 4
    keep_ref[...] = total[:quarter]
    near_ref[...] = total[quarter : 2 * quarter]
    send_ref[...] = total[2 * quarter :].astype(BF16)


def summed(keep_ref, core_ref, far_ref):
    return keep_ref[...] + core_ref[: keep_ref.shape[0]].astype(F32) + far_ref[...].astype(F32)


def attention_pack(layer, qkv_ref, out_ref):
    out = out_ref[layer].astype(F32).T.astype(BF16)
    return jnp.concatenate([qkv_ref[layer, 0], qkv_ref[layer, 1], qkv_ref[layer, 2], out], axis=1)


def pack_block_kernel(layer, qkv_ref, out_ref, up_ref, down_ref, pack_ref):
    wide = 4 * out_ref.shape[1]
    units = up_ref.shape[2]
    pack_ref[:, :wide] = attention_pack(layer, qkv_ref, out_ref)
    pack_ref[:, wide : wide + units] = up_ref[layer]
    pack_ref[:, wide + units :] = down_ref[layer]


def pack_first_kernel(qkv_ref, out_ref, bias_ref, pack_ref):
    shard = out_ref.shape[2]
    pack_ref[:shard] = attention_pack(0, qkv_ref, out_ref)
    pack_ref[shard:] = bias_ref[...]


def pack_mlp_kernel(up_ref, down_ref, pack_ref):
    units = up_ref.shape[2]
    pack_ref[:, :units] = up_ref[0]
    pack_ref[:, units:] = down_ref[0]


def join_moves(place_ref, ins, outs):
    shard = outs[0].shape[2]
    moves = []
    for j, part in enumerate(ins):
        at = place_ref[0] ^ j
        moves.append((part.at[:, :shard], outs[0].at[at]))
        if len(outs) == 2:
            moves.append((part.at[:, shard:], outs[1].at[at]))
    return moves


def assemble_kernel(place_ref, *refs):
    parts, out_ref = refs[:-1], refs[-1]
    cols = parts[0].shape[2]
    for layer in range(out_ref.shape[0]):
        for at in range(4):
            quarter = sum(
                jnp.where(place_ref[3] ^ mask == at, part[layer], 0.0) for mask, part in enumerate(parts)
            )
            out_ref[layer, :, at * cols : (at + 1) * cols] = quarter


def spread_kernel(place_ref, *refs):
    parts, out_ref = refs[:-1], refs[-1]
    for j, part in enumerate(parts):
        out_ref[place_ref[0] ^ j] = part[...]


def couple_kernel(place_ref, own_ref, other_ref, *out_refs):
    first = place_ref[1] == 0
    at = 0
    for out_ref in out_refs:
        end = at + out_ref.shape[-1]
        own, other = own_ref[..., at:end], other_ref[..., at:end]
        out_ref[0] = jnp.where(first, own, other)
        out_ref[1] = jnp.where(first, other, own)
        at = end


def head_select(n_dp, piece, cols):
    row = lax.broadcasted_iota(jnp.int32, (3 * piece, cols), 0)
    col = lax.broadcasted_iota(jnp.int32, (3 * piece, cols), 1)
    return (row == col // HD * piece + col % piece).astype(F32)


def head_mask(n_dp, piece, cols):
    row = lax.broadcasted_iota(jnp.int32, (n_dp, cols), 0)
    col = lax.broadcasted_iota(jnp.int32, (n_dp, cols), 1)
    return (col % HD // piece == row).astype(F32)


def exact(a, b):
    return lax.dot_general(
        a, b, (((1,), (0,)), ((), ())), preferred_element_type=F32, precision=lax.Precision.HIGHEST
    )


def heads_back(line, at, n_dp, length):
    cols, piece = line.shape[1], HD // n_dp
    row = lax.broadcasted_iota(jnp.int32, (length, cols), 0) - at
    col = lax.broadcasted_iota(jnp.int32, (length, cols), 1)
    select = (row == col // HD * piece + col % piece).astype(F32)
    return lax.dot_general(
        head_mask(n_dp, piece, cols) * line,
        select,
        (((1,), (1,)), ((), ())),
        preferred_element_type=F32,
        precision=lax.Precision.HIGHEST,
    )


def units_back(line, at, n_dp, length):
    units = line.shape[1]
    width = units // n_dp
    row = lax.broadcasted_iota(jnp.int32, (length, units), 0) - at
    col = lax.broadcasted_iota(jnp.int32, (length, units), 1)
    mask = (
        lax.broadcasted_iota(jnp.int32, (n_dp, units), 1) // width
        == lax.broadcasted_iota(jnp.int32, (n_dp, units), 0)
    )
    return lax.dot_general(
        mask.astype(F32) * line,
        (col % width == row).astype(F32),
        (((1,), (1,)), ((), ())),
        preferred_element_type=F32,
        precision=lax.Precision.HIGHEST,
    )


def own_quarter(line, cols, place_ref):
    return sum(
        jnp.where(place_ref[2] == i, line[:, i * cols : (i + 1) * cols], 0.0) for i in range(line.shape[1] // cols)
    )


def bias_kernel(place_ref, vec_ref, qkv_ref, wide_ref, up_ref):
    n_dp, piece = vec_ref.shape[0] // 16, HD * 16 // vec_ref.shape[0]
    vec_row = lax.broadcasted_iota(jnp.int32, (n_dp, vec_ref.shape[0]), 0)
    vec_col = lax.broadcasted_iota(jnp.int32, (n_dp, vec_ref.shape[0]), 1)
    cols, units = qkv_ref.shape[2] // 3, up_ref.shape[2]
    select, mask = head_select(n_dp, piece, cols), head_mask(n_dp, piece, cols)
    width = units // n_dp
    row = lax.broadcasted_iota(jnp.int32, (width, units), 0)
    col = lax.broadcasted_iota(jnp.int32, (width, units), 1)
    up_select = (col % width == row).astype(F32)
    up_row = lax.broadcasted_iota(jnp.int32, (n_dp, units), 0)
    up_col = lax.broadcasted_iota(jnp.int32, (n_dp, units), 1)
    up_mask = (up_col // width == up_row).astype(F32)
    quarters = wide_ref.shape[2] // cols
    place = lax.broadcasted_iota(jnp.int32, (1, quarters * cols), 1) // cols == place_ref[2]
    for layer in range(qkv_ref.shape[0]):
        vec = dot((vec_col == 16 * vec_row + layer).astype(BF16), vec_ref[...])
        heads = [col_sum(exact(vec[:, 3 * t * piece : 3 * (t + 1) * piece], select) * mask) for t in range(4)]
        qkv_ref[layer] = jnp.concatenate([heads[0], jnp.zeros_like(heads[0]), heads[1]], axis=1)
        for t in range(2):
            wide_ref[layer, t : t + 1] = jnp.where(place, jnp.concatenate([heads[2 + t]] * quarters, axis=1), 0.0)
        up_ref[layer] = col_sum(exact(vec[:, 12 * piece : 12 * piece + width], up_select) * up_mask)


def sum_parts_kernel(count, shard, place_ref, *refs):
    parts, (same_ref, other_ref) = refs[:-2], refs[-2:]
    first = place_ref[1] == 0
    at = 0
    for start in range(0, len(parts), count):
        low = sum(part[...].astype(F32) for part in parts[start : start + count])
        end = at + low.shape[1]
        mine, far = low[:shard], low[shard : 2 * shard]
        same_ref[:shard, at:end] = jnp.where(first, mine, far).astype(BF16)
        other_ref[:shard, at:end] = jnp.where(first, far, mine).astype(BF16)
        if low.shape[0] > 2 * shard:
            mine, far = low[2 * shard : 2 * shard + 1], low[2 * shard + 1 : 2 * shard + 2]
            same_ref[shard:, at:end] = jnp.broadcast_to(jnp.where(first, mine, far), (16, end - at)).astype(BF16)
            other_ref[shard:, at:end] = jnp.broadcast_to(jnp.where(first, far, mine), (16, end - at)).astype(BF16)
        at = end


def finish_kernel(last_ref, flow_ref, *refs):
    parts, (last_out_ref, flow_out_ref, qkv_ref, out_ref, up_ref, down_ref, vec_ref) = refs[:-7], refs[-7:]
    last_out_ref[...] = last_ref[...]
    flow_out_ref[...] = flow_ref[...]
    shard, cols, units = up_ref.shape[1], out_ref.shape[1], up_ref.shape[2]
    for layer in range(qkv_ref.shape[0]):
        if layer == 0:
            total = parts[0][...].astype(F32) + parts[1][...].astype(F32)
            vec_ref[...] = total[shard : shard + 8]
            mlp = parts[2][...].astype(F32) + parts[3][...].astype(F32)
        else:
            total = parts[2 * layer + 2][...].astype(F32) + parts[2 * layer + 3][...].astype(F32)
            mlp = total[:, 4 * cols :]
        for i in range(3):
            qkv_ref[layer, i] = total[:shard, i * cols : (i + 1) * cols]
        out_ref[layer] = total[:shard, 3 * cols : 4 * cols].T
        up_ref[layer] = mlp[:, :units]
        down_ref[layer] = mlp[:, units:]


def enter_kernel(moved_ref, mod_ref, res_ref, far_res_ref, in_ref):
    residual = moved_ref[: res_ref.shape[0]].astype(F32)
    far_res_ref[...] = residual
    res_ref[...] = residual
    in_ref[...] = modulate(residual, mod_ref[...], 0, 1)


def attention_kernel(x0, x1, x2, x3, w_ref, bias_ref, bo_ref, x_ref, qkv_ref, att_ref, keep_ref, near_ref, send_ref):
    x = rows_of((x0, x1, x2, x3))
    x_ref[...] = x
    cols = w_ref.shape[1] // 4
    qkv = (dot(x, w_ref[:, : 3 * cols]) + bias_ref[...]).astype(BF16)
    qkv_ref[...] = qkv
    parts = []
    for head in range(cols // HD):
        at = head * HD
        q = qkv[:, at : at + HD]
        k = qkv[:, cols + at : cols + at + HD]
        v = qkv[:, 2 * cols + at : 2 * cols + at + HD]
        scores = dot(q, k, 1, 1) * (1.0 / math.sqrt(HD))
        expo = jnp.exp(scores - jnp.max(scores, axis=-1, keepdims=True))
        probs = expo / jnp.sum(expo, axis=-1, keepdims=True)
        parts.append(dot(probs.astype(BF16), v))
    att = jnp.concatenate(parts, axis=1).astype(BF16)
    att_ref[...] = att
    split_out(dot(att, w_ref[:, 3 * cols :], 1, 1) + bo_ref[...], keep_ref, near_ref, send_ref)


def middle_kernel(res_ref, mod_ref, keep_ref, core_ref, far_ref, branch_ref, far_mid_ref, mid_ref, in_ref):
    mod = mod_ref[...]
    branch = summed(keep_ref, core_ref, far_ref)
    branch_ref[...] = branch
    middle = res_ref[...] + mod[2:3] * branch
    far_mid_ref[...] = middle
    mid_ref[...] = middle
    in_ref[...] = modulate(middle, mod, 3, 4)


def mlp_kernel(x0, x1, x2, x3, w_ref, bu_ref, bd_ref, x_ref, hid_ref, act_ref, keep_ref, near_ref, send_ref):
    x = rows_of((x0, x1, x2, x3))
    x_ref[...] = x
    units = w_ref.shape[1] // 2
    hidden = dot(x, w_ref[:, :units]) + bu_ref[...]
    hid_ref[...] = hidden
    act = (0.5 * hidden * (1.0 + lax.erf(hidden * 0.7071067811865476))).astype(BF16)
    act_ref[...] = act
    split_out(dot(act, w_ref[:, units:], 1, 1) + bd_ref[...], keep_ref, near_ref, send_ref)


def next_kernel(
    mid_ref, mod_ref, keep_ref, core_ref, far_ref, mod_next_ref, out_ref, far_res_ref, res_ref, in_ref
):
    mlp_out = summed(keep_ref, core_ref, far_ref)
    out_ref[...] = mlp_out
    residual = mid_ref[...] + mod_ref[5:6] * mlp_out
    far_res_ref[...] = residual
    res_ref[...] = residual
    in_ref[...] = modulate(residual, mod_next_ref[...], 0, 1)


def last_kernel(mid_ref, mod_ref, keep_ref, core_ref, far_ref, g_ref, out_ref, dgate_ref):
    mlp_out = summed(keep_ref, core_ref, far_ref)
    out_ref[...] = (mid_ref[...] + mod_ref[5:6] * mlp_out).astype(BF16)
    dgate_ref[...] = col_sum(g_ref[...] * mlp_out)


def turn_kernel(moved_ref, mod_ref, g_ref, dmlp_ref):
    g = moved_ref[dmlp_ref.shape[0] :].astype(F32)
    g_ref[...] = g
    dmlp_ref[...] = (g * mod_ref[5:6]).astype(BF16)


def mlp_back_kernel(x0, x1, x2, x3, w_ref, hid_ref, x_ref, dhid_ref, keep_ref, near_ref, send_ref):
    x = rows_of((x0, x1, x2, x3))
    x_ref[...] = x
    units = w_ref.shape[1] // 2
    hidden = hid_ref[...]
    d_active = dot(x, w_ref[:, units:])
    cumulative = 0.5 * (1.0 + lax.erf(hidden * 0.7071067811865476))
    density = jnp.exp(-0.5 * hidden * hidden) * 0.3989422804014327
    d_hidden = (d_active * (cumulative + hidden * density)).astype(BF16)
    dhid_ref[...] = d_hidden
    split_out(dot(d_hidden, w_ref[:, :units], 1, 1), keep_ref, near_ref, send_ref)


def give_parts(grad, place_ref, scratch_ref, part_refs):
    if len(part_refs) == 1:
        part_refs[0][...] = grad.astype(BF16)
        return
    scratch_ref[...] = grad.astype(BF16)
    rows = part_refs[0].shape[0]
    for j, part in enumerate(part_refs):
        start = pl.multiple_of((place_ref[0] ^ j) * rows, rows)
        part[...] = scratch_ref[pl.ds(start, rows), :]


def mlp_grad_kernel(place_ref, y_ref, x_ref, dhid_ref, act_ref, *refs):
    part_refs, (vec_ref, scratch_ref) = refs[:-2], refs[-2:]
    y = y_ref[...]
    d_hidden = dhid_ref[...]
    grad = jnp.concatenate([dot(x_ref[...], d_hidden, 0, 0), dot(y, act_ref[...], 0, 0)], axis=1)
    give_parts(grad, place_ref, scratch_ref, part_refs)
    n_dp, length = vec_ref.shape
    piece = HD // n_dp
    cols = y.shape[1] // 4
    down = own_quarter(col_sum(y.astype(F32)), cols, place_ref)
    up = col_sum(d_hidden.astype(F32))
    vec_ref[...] = heads_back(down, 9 * piece, n_dp, length) + units_back(up, 12 * piece, n_dp, length)


def middle_back_kernel(g_ref, mod_ref, keep_ref, core_ref, far_ref, mid_ref, branch_ref, dmid_ref, dbranch_ref, sums_ref):
    mod = mod_ref[...]
    incoming = summed(keep_ref, core_ref, far_ref)
    normed, inverse = normalize(mid_ref[...])
    d_middle = g_ref[...] + norm_back(incoming * (1.0 + mod[4:5]), normed, inverse)
    dmid_ref[...] = d_middle
    dbranch_ref[...] = (d_middle * mod[2:3]).astype(BF16)
    sums_ref[...] = jnp.concatenate(
        [col_sum(d_middle * branch_ref[...]), col_sum(incoming), col_sum(incoming * normed)], axis=0
    )


def attention_back_kernel(x0, x1, x2, x3, w_ref, qkv_ref, x_ref, dqkv_ref, keep_ref, near_ref, send_ref):
    x = rows_of((x0, x1, x2, x3))
    x_ref[...] = x
    cols = w_ref.shape[1] // 4
    qkv = qkv_ref[...]
    scaling = 1.0 / math.sqrt(HD)
    d_att = dot(x, w_ref[:, 3 * cols :]).astype(BF16)
    grads = ([], [], [])
    for head in range(cols // HD):
        at = head * HD
        q = qkv[:, at : at + HD]
        k = qkv[:, cols + at : cols + at + HD]
        v = qkv[:, 2 * cols + at : 2 * cols + at + HD]
        d_out = d_att[:, at : at + HD]
        scores = dot(q, k, 1, 1) * scaling
        expo = jnp.exp(scores - jnp.max(scores, axis=-1, keepdims=True))
        probs = expo / jnp.sum(expo, axis=-1, keepdims=True)
        d_probs = dot(d_out, v, 1, 1)
        d_scores = (probs * (d_probs - jnp.sum(probs * d_probs, axis=-1, keepdims=True))).astype(BF16)
        grads[0].append(dot(d_scores, k) * scaling)
        grads[1].append(dot(d_scores, q, 0, 0) * scaling)
        grads[2].append(dot(probs.astype(BF16), d_out, 0, 0))
    d_qkv = jnp.concatenate(grads[0] + grads[1] + grads[2], axis=1).astype(BF16)
    dqkv_ref[...] = d_qkv
    split_out(dot(d_qkv, w_ref[:, : 3 * cols], 1, 1), keep_ref, near_ref, send_ref)


def attention_grad_kernel(n_parts, place_ref, y_ref, x_ref, dqkv_ref, att_ref, vecs_ref, *refs):
    part_refs, (vec_ref, scratch_ref) = refs[:-2], refs[-2:]
    y = y_ref[...]
    d_qkv = dqkv_ref[...]
    cols = d_qkv.shape[1] // 3
    wide = 4 * cols
    grad = jnp.concatenate([dot(x_ref[...], d_qkv, 0, 0), dot(y, att_ref[...], 0, 0)], axis=1)
    scratch_ref[...] = grad.astype(BF16)
    n_dp, length = vec_ref.shape
    piece = HD // n_dp
    total = col_sum(d_qkv.astype(F32))
    out = own_quarter(col_sum(y.astype(F32)), cols, place_ref)
    vec = vecs_ref[...] + (
        heads_back(total[:, :cols], 0, n_dp, length)
        + heads_back(total[:, 2 * cols :], 3 * piece, n_dp, length)
        + heads_back(out, 6 * piece, n_dp, length)
    )
    vec_ref[...] = vec
    if n_parts == 1:
        part_refs[0][...] = scratch_ref[...]
        return
    rows = scratch_ref.shape[0] // n_parts
    for j, part in enumerate(part_refs):
        at = place_ref[0] ^ j
        part[:rows] = scratch_ref[pl.ds(pl.multiple_of(at * rows, rows), rows), :]


def attention_grad_last_kernel(n_parts, place_ref, y_ref, x_ref, dqkv_ref, att_ref, vecs_ref, high_ref, *refs):
    part_refs, (vec_ref, scratch_ref) = refs[:-2], refs[-2:]
    rows = scratch_ref.shape[0] // n_parts
    attention_grad_kernel(
        n_parts, place_ref, y_ref, x_ref, dqkv_ref, att_ref, vecs_ref, *part_refs, vec_ref, scratch_ref
    )
    low = vec_ref[...]
    n_dp, length = low.shape
    width = scratch_ref.shape[1]
    row = lax.broadcasted_iota(jnp.int32, (16, n_dp), 0)
    col = lax.broadcasted_iota(jnp.int32, (16, n_dp), 1)
    lane = lax.broadcasted_iota(jnp.int32, (length, width), 0)
    place = lax.broadcasted_iota(jnp.int32, (length, width), 1)
    spread = exact(low, (place == lane).astype(F32)) + exact(high_ref[...], (place == lane + length).astype(F32))
    for j, part in enumerate(part_refs):
        part[rows:] = exact((col == 2 * (place_ref[0] ^ j) + row).astype(F32), spread).astype(BF16)


def enter_back(dmid_ref, mod_ref, keep_ref, core_ref, far_ref, res_ref):
    incoming = summed(keep_ref, core_ref, far_ref)
    normed, inverse = normalize(res_ref[...])
    g = dmid_ref[...] + norm_back(incoming * (1.0 + mod_ref[1:2]), normed, inverse)
    return g, col_sum(incoming), col_sum(incoming * normed)


def enter_back_kernel(dmid_ref, mod_ref, keep_ref, core_ref, far_ref, res_ref, g_ref, sums_ref):
    g, shift, scale = enter_back(dmid_ref, mod_ref, keep_ref, core_ref, far_ref, res_ref)
    g_ref[...] = g
    sums_ref[...] = jnp.concatenate([shift, scale], axis=0)


def previous_kernel(
    dmid_ref, mod_ref, keep_ref, core_ref, far_ref, res_ref, mod_prev_ref, out_prev_ref, g_ref, sums_ref, dmlp_ref, dgate_ref
):
    g, shift, scale = enter_back(dmid_ref, mod_ref, keep_ref, core_ref, far_ref, res_ref)
    g_ref[...] = g
    sums_ref[...] = jnp.concatenate([shift, scale], axis=0)
    dmlp_ref[...] = (g * mod_prev_ref[5:6]).astype(BF16)
    dgate_ref[...] = col_sum(g * out_prev_ref[...])


def body(
    tokens,
    condition,
    cotangent,
    mod_weight,
    mod_bias,
    qkv_weight,
    qv_bias,
    out_weight,
    out_bias,
    up_weight,
    up_bias,
    down_weight,
    down_bias,
):
    layers = mod_weight.shape[0]
    n_dp = lax.axis_size("dp")
    n_chips = n_dp // 2
    n_all = n_dp * 4
    dp = lax.axis_index("dp")
    z = lax.axis_index("tensor")
    chip = dp // 2
    core = dp % 2
    half = z // 2
    quarter = 2 * (half ^ core) + z % 2
    cols = mod_weight.shape[3]
    rows = tokens.shape[1]
    shard = qkv_weight.shape[1]
    units = up_weight.shape[2]
    piece = qv_bias.shape[3]

    place = jnp.stack([chip, core, quarter, z]).astype(jnp.int32)

    def move(values, target):
        return lax.ppermute(values, AXES, [(i, target(i)) for i in range(n_all)])

    def xor(values, mask):
        return move(values, lambda i: i ^ mask)

    def swap_core_half(i):
        return i & ~6 | (i & HALF) << 1 | (i & CORE) >> 1

    def to_other(i):
        return i ^ CORE if i & CORE else i ^ CORE ^ HALF

    def from_other(i):
        return i ^ CORE ^ HALF if i & CORE else i ^ CORE

    def to_same(i):
        return i ^ HALF if i & CORE else i

    def pick(values, index):
        return lax.dynamic_index_in_dim(values, index, 0, keepdims=False)

    def chip_gather(values, after=()):
        if n_chips > 8:
            groups = [[2 * i + c for i in range(n_chips)] for c in range(2)]
            return lax.all_gather(values, "dp", axis_index_groups=groups)
        parts = [xor(values, CHIP * j) if j else values for j in range(n_chips)]
        out = sds((n_chips,) + values.shape, values.dtype)
        return call(spread_kernel, [out], *parts, scalars=place, after=after, name="spread")[0]

    def chip_swap(values):
        if n_chips > 8:
            groups = [[2 * i + c for i in range(n_chips)] for c in range(2)]
            got = lax.all_to_all(values, "dp", 0, 0, axis_index_groups=groups, tiled=True)
            return [got[i] for i in range(n_chips)]
        return [xor(pick(values, chip ^ j), CHIP * j) if j else pick(values, chip) for j in range(n_chips)]

    def chip_sum(values):
        return sum(part.astype(F32) for part in chip_swap(values))

    def fetch_near(own, *widths):
        widths = widths or (own.shape[1],)
        return call(
            couple_kernel,
            [sds((2, own.shape[0], width), BF16) for width in widths],
            move(own, to_same),
            move(own, to_other),
            scalars=place,
            kept=tuple(range(len(widths))),
            name="couple",
        )

    def fetch_chips(pair):
        if n_chips > 8:
            return [chip_gather(pair)]
        return send_chips([pair] * n_chips, pair.shape[2] < 2 * units)

    def send_chips(parts, at_once=False):
        if at_once:
            return [parts[0]] + [xor(parts[j], CHIP * j) for j in range(1, n_chips)]
        out = [parts[0]] + [xor(parts[j], CHIP * j) for j in range(1, min(3, n_chips))]
        return out + [xor(gate(parts[j], *out[1:]), CHIP * j) for j in range(3, n_chips)]

    def join(parts):
        if n_chips > 8:
            joined, extra = parts[0][:, :, :shard], parts[0][:, :, shard:]
        else:
            height, width = parts[0].shape[1:]
            out = [sds((n_chips, 2, shard, width), BF16)]
            if height > shard:
                out.append(sds((n_chips, 2, height - shard, width), BF16))
            joined, *extra = place_parts(
                join_moves, out, *parts, scalars=place, name="join", copies=len(out) * n_chips
            )
            extra = extra[0] if extra else None
        return joined.reshape(D, joined.shape[3]), extra

    def give_chips(parts, at_once=False):
        if n_chips > 8:
            return chip_swap(parts[0].reshape(n_chips, -1, parts[0].shape[1]))
        return send_chips(parts, at_once)

    def sum_given(parts, height, *after):
        width = sum(part.shape[1] for part in parts) // n_chips
        out = sds((height, width), BF16)
        return call(
            functools.partial(sum_parts_kernel, n_chips, shard),
            [out, out],
            *parts,
            scalars=place,
            after=after,
            stored=tuple(range(len(parts))),
            kept=(0, 1),
            name="sum_parts",
        )

    def give_near(low):
        return [move(low[0], to_same), move(low[1], from_other)]

    def all_rows(values):
        other = xor(values, PARITY)
        return (values, other, xor(values, CORE), xor(other, CORE))

    def sum_rows(keep, near, send):
        got = xor(send, CORE)
        return keep, got, xor((near + got[rows:].astype(F32)).astype(BF16), PARITY)

    cond_full = condition.astype(F32)
    cond_act = jax.nn.silu(cond_full).astype(BF16)
    (cond_pair,) = call(
        couple_kernel, [sds((2, 1, D), BF16)], cond_act, xor(cond_act, CORE), scalars=place, name="couple"
    )
    cond_every = chip_gather(cond_pair).reshape(n_dp, D)
    qv_bias, out_bias, down_bias, up_bias, up_weight, _ = lax.optimization_barrier(
        (qv_bias, out_bias, down_bias, up_bias, up_weight, cond_every)
    )
    moved = move(jnp.concatenate([tokens[0], cotangent[0]]), swap_core_half)
    qkv_own = jnp.transpose(qkv_weight, (0, 2, 1, 3))
    down_own = jnp.transpose(down_weight, (0, 2, 1))

    bias_len = 12 * piece + up_bias.shape[2]
    bias_vec = jnp.concatenate(
        [
            qv_bias.reshape(layers, 6 * piece),
            out_bias.reshape(layers, 3 * piece),
            down_bias.reshape(layers, 3 * piece),
            up_bias.reshape(layers, -1),
        ],
        axis=1,
    )
    bias_block = lax.dynamic_update_slice(jnp.zeros((16, D), BF16), bias_vec, (0, 0))
    def pack_block(layer):
        return call(
            functools.partial(pack_block_kernel, layer),
            [sds((shard, 4 * cols + 2 * units), BF16)],
            qkv_own,
            out_weight,
            up_weight,
            down_own,
            name="pack_block",
        )[0]

    (own_attention,) = call(
        pack_first_kernel, [sds((shard + 16, 4 * cols), BF16)], qkv_own, out_weight, bias_block, name="pack_first"
    )
    (own_mlp,) = call(pack_mlp_kernel, [sds((shard, 2 * units), BF16)], up_weight, down_own, name="pack_mlp")
    (pair_mlp,) = fetch_near(own_mlp)
    attention_weights = [None] * layers
    mlp_weights = [None] * layers
    (pair_attention,) = fetch_near(own_attention)

    cond_slice = lax.dynamic_slice_in_dim(cond_every, dp * shard, shard, 1)
    bias_at = lax.dynamic_update_slice(
        jnp.zeros((layers, 6, cols // HD, HD), F32), mod_bias.astype(F32), (0, 0, 0, dp * piece)
    ).reshape(layers, 6, cols)
    partial_mod = jnp.einsum("ld,ydkc->lykc", cond_slice, mod_weight, preferred_element_type=F32) + bias_at
    mod_sum = chip_sum(partial_mod.reshape((n_chips, 2) + partial_mod.shape[1:]))
    parts_first = fetch_chips(gate(pair_attention, partial_mod))
    mod_sum = gate(mod_sum, pair_mlp)
    attention_weights[0], bias_every = join(parts_first)
    mod_sum = mod_sum + xor(mod_sum, CORE)
    mod_own = pick(mod_sum, half)
    mod_far = pick(mod_sum, half ^ 1)
    quarters = [xor(mod_far if mask & HALF else mod_own, mask) if mask else mod_own for mask in range(4)]
    (modulation,) = call(
        assemble_kernel,
        [sds((layers, 6, D), F32)],
        *quarters,
        scalars=place,
        after=(pair_mlp,) + tuple(parts_first[1:]),
        name="assemble",
    )

    parts_attention = [None] * layers
    parts_mlp = [None] * layers
    parts_mlp[0] = fetch_chips(gate(pair_mlp, modulation))
    qkv_bias_all, wide_bias, up_bias_all = call(
        bias_kernel,
        [sds((layers, 1, 3 * cols), F32), sds((layers, 2, D), F32), sds((layers, 1, units), F32)],
        bias_every.reshape(n_dp * 16, D),
        scalars=place,
        name="bias",
    )
    cotan, d_mlp = call(
        turn_kernel, [sds((rows, D), F32), sds((rows, D), BF16)], moved, modulation[layers - 1], kept=(0,), name="turn"
    )
    d_mlp_rows = all_rows(d_mlp)

    full = 4 * rows
    keep_send = [sds((rows, D), F32), sds((rows, D), F32), sds((full // 2, D), BF16)]
    row_f32 = sds((rows, D), F32)
    row_bf16 = sds((rows, D), BF16)
    line = sds((1, D), F32)
    attention_flops = 2 * full * D * 4 * cols + 4 * full * full * cols
    mlp_flops = 4 * full * D * units

    def parts_of(width, extra=0):
        if n_chips > 8:
            return [sds((D, width), BF16)]
        return [sds((D // n_chips + extra, width), BF16)] * n_chips

    saved = []
    residual, far_residual, attn_in = call(
        enter_kernel,
        [row_f32, row_f32, row_bf16],
        moved,
        modulation[0],
        kept=(1,),
        after=(attention_weights[0],),
        name="enter",
    )
    for layer in range(layers):
        mod = modulation[layer]
        more = layer + 1 < layers
        attn_rows = all_rows(attn_in)
        if more:
            own_block = gate(pack_block(layer + 1), attn_rows[3])
            pair_attention, pair_mlp = fetch_near(own_block, 4 * cols, 2 * units)
            parts_attention[layer + 1] = fetch_chips(gate(pair_attention, parts_mlp[layer][-1]))
            parts_mlp[layer + 1] = fetch_chips(gate(pair_mlp, parts_attention[layer + 1][-1]))
        if layer:
            attention_weights[layer] = join(parts_attention[layer])[0]
        attn_x, qkv, att, *partial = call(
            attention_kernel,
            [sds((full, D), BF16), sds((full, 3 * cols), BF16), sds((full, cols), BF16)] + keep_send,
            *attn_rows,
            attention_weights[layer],
            qkv_bias_all[layer],
            wide_bias[layer, :1],
            flops=attention_flops,
            stored=(4,),
            kept=(0, 1, 2),
            name="attention",
        )
        partial[2] = gate(partial[2], *parts_mlp[layer][1:3])
        branch, far_middle, middle, mlp_in = call(
            middle_kernel,
            [row_f32, row_f32, row_f32, row_bf16],
            residual,
            mod,
            *sum_rows(*partial),
            kept=(0, 1),
            name="middle",
        )
        mlp_rows = all_rows(mlp_in)
        mlp_weights[layer] = join(parts_mlp[layer])[0]
        mlp_x, hidden, act, *partial = call(
            mlp_kernel,
            [sds((full, D), BF16), sds((full, units), F32), sds((full, units), BF16)] + keep_send,
            *mlp_rows,
            mlp_weights[layer],
            up_bias_all[layer],
            wide_bias[layer, 1:],
            flops=mlp_flops,
            stored=(4,),
            kept=(0, 1, 2),
            name="mlp",
        )
        if more:
            partial[2] = gate(partial[2], *parts_attention[layer + 1][1:3])
        arrived = sum_rows(*partial)
        saved.append((far_residual, attn_x, qkv, att, branch, far_middle, mlp_x, hidden, act))
        if more:
            arrived = (gate(arrived[0], parts_attention[layer + 1][-1]),) + arrived[1:]
            mlp_out, far_residual, residual, attn_in = call(
                next_kernel,
                [row_f32, row_f32, row_f32, row_bf16],
                middle,
                mod,
                *arrived,
                modulation[layer + 1],
                kept=(0, 1),
                name="next",
            )
            saved[-1] += (mlp_out,)
        else:
            output, d_gate_two = call(
                last_kernel, [row_bf16, line], middle, mod, *arrived, cotan, stored=(5,), name="last"
            )

    output = move(output, swap_core_half)
    flow = cotan
    mod_lines = [None] * layers
    vecs = [None] * layers
    low = [None] * layers
    near_packs = [None] * layers
    given_attention = [None] * layers
    given_mlp = [None] * layers
    vec_shape = sds((n_dp, bias_len), F32)
    for layer in reversed(range(layers)):
        far_residual, attn_x, qkv, att, branch, far_middle, mlp_x, hidden, act = saved[layer][:9]
        mod = modulation[layer]
        more = layer + 1 < layers
        if more:
            d_mlp_rows = all_rows(d_mlp)
        mlp_y, d_hidden, *partial = call(
            mlp_back_kernel,
            [sds((full, D), BF16), sds((full, units), BF16)] + keep_send,
            *d_mlp_rows,
            mlp_weights[layer],
            hidden,
            flops=mlp_flops,
            stored=(4, 5),
            kept=(0, 1),
            name="mlp_back",
        )
        if more:
            partial[2] = gate(partial[2], *given_mlp[layer + 1][1:3])
        arrived = sum_rows(*partial)
        *grad_mlp, vec_mlp = call(
            mlp_grad_kernel,
            parts_of(2 * units) + [vec_shape],
            mlp_y,
            mlp_x,
            d_hidden,
            act,
            flops=mlp_flops,
            scalars=place,
            scratch=[pltpu.VMEM((D, 2 * units), BF16)],
            stored=(0, 1, 2, 3),
            kept=(0,),
            name="mlp_grad",
        )
        arrived = (gate(arrived[0], grad_mlp[0], *(given_mlp[layer + 1][3:] if more else ())),) + arrived[1:]
        if more:
            grad_mlp = [gate(part, *given_attention[layer + 1][1:]) for part in grad_mlp]
        given_mlp[layer] = give_chips(grad_mlp)
        d_middle, d_branch, sums_mid = call(
            middle_back_kernel,
            [row_f32, row_bf16, sds((3, D), F32)],
            flow,
            mod,
            *arrived,
            far_middle,
            branch,
            stored=(5, 6) if more else (0, 5, 6),
            name="middle_back",
        )
        if more:
            d_branch = gate(d_branch, *given_attention[layer + 1][1:])
            low[layer + 1] = sum_given(list(given_attention[layer + 1]) + list(given_mlp[layer + 1]), shard)
            near_packs[layer + 1] = give_near(low[layer + 1])
        d_branch_rows = all_rows(d_branch)
        attn_y, d_qkv, *partial = call(
            attention_back_kernel,
            [sds((full, D), BF16), sds((full, 3 * cols), BF16)] + keep_send,
            *d_branch_rows,
            attention_weights[layer],
            qkv,
            flops=attention_flops * 2,
            stored=(4, 5),
            kept=(0, 1),
            name="attention_back",
        )
        if more:
            partial[2] = gate(partial[2], *given_mlp[layer][1:3], near_packs[layer + 1][0])
        arrived = sum_rows(*partial)
        *grad_attention, vecs[layer] = call(
            functools.partial(
                attention_grad_kernel if layer or n_chips > 8 else attention_grad_last_kernel,
                1 if n_chips > 8 else n_chips,
            ),
            parts_of(4 * cols, 0 if layer else 16) + [vec_shape],
            attn_y,
            attn_x,
            d_qkv,
            att,
            vec_mlp,
            *(() if layer or n_chips > 8 else (vecs[1],)),
            flops=attention_flops,
            scalars=place,
            scratch=[pltpu.VMEM((D, 4 * cols), BF16)],
            stored=(0, 1, 2, 3),
            kept=(0,),
            name="attention_grad",
        )
        after = (grad_attention[0],)
        if layer == 0:
            after = after + (output,) + tuple(given_mlp[0][3:]) + tuple(near_packs[upper][1] for upper in range(1, layers))
        if layer == 0:
            height = 2 * shard + 16
            if n_chips > 8:
                rows_bias = jnp.concatenate([vecs[i] for i in range(layers)], axis=1).astype(BF16)
                rows_bias = jnp.pad(
                    rows_bias.reshape(n_chips, 2, -1), ((0, 0), (0, 14), (0, 4 * cols - layers * bias_len))
                )
                rows_all = jnp.concatenate(
                    [grad_attention[0].reshape(n_chips, 2 * shard, 4 * cols), rows_bias], axis=1
                )
                grad_attention = [rows_all.reshape(n_chips * height, 4 * cols)]
        given_attention[layer] = give_chips([gate(part, *given_mlp[layer][1:]) for part in grad_attention], True)
        if layer:
            flow, sums_in, d_mlp, gate_next = call(
                previous_kernel,
                [row_f32, sds((2, D), F32), row_bf16, line],
                d_middle,
                mod,
                *arrived,
                far_residual,
                modulation[layer - 1],
                saved[layer - 1][9],
                stored=(5, 7),
                after=after,
                name="previous",
            )
        else:
            flow, sums_in = call(
                enter_back_kernel,
                [row_f32, sds((2, D), F32)],
                d_middle,
                mod,
                *arrived,
                far_residual,
                stored=(5,),
                after=after,
                name="enter_back",
            )
            gate_next = None
        mod_lines[layer] = jnp.concatenate([sums_in, sums_mid, d_gate_two], axis=0)
        d_gate_two = gate_next

    d_mod = jnp.stack(mod_lines)
    d_mod = d_mod + xor(d_mod, CORE)
    d_mod = (d_mod + xor(d_mod, PARITY)).astype(BF16).reshape(layers * 6, 4, cols)
    d_mod = jnp.transpose(d_mod, (1, 0, 2))
    mine = pick(d_mod, z)
    far = xor(pick(d_mod, z ^ HALF), HALF)
    d_mod_pair = jnp.where(half == 0, jnp.stack([mine, far]), jnp.stack([far, mine]))
    low_attention = sum_given(list(given_attention[0]), shard + 16)
    near_attention = give_near(low_attention)
    near_mlp = give_near(sum_given(list(given_mlp[0]), shard))
    near_packs[0] = near_attention + near_mlp
    d_mod_pair = gate(d_mod_pair, *given_attention[0][1:])
    d_mod_every = gate(chip_gather(d_mod_pair), *near_mlp).reshape(n_dp, layers, 6, cols)
    grad_mod_w = jnp.einsum("ld,lykc->ykdc", cond_slice, d_mod_every, preferred_element_type=F32)
    grad_mod_w = jnp.transpose(grad_mod_w, (0, 2, 1, 3))
    grad_mod_b = jnp.sum(d_mod_every.astype(F32), axis=0).reshape(layers, 6, cols // HD, HD)
    grad_mod_b = lax.dynamic_slice_in_dim(grad_mod_b, dp * piece, piece, 3)
    cond_pieces = jnp.einsum("lykc,ydkc->ld", d_mod_every, mod_weight, preferred_element_type=F32)
    mixed = jnp.stack(chip_swap(cond_pieces.reshape(n_chips, 2, shard)))
    if n_chips <= 8:
        mixed = jnp.take(mixed, chip ^ jnp.arange(n_chips), axis=0)
    cond_pieces = jnp.transpose(mixed, (1, 0, 2))
    cond_pieces = gate(cond_pieces, *low_attention)
    cond_mine = pick(cond_pieces, core)
    cond_sent = xor(pick(cond_pieces, core ^ 1), CORE)
    cond_total = jnp.where(
        core == 0, jnp.stack([cond_mine, cond_sent], axis=1), jnp.stack([cond_sent, cond_mine], axis=1)
    ).reshape(1, D)
    cond_total = gate(cond_total + xor(cond_total, PARITY), *near_attention)
    cond_total = cond_total + xor(cond_total, HALF)
    sigmoid_cond = jax.nn.sigmoid(cond_full)
    grad_condition = cond_total * sigmoid_cond * (1.0 + cond_full * (1.0 - sigmoid_cond))

    grad_tokens = move(gate(flow, cond_mine), swap_core_half)
    output, grad_tokens, grad_qkv, grad_out, grad_up, grad_down, vec = call(
        finish_kernel,
        [
            row_bf16,
            row_f32,
            sds((layers, 3, shard, cols), F32),
            sds((layers, cols, shard), F32),
            sds((layers, shard, units), F32),
            sds((layers, shard, units), F32),
            sds((8, 4 * cols), F32),
        ],
        output,
        grad_tokens,
        *[part for layer in range(layers) for part in near_packs[layer]],
        kept=(0, 1, 2, 3, 4, 5),
        name="finish",
    )
    vec = vec[0, : layers * bias_len].reshape(layers, bias_len)
    vec_heads = vec[:, : 12 * piece].reshape(layers, 4, 3, piece)
    return (
        output[None],
        grad_tokens[None],
        grad_condition,
        grad_mod_w,
        grad_mod_b,
        jnp.transpose(grad_qkv, (0, 2, 1, 3)),
        vec_heads[:, :2],
        grad_out,
        vec_heads[:, 2],
        grad_up,
        vec[:, 12 * piece :].reshape(layers, 1, -1),
        jnp.transpose(grad_down, (0, 2, 1)),
        vec_heads[:, 3],
    )


def solution(mesh):
    in_specs = (
        P("dp", "tensor", None),
        P("dp", None),
        P("dp", "tensor", None),
        P(None, "dp", None, "tensor"),
        P(None, None, "tensor", "dp"),
        P(None, "dp", None, "tensor"),
        P(None, None, "tensor", "dp"),
        P(None, "tensor", "dp"),
        P(None, "tensor", "dp"),
        P(None, "dp", "tensor"),
        P(None, "tensor", "dp"),
        P(None, "tensor", "dp"),
        P(None, "tensor", "dp"),
    )
    out_specs = (
        P("dp", "tensor", None),
        P("dp", "tensor", None),
        P("dp", None),
        P(None, "dp", None, "tensor"),
        P(None, None, "tensor", "dp"),
        P(None, "dp", None, "tensor"),
        P(None, None, "tensor", "dp"),
        P(None, "tensor", "dp"),
        P(None, "tensor", "dp"),
        P(None, "dp", "tensor"),
        P(None, "tensor", "dp"),
        P(None, "tensor", "dp"),
        P(None, "tensor", "dp"),
    )
    return jax.shard_map(body, mesh=mesh, in_specs=in_specs, out_specs=out_specs, check_vma=False)
```

```python
import functools
import math

import jax
import jax.numpy as jnp
from jax import lax
from jax.experimental import pallas as pl
from jax.experimental.pallas import tpu as pltpu
from jax.sharding import PartitionSpec as P

D = 768
HD = 64
EPS = 1e-06
AXES = ("dp", "tensor")
F32 = jnp.float32
BF16 = jnp.bfloat16
VMEM_LIMIT = 16 * 1024 * 1024

PARITY = 1
HALF = 2
CORE = 4
CHIP = 8


class Stored:
    def __init__(self, source, target, sem, local):
        self.copy = pltpu.make_async_copy(source, target, sem)
        self.local = local
        self.shape = local.shape
        self.busy = False
        self.dirty = False

    def start(self):
        self.copy.start()
        self.busy = True
        self.dirty = False

    def settle(self):
        if self.busy:
            self.copy.wait()
            self.busy = False

    def __getitem__(self, index):
        self.settle()
        return self.local[index]

    def __setitem__(self, index, value):
        self.local[index] = value
        self.dirty = True
        if index is Ellipsis:
            self.start()


def call(
    kernel, out_shape, *args, flops=0, name=None, scalars=None, after=(), scratch=(), stored=(), kept=(), window=()
):
    size = sum(a.size * a.dtype.itemsize for a in args) + sum(math.prod(o.shape) * o.dtype.itemsize for o in out_shape)
    hbm = pl.BlockSpec(memory_space=pltpu.HBM)
    vmem = pl.BlockSpec(memory_space=pltpu.VMEM)
    in_specs = [hbm if i in stored else vmem for i in range(len(args))]
    out_specs = [hbm if i in kept else vmem for i in range(len(out_shape))]
    window = dict(window)
    copies = [pltpu.VMEM((args[i].shape[0], window[i][1]) if i in window else args[i].shape, args[i].dtype) for i in stored]
    copies += [pltpu.VMEM(out_shape[i].shape, out_shape[i].dtype) for i in kept]
    lead = 0
    if after:
        args = (gate(args[0], *after),) + args[1:]
    if scalars is not None:
        args = (scalars,) + args
        in_specs = [pl.BlockSpec(memory_space=pltpu.SMEM)] + in_specs
        lead = 1

    def run(*refs):
        ins = list(refs[: len(args)])
        outs = list(refs[len(args) : len(args) + len(out_shape)])
        rest = refs[len(args) + len(out_shape) :]
        own, local = rest[: len(scratch)], rest[len(scratch) :]
        held = []
        for n, i in enumerate(stored):
            source = ins[lead + i].at[:, pl.ds(*window[i])] if i in window else ins[lead + i]
            held.append(Stored(source, local[n], local[-1].at[n], local[n]))
            held[-1].start()
            ins[lead + i] = held[-1]
        for n, i in enumerate(kept, len(stored)):
            held.append(Stored(local[n], outs[i], local[-1].at[n], local[n]))
            outs[i] = held[-1]
        kernel(*ins, *outs, *own)
        for item in held:
            if item.dirty:
                item.start()
        for item in held:
            item.settle()

    return pl.pallas_call(
        run,
        out_shape=out_shape,
        in_specs=in_specs,
        out_specs=out_specs,
        scratch_shapes=list(scratch) + copies + ([pltpu.SemaphoreType.DMA((len(copies),))] if copies else []),
        compiler_params=pltpu.CompilerParams(vmem_limit_bytes=VMEM_LIMIT),
        cost_estimate=pl.CostEstimate(flops=flops, bytes_accessed=size, transcendentals=0),
        name=name,
    )(*args)


def gate(value, *others):
    return lax.optimization_barrier((value,) + others)[0]


def place_parts(kernel, out_shape, *args, scalars, name, copies):
    count = len(args)

    def run(place_ref, *refs):
        outs = refs[count : count + len(out_shape)]
        sems = refs[-1]
        moves = [
            pltpu.make_async_copy(source, target, sems.at[n])
            for n, (source, target) in enumerate(kernel(place_ref, refs[:count], outs))
        ]
        for item in moves:
            item.start()
        for item in moves:
            item.wait()

    size = sum(a.size * a.dtype.itemsize for a in args)
    return pl.pallas_call(
        run,
        out_shape=out_shape,
        in_specs=[pl.BlockSpec(memory_space=pltpu.SMEM)]
        + [pl.BlockSpec(memory_space=pltpu.HBM)] * count,
        out_specs=[pl.BlockSpec(memory_space=pltpu.HBM)] * len(out_shape),
        scratch_shapes=[pltpu.SemaphoreType.DMA((copies,))],
        compiler_params=pltpu.CompilerParams(vmem_limit_bytes=VMEM_LIMIT),
        cost_estimate=pl.CostEstimate(flops=0, bytes_accessed=2 * size, transcendentals=0),
        name=name,
    )(scalars, *args)


def sds(shape, dtype):
    return jax.ShapeDtypeStruct(shape, dtype)


def dot(a, b, ca=1, cb=0):
    return lax.dot_general(a, b, (((ca,), (cb,)), ((), ())), preferred_element_type=F32)


def normalize(values):
    centered = values - jnp.mean(values, axis=-1, keepdims=True)
    inverse = lax.rsqrt(jnp.mean(centered * centered, axis=-1, keepdims=True) + EPS)
    return centered * inverse, inverse


def norm_back(incoming, normed, inverse):
    average = jnp.mean(incoming, axis=-1, keepdims=True)
    along = jnp.mean(incoming * normed, axis=-1, keepdims=True)
    return inverse * (incoming - average - normed * along)


def col_sum(values):
    return jnp.sum(values, axis=0, keepdims=True)


def modulate(values, mod, shift, scale):
    normed, _ = normalize(values)
    return (normed * (1.0 + mod[scale : scale + 1]) + mod[shift : shift + 1]).astype(BF16)


def rows_of(refs):
    return jnp.concatenate([ref[...] for ref in refs], axis=0)


def split_out(total, keep_ref, near_ref, send_ref):
    quarter = total.shape[0] // 4
    keep_ref[...] = total[:quarter]
    near_ref[...] = total[quarter : 2 * quarter]
    send_ref[...] = total[2 * quarter :].astype(BF16)


def summed(keep_ref, core_ref, far_ref):
    return keep_ref[...] + core_ref[: keep_ref.shape[0]].astype(F32) + far_ref[...].astype(F32)


def attention_pack(layer, qkv_ref, out_ref):
    out = out_ref[layer].astype(F32).T.astype(BF16)
    return jnp.concatenate([qkv_ref[layer, 0], qkv_ref[layer, 1], qkv_ref[layer, 2], out], axis=1)


def pack_block_kernel(layer, qkv_ref, out_ref, up_ref, down_ref, pack_ref):
    wide = 4 * out_ref.shape[1]
    units = up_ref.shape[2]
    pack_ref[:, :wide] = attention_pack(layer, qkv_ref, out_ref)
    pack_ref[:, wide : wide + units] = up_ref[layer]
    pack_ref[:, wide + units :] = down_ref[layer]


def pack_first_kernel(qkv_ref, out_ref, bias_ref, pack_ref):
    shard = out_ref.shape[2]
    pack_ref[:shard] = attention_pack(0, qkv_ref, out_ref)
    pack_ref[shard:] = bias_ref[...]


def pack_mlp_kernel(up_ref, down_ref, pack_ref):
    units = up_ref.shape[2]
    pack_ref[:, :units] = up_ref[0]
    pack_ref[:, units:] = down_ref[0]


def join_moves(place_ref, ins, outs):
    shard = outs[0].shape[2]
    moves = []
    for j, part in enumerate(ins):
        at = place_ref[0] ^ j
        moves.append((part.at[:, :shard], outs[0].at[at]))
        if len(outs) == 2:
            moves.append((part.at[:, shard:], outs[1].at[at]))
    return moves


def assemble_kernel(place_ref, *refs):
    parts, out_ref = refs[:-1], refs[-1]
    cols = parts[0].shape[2]
    for layer in range(out_ref.shape[0]):
        for at in range(4):
            quarter = sum(
                jnp.where(place_ref[3] ^ mask == at, part[layer], 0.0) for mask, part in enumerate(parts)
            )
            out_ref[layer, :, at * cols : (at + 1) * cols] = quarter


def spread_kernel(place_ref, *refs):
    parts, out_ref = refs[:-1], refs[-1]
    for j, part in enumerate(parts):
        out_ref[place_ref[0] ^ j] = part[...]


def couple_kernel(place_ref, own_ref, other_ref, *out_refs):
    first = place_ref[1] == 0
    at = 0
    for out_ref in out_refs:
        end = at + out_ref.shape[-1]
        own, other = own_ref[..., at:end], other_ref[..., at:end]
        out_ref[0] = jnp.where(first, own, other)
        out_ref[1] = jnp.where(first, other, own)
        at = end


def head_select(n_dp, piece, cols):
    row = lax.broadcasted_iota(jnp.int32, (3 * piece, cols), 0)
    col = lax.broadcasted_iota(jnp.int32, (3 * piece, cols), 1)
    return (row == col // HD * piece + col % piece).astype(F32)


def head_mask(n_dp, piece, cols):
    row = lax.broadcasted_iota(jnp.int32, (n_dp, cols), 0)
    col = lax.broadcasted_iota(jnp.int32, (n_dp, cols), 1)
    return (col % HD // piece == row).astype(F32)


def exact(a, b):
    return lax.dot_general(
        a, b, (((1,), (0,)), ((), ())), preferred_element_type=F32, precision=lax.Precision.HIGHEST
    )


def heads_back(line, at, n_dp, length):
    cols, piece = line.shape[1], HD // n_dp
    row = lax.broadcasted_iota(jnp.int32, (length, cols), 0) - at
    col = lax.broadcasted_iota(jnp.int32, (length, cols), 1)
    select = (row == col // HD * piece + col % piece).astype(F32)
    return lax.dot_general(
        head_mask(n_dp, piece, cols) * line,
        select,
        (((1,), (1,)), ((), ())),
        preferred_element_type=F32,
        precision=lax.Precision.HIGHEST,
    )


def units_back(line, at, n_dp, length):
    units = line.shape[1]
    width = units // n_dp
    row = lax.broadcasted_iota(jnp.int32, (length, units), 0) - at
    col = lax.broadcasted_iota(jnp.int32, (length, units), 1)
    mask = (
        lax.broadcasted_iota(jnp.int32, (n_dp, units), 1) // width
        == lax.broadcasted_iota(jnp.int32, (n_dp, units), 0)
    )
    return lax.dot_general(
        mask.astype(F32) * line,
        (col % width == row).astype(F32),
        (((1,), (1,)), ((), ())),
        preferred_element_type=F32,
        precision=lax.Precision.HIGHEST,
    )


def own_quarter(line, cols, place_ref):
    return sum(
        jnp.where(place_ref[2] == i, line[:, i * cols : (i + 1) * cols], 0.0) for i in range(line.shape[1] // cols)
    )


def bias_kernel(place_ref, vec_ref, qkv_ref, wide_ref, up_ref):
    n_dp, piece = vec_ref.shape[0] // 16, HD * 16 // vec_ref.shape[0]
    vec_row = lax.broadcasted_iota(jnp.int32, (n_dp, vec_ref.shape[0]), 0)
    vec_col = lax.broadcasted_iota(jnp.int32, (n_dp, vec_ref.shape[0]), 1)
    cols, units = qkv_ref.shape[2] // 3, up_ref.shape[2]
    select, mask = head_select(n_dp, piece, cols), head_mask(n_dp, piece, cols)
    width = units // n_dp
    row = lax.broadcasted_iota(jnp.int32, (width, units), 0)
    col = lax.broadcasted_iota(jnp.int32, (width, units), 1)
    up_select = (col % width == row).astype(F32)
    up_row = lax.broadcasted_iota(jnp.int32, (n_dp, units), 0)
    up_col = lax.broadcasted_iota(jnp.int32, (n_dp, units), 1)
    up_mask = (up_col // width == up_row).astype(F32)
    quarters = wide_ref.shape[2] // cols
    place = lax.broadcasted_iota(jnp.int32, (1, quarters * cols), 1) // cols == place_ref[2]
    for layer in range(qkv_ref.shape[0]):
        vec = dot((vec_col == 16 * vec_row + layer).astype(BF16), vec_ref[...])
        heads = [col_sum(exact(vec[:, 3 * t * piece : 3 * (t + 1) * piece], select) * mask) for t in range(4)]
        qkv_ref[layer] = jnp.concatenate([heads[0], jnp.zeros_like(heads[0]), heads[1]], axis=1)
        for t in range(2):
            wide_ref[layer, t : t + 1] = jnp.where(place, jnp.concatenate([heads[2 + t]] * quarters, axis=1), 0.0)
        up_ref[layer] = col_sum(exact(vec[:, 12 * piece : 12 * piece + width], up_select) * up_mask)


def sum_parts_kernel(count, shard, place_ref, *refs):
    parts, (same_ref, other_ref) = refs[:-2], refs[-2:]
    first = place_ref[1] == 0
    at = 0
    for start in range(0, len(parts), count):
        low = sum(part[...].astype(F32) for part in parts[start : start + count])
        end = at + low.shape[1]
        mine, far = low[:shard], low[shard : 2 * shard]
        same_ref[:shard, at:end] = jnp.where(first, mine, far).astype(BF16)
        other_ref[:shard, at:end] = jnp.where(first, far, mine).astype(BF16)
        if low.shape[0] > 2 * shard:
            mine, far = low[2 * shard : 2 * shard + 1], low[2 * shard + 1 : 2 * shard + 2]
            same_ref[shard:, at:end] = jnp.broadcast_to(jnp.where(first, mine, far), (16, end - at)).astype(BF16)
            other_ref[shard:, at:end] = jnp.broadcast_to(jnp.where(first, far, mine), (16, end - at)).astype(BF16)
        at = end


def finish_kernel(last_ref, flow_ref, *refs):
    parts, (last_out_ref, flow_out_ref, qkv_ref, out_ref, up_ref, down_ref, vec_ref) = refs[:-7], refs[-7:]
    last_out_ref[...] = last_ref[...]
    flow_out_ref[...] = flow_ref[...]
    shard, cols, units = up_ref.shape[1], out_ref.shape[1], up_ref.shape[2]
    for layer in range(qkv_ref.shape[0]):
        if layer == 0:
            total = parts[0][...].astype(F32) + parts[1][...].astype(F32)
            vec_ref[...] = total[shard : shard + 8]
            mlp = parts[2][...].astype(F32) + parts[3][...].astype(F32)
        else:
            total = parts[2 * layer + 2][...].astype(F32) + parts[2 * layer + 3][...].astype(F32)
            mlp = total[:, 4 * cols :]
        for i in range(3):
            qkv_ref[layer, i] = total[:shard, i * cols : (i + 1) * cols]
        out_ref[layer] = total[:shard, 3 * cols : 4 * cols].T
        up_ref[layer] = mlp[:, :units]
        down_ref[layer] = mlp[:, units:]


def enter_kernel(moved_ref, mod_ref, res_ref, far_res_ref, in_ref):
    residual = moved_ref[: res_ref.shape[0]].astype(F32)
    far_res_ref[...] = residual
    res_ref[...] = residual
    in_ref[...] = modulate(residual, mod_ref[...], 0, 1)


def attention_kernel(x0, x1, x2, x3, w_ref, bias_ref, bo_ref, x_ref, qkv_ref, att_ref, keep_ref, near_ref, send_ref):
    x = rows_of((x0, x1, x2, x3))
    x_ref[...] = x
    cols = w_ref.shape[1] // 4
    qkv = (dot(x, w_ref[:, : 3 * cols]) + bias_ref[...]).astype(BF16)
    qkv_ref[...] = qkv
    parts = []
    for head in range(cols // HD):
        at = head * HD
        q = qkv[:, at : at + HD]
        k = qkv[:, cols + at : cols + at + HD]
        v = qkv[:, 2 * cols + at : 2 * cols + at + HD]
        scores = dot(q, k, 1, 1) * (1.0 / math.sqrt(HD))
        expo = jnp.exp(scores - jnp.max(scores, axis=-1, keepdims=True))
        probs = expo / jnp.sum(expo, axis=-1, keepdims=True)
        parts.append(dot(probs.astype(BF16), v))
    att = jnp.concatenate(parts, axis=1).astype(BF16)
    att_ref[...] = att
    split_out(dot(att, w_ref[:, 3 * cols :], 1, 1) + bo_ref[...], keep_ref, near_ref, send_ref)


def middle_kernel(res_ref, mod_ref, keep_ref, core_ref, far_ref, branch_ref, far_mid_ref, mid_ref, in_ref):
    mod = mod_ref[...]
    branch = summed(keep_ref, core_ref, far_ref)
    branch_ref[...] = branch
    middle = res_ref[...] + mod[2:3] * branch
    far_mid_ref[...] = middle
    mid_ref[...] = middle
    in_ref[...] = modulate(middle, mod, 3, 4)


def mlp_kernel(x0, x1, x2, x3, w_ref, bu_ref, bd_ref, x_ref, hid_ref, act_ref, keep_ref, near_ref, send_ref):
    x = rows_of((x0, x1, x2, x3))
    x_ref[...] = x
    units = w_ref.shape[1] // 2
    hidden = dot(x, w_ref[:, :units]) + bu_ref[...]
    hid_ref[...] = hidden
    act = (0.5 * hidden * (1.0 + lax.erf(hidden * 0.7071067811865476))).astype(BF16)
    act_ref[...] = act
    split_out(dot(act, w_ref[:, units:], 1, 1) + bd_ref[...], keep_ref, near_ref, send_ref)


def next_kernel(
    mid_ref, mod_ref, keep_ref, core_ref, far_ref, mod_next_ref, out_ref, far_res_ref, res_ref, in_ref
):
    mlp_out = summed(keep_ref, core_ref, far_ref)
    out_ref[...] = mlp_out
    residual = mid_ref[...] + mod_ref[5:6] * mlp_out
    far_res_ref[...] = residual
    res_ref[...] = residual
    in_ref[...] = modulate(residual, mod_next_ref[...], 0, 1)


def last_kernel(mid_ref, mod_ref, keep_ref, core_ref, far_ref, g_ref, out_ref, dgate_ref):
    mlp_out = summed(keep_ref, core_ref, far_ref)
    out_ref[...] = (mid_ref[...] + mod_ref[5:6] * mlp_out).astype(BF16)
    dgate_ref[...] = col_sum(g_ref[...] * mlp_out)


def turn_kernel(moved_ref, mod_ref, g_ref, dmlp_ref):
    g = moved_ref[dmlp_ref.shape[0] :].astype(F32)
    g_ref[...] = g
    dmlp_ref[...] = (g * mod_ref[5:6]).astype(BF16)


def mlp_back_kernel(x0, x1, x2, x3, w_ref, hid_ref, x_ref, dhid_ref, keep_ref, near_ref, send_ref):
    x = rows_of((x0, x1, x2, x3))
    x_ref[...] = x
    units = w_ref.shape[1] // 2
    hidden = hid_ref[...]
    d_active = dot(x, w_ref[:, units:])
    cumulative = 0.5 * (1.0 + lax.erf(hidden * 0.7071067811865476))
    density = jnp.exp(-0.5 * hidden * hidden) * 0.3989422804014327
    d_hidden = (d_active * (cumulative + hidden * density)).astype(BF16)
    dhid_ref[...] = d_hidden
    split_out(dot(d_hidden, w_ref[:, :units], 1, 1), keep_ref, near_ref, send_ref)


def give_parts(grad, place_ref, scratch_ref, part_refs):
    if len(part_refs) == 1:
        part_refs[0][...] = grad.astype(BF16)
        return
    scratch_ref[...] = grad.astype(BF16)
    rows = part_refs[0].shape[0]
    for j, part in enumerate(part_refs):
        start = pl.multiple_of((place_ref[0] ^ j) * rows, rows)
        part[...] = scratch_ref[pl.ds(start, rows), :]


def mlp_grad_kernel(place_ref, y_ref, x_ref, dhid_ref, act_ref, *refs):
    part_refs, (vec_ref, scratch_ref) = refs[:-2], refs[-2:]
    y = y_ref[...]
    d_hidden = dhid_ref[...]
    grad = jnp.concatenate([dot(x_ref[...], d_hidden, 0, 0), dot(y, act_ref[...], 0, 0)], axis=1)
    give_parts(grad, place_ref, scratch_ref, part_refs)
    n_dp, length = vec_ref.shape
    piece = HD // n_dp
    cols = y.shape[1] // 4
    down = own_quarter(col_sum(y.astype(F32)), cols, place_ref)
    up = col_sum(d_hidden.astype(F32))
    vec_ref[...] = heads_back(down, 9 * piece, n_dp, length) + units_back(up, 12 * piece, n_dp, length)


def middle_back_kernel(g_ref, mod_ref, keep_ref, core_ref, far_ref, mid_ref, branch_ref, dmid_ref, dbranch_ref, sums_ref):
    mod = mod_ref[...]
    incoming = summed(keep_ref, core_ref, far_ref)
    normed, inverse = normalize(mid_ref[...])
    d_middle = g_ref[...] + norm_back(incoming * (1.0 + mod[4:5]), normed, inverse)
    dmid_ref[...] = d_middle
    dbranch_ref[...] = (d_middle * mod[2:3]).astype(BF16)
    sums_ref[...] = jnp.concatenate(
        [col_sum(d_middle * branch_ref[...]), col_sum(incoming), col_sum(incoming * normed)], axis=0
    )


def attention_back_kernel(x0, x1, x2, x3, w_ref, qkv_ref, x_ref, dqkv_ref, keep_ref, near_ref, send_ref):
    x = rows_of((x0, x1, x2, x3))
    x_ref[...] = x
    cols = w_ref.shape[1] // 4
    qkv = qkv_ref[...]
    scaling = 1.0 / math.sqrt(HD)
    d_att = dot(x, w_ref[:, 3 * cols :]).astype(BF16)
    grads = ([], [], [])
    for head in range(cols // HD):
        at = head * HD
        q = qkv[:, at : at + HD]
        k = qkv[:, cols + at : cols + at + HD]
        v = qkv[:, 2 * cols + at : 2 * cols + at + HD]
        d_out = d_att[:, at : at + HD]
        scores = dot(q, k, 1, 1) * scaling
        expo = jnp.exp(scores - jnp.max(scores, axis=-1, keepdims=True))
        probs = expo / jnp.sum(expo, axis=-1, keepdims=True)
        d_probs = dot(d_out, v, 1, 1)
        d_scores = (probs * (d_probs - jnp.sum(probs * d_probs, axis=-1, keepdims=True))).astype(BF16)
        grads[0].append(dot(d_scores, k) * scaling)
        grads[1].append(dot(d_scores, q, 0, 0) * scaling)
        grads[2].append(dot(probs.astype(BF16), d_out, 0, 0))
    d_qkv = jnp.concatenate(grads[0] + grads[1] + grads[2], axis=1).astype(BF16)
    dqkv_ref[...] = d_qkv
    split_out(dot(d_qkv, w_ref[:, : 3 * cols], 1, 1), keep_ref, near_ref, send_ref)


def attention_grad_kernel(n_parts, place_ref, y_ref, x_ref, dqkv_ref, att_ref, vecs_ref, *refs):
    part_refs, (vec_ref, scratch_ref) = refs[:-2], refs[-2:]
    y = y_ref[...]
    d_qkv = dqkv_ref[...]
    cols = d_qkv.shape[1] // 3
    wide = 4 * cols
    grad = jnp.concatenate([dot(x_ref[...], d_qkv, 0, 0), dot(y, att_ref[...], 0, 0)], axis=1)
    scratch_ref[...] = grad.astype(BF16)
    n_dp, length = vec_ref.shape
    piece = HD // n_dp
    total = col_sum(d_qkv.astype(F32))
    out = own_quarter(col_sum(y.astype(F32)), cols, place_ref)
    vec = vecs_ref[...] + (
        heads_back(total[:, :cols], 0, n_dp, length)
        + heads_back(total[:, 2 * cols :], 3 * piece, n_dp, length)
        + heads_back(out, 6 * piece, n_dp, length)
    )
    vec_ref[...] = vec
    if n_parts == 1:
        part_refs[0][...] = scratch_ref[...]
        return
    rows = scratch_ref.shape[0] // n_parts
    for j, part in enumerate(part_refs):
        at = place_ref[0] ^ j
        part[:rows] = scratch_ref[pl.ds(pl.multiple_of(at * rows, rows), rows), :]


def attention_grad_last_kernel(n_parts, place_ref, y_ref, x_ref, dqkv_ref, att_ref, vecs_ref, high_ref, *refs):
    part_refs, (vec_ref, scratch_ref) = refs[:-2], refs[-2:]
    rows = scratch_ref.shape[0] // n_parts
    attention_grad_kernel(
        n_parts, place_ref, y_ref, x_ref, dqkv_ref, att_ref, vecs_ref, *part_refs, vec_ref, scratch_ref
    )
    low = vec_ref[...]
    n_dp, length = low.shape
    width = scratch_ref.shape[1]
    row = lax.broadcasted_iota(jnp.int32, (16, n_dp), 0)
    col = lax.broadcasted_iota(jnp.int32, (16, n_dp), 1)
    lane = lax.broadcasted_iota(jnp.int32, (length, width), 0)
    place = lax.broadcasted_iota(jnp.int32, (length, width), 1)
    spread = exact(low, (place == lane).astype(F32)) + exact(high_ref[...], (place == lane + length).astype(F32))
    for j, part in enumerate(part_refs):
        part[rows:] = exact((col == 2 * (place_ref[0] ^ j) + row).astype(F32), spread).astype(BF16)


def enter_back(dmid_ref, mod_ref, keep_ref, core_ref, far_ref, res_ref):
    incoming = summed(keep_ref, core_ref, far_ref)
    normed, inverse = normalize(res_ref[...])
    g = dmid_ref[...] + norm_back(incoming * (1.0 + mod_ref[1:2]), normed, inverse)
    return g, col_sum(incoming), col_sum(incoming * normed)


def enter_back_kernel(dmid_ref, mod_ref, keep_ref, core_ref, far_ref, res_ref, g_ref, sums_ref):
    g, shift, scale = enter_back(dmid_ref, mod_ref, keep_ref, core_ref, far_ref, res_ref)
    g_ref[...] = g
    sums_ref[...] = jnp.concatenate([shift, scale], axis=0)


def previous_kernel(
    dmid_ref, mod_ref, keep_ref, core_ref, far_ref, res_ref, mod_prev_ref, out_prev_ref, g_ref, sums_ref, dmlp_ref, dgate_ref
):
    g, shift, scale = enter_back(dmid_ref, mod_ref, keep_ref, core_ref, far_ref, res_ref)
    g_ref[...] = g
    sums_ref[...] = jnp.concatenate([shift, scale], axis=0)
    dmlp_ref[...] = (g * mod_prev_ref[5:6]).astype(BF16)
    dgate_ref[...] = col_sum(g * out_prev_ref[...])


def body(
    tokens,
    condition,
    cotangent,
    mod_weight,
    mod_bias,
    qkv_weight,
    qv_bias,
    out_weight,
    out_bias,
    up_weight,
    up_bias,
    down_weight,
    down_bias,
):
    layers = mod_weight.shape[0]
    n_dp = lax.axis_size("dp")
    n_chips = n_dp // 2
    n_all = n_dp * 4
    dp = lax.axis_index("dp")
    z = lax.axis_index("tensor")
    chip = dp // 2
    core = dp % 2
    half = z // 2
    quarter = 2 * (half ^ core) + z % 2
    cols = mod_weight.shape[3]
    rows = tokens.shape[1]
    shard = qkv_weight.shape[1]
    units = up_weight.shape[2]
    piece = qv_bias.shape[3]

    place = jnp.stack([chip, core, quarter, z]).astype(jnp.int32)

    def move(values, target):
        return lax.ppermute(values, AXES, [(i, target(i)) for i in range(n_all)])

    def xor(values, mask):
        return move(values, lambda i: i ^ mask)

    def swap_core_half(i):
        return i & ~6 | (i & HALF) << 1 | (i & CORE) >> 1

    def to_other(i):
        return i ^ CORE if i & CORE else i ^ CORE ^ HALF

    def from_other(i):
        return i ^ CORE ^ HALF if i & CORE else i ^ CORE

    def to_same(i):
        return i ^ HALF if i & CORE else i

    def pick(values, index):
        return lax.dynamic_index_in_dim(values, index, 0, keepdims=False)

    def chip_gather(values, after=()):
        if n_chips > 8:
            groups = [[2 * i + c for i in range(n_chips)] for c in range(2)]
            return lax.all_gather(values, "dp", axis_index_groups=groups)
        parts = [xor(values, CHIP * j) if j else values for j in range(n_chips)]
        out = sds((n_chips,) + values.shape, values.dtype)
        return call(spread_kernel, [out], *parts, scalars=place, after=after, name="spread")[0]

    def chip_swap(values):
        if n_chips > 8:
            groups = [[2 * i + c for i in range(n_chips)] for c in range(2)]
            got = lax.all_to_all(values, "dp", 0, 0, axis_index_groups=groups, tiled=True)
            return [got[i] for i in range(n_chips)]
        return [xor(pick(values, chip ^ j), CHIP * j) if j else pick(values, chip) for j in range(n_chips)]

    def chip_sum(values):
        return sum(part.astype(F32) for part in chip_swap(values))

    def fetch_near(own, *widths):
        widths = widths or (own.shape[1],)
        return call(
            couple_kernel,
            [sds((2, own.shape[0], width), BF16) for width in widths],
            move(own, to_same),
            move(own, to_other),
            scalars=place,
            kept=tuple(range(len(widths))),
            name="couple",
        )

    def fetch_chips(pair):
        if n_chips > 8:
            return [chip_gather(pair)]
        return send_chips([pair] * n_chips, pair.shape[2] < 2 * units)

    def send_chips(parts, at_once=False):
        if at_once:
            return [parts[0]] + [xor(parts[j], CHIP * j) for j in range(1, n_chips)]
        out = [parts[0]] + [xor(parts[j], CHIP * j) for j in range(1, min(3, n_chips))]
        return out + [xor(gate(parts[j], *out[1:]), CHIP * j) for j in range(3, n_chips)]

    def join(parts):
        if n_chips > 8:
            joined, extra = parts[0][:, :, :shard], parts[0][:, :, shard:]
        else:
            height, width = parts[0].shape[1:]
            out = [sds((n_chips, 2, shard, width), BF16)]
            if height > shard:
                out.append(sds((n_chips, 2, height - shard, width), BF16))
            joined, *extra = place_parts(
                join_moves, out, *parts, scalars=place, name="join", copies=len(out) * n_chips
            )
            extra = extra[0] if extra else None
        return joined.reshape(D, joined.shape[3]), extra

    def give_chips(parts, at_once=False):
        if n_chips > 8:
            return chip_swap(parts[0].reshape(n_chips, -1, parts[0].shape[1]))
        return send_chips(parts, at_once)

    def sum_given(parts, height, *after):
        width = sum(part.shape[1] for part in parts) // n_chips
        out = sds((height, width), BF16)
        return call(
            functools.partial(sum_parts_kernel, n_chips, shard),
            [out, out],
            *parts,
            scalars=place,
            after=after,
            stored=tuple(range(len(parts))),
            kept=(0, 1),
            name="sum_parts",
        )

    def give_near(low):
        return [move(low[0], to_same), move(low[1], from_other)]

    def all_rows(values):
        other = xor(values, PARITY)
        return (values, other, xor(values, CORE), xor(other, CORE))

    def sum_rows(keep, near, send):
        got = xor(send, CORE)
        return keep, got, xor((near + got[rows:].astype(F32)).astype(BF16), PARITY)

    cond_full = condition.astype(F32)
    cond_act = jax.nn.silu(cond_full).astype(BF16)
    (cond_pair,) = call(
        couple_kernel, [sds((2, 1, D), BF16)], cond_act, xor(cond_act, CORE), scalars=place, name="couple"
    )
    cond_every = chip_gather(cond_pair).reshape(n_dp, D)
    qv_bias, out_bias, down_bias, up_bias, up_weight, _ = lax.optimization_barrier(
        (qv_bias, out_bias, down_bias, up_bias, up_weight, cond_every)
    )
    moved = move(jnp.concatenate([tokens[0], cotangent[0]]), swap_core_half)
    qkv_own = jnp.transpose(qkv_weight, (0, 2, 1, 3))
    down_own = jnp.transpose(down_weight, (0, 2, 1))

    bias_len = 12 * piece + up_bias.shape[2]
    bias_vec = jnp.concatenate(
        [
            qv_bias.reshape(layers, 6 * piece),
            out_bias.reshape(layers, 3 * piece),
            down_bias.reshape(layers, 3 * piece),
            up_bias.reshape(layers, -1),
        ],
        axis=1,
    )
    bias_block = lax.dynamic_update_slice(jnp.zeros((16, D), BF16), bias_vec, (0, 0))
    def pack_block(layer):
        return call(
            functools.partial(pack_block_kernel, layer),
            [sds((shard, 4 * cols + 2 * units), BF16)],
            qkv_own,
            out_weight,
            up_weight,
            down_own,
            name="pack_block",
        )[0]

    (own_attention,) = call(
        pack_first_kernel, [sds((shard + 16, 4 * cols), BF16)], qkv_own, out_weight, bias_block, name="pack_first"
    )
    (own_mlp,) = call(pack_mlp_kernel, [sds((shard, 2 * units), BF16)], up_weight, down_own, name="pack_mlp")
    (pair_mlp,) = fetch_near(own_mlp)
    attention_weights = [None] * layers
    mlp_weights = [None] * layers
    (pair_attention,) = fetch_near(own_attention)

    cond_slice = lax.dynamic_slice_in_dim(cond_every, dp * shard, shard, 1)
    bias_at = lax.dynamic_update_slice(
        jnp.zeros((layers, 6, cols // HD, HD), F32), mod_bias.astype(F32), (0, 0, 0, dp * piece)
    ).reshape(layers, 6, cols)
    partial_mod = jnp.einsum("ld,ydkc->lykc", cond_slice, mod_weight, preferred_element_type=F32) + bias_at
    mod_sum = chip_sum(partial_mod.reshape((n_chips, 2) + partial_mod.shape[1:]))
    parts_first = fetch_chips(gate(pair_attention, partial_mod))
    mod_sum = gate(mod_sum, pair_mlp)
    attention_weights[0], bias_every = join(parts_first)
    mod_sum = mod_sum + xor(mod_sum, CORE)
    mod_own = pick(mod_sum, half)
    mod_far = pick(mod_sum, half ^ 1)
    quarters = [xor(mod_far if mask & HALF else mod_own, mask) if mask else mod_own for mask in range(4)]
    (modulation,) = call(
        assemble_kernel,
        [sds((layers, 6, D), F32)],
        *quarters,
        scalars=place,
        after=(pair_mlp,) + tuple(parts_first[1:]),
        name="assemble",
    )

    parts_attention = [None] * layers
    parts_mlp = [None] * layers
    parts_mlp[0] = fetch_chips(gate(pair_mlp, modulation))
    qkv_bias_all, wide_bias, up_bias_all = call(
        bias_kernel,
        [sds((layers, 1, 3 * cols), F32), sds((layers, 2, D), F32), sds((layers, 1, units), F32)],
        bias_every.reshape(n_dp * 16, D),
        scalars=place,
        name="bias",
    )
    cotan, d_mlp = call(
        turn_kernel, [sds((rows, D), F32), sds((rows, D), BF16)], moved, modulation[layers - 1], kept=(0,), name="turn"
    )
    d_mlp_rows = all_rows(d_mlp)

    full = 4 * rows
    keep_send = [sds((rows, D), F32), sds((rows, D), F32), sds((full // 2, D), BF16)]
    row_f32 = sds((rows, D), F32)
    row_bf16 = sds((rows, D), BF16)
    line = sds((1, D), F32)
    attention_flops = 2 * full * D * 4 * cols + 4 * full * full * cols
    mlp_flops = 4 * full * D * units

    def parts_of(width, extra=0):
        if n_chips > 8:
            return [sds((D, width), BF16)]
        return [sds((D // n_chips + extra, width), BF16)] * n_chips

    saved = []
    residual, far_residual, attn_in = call(
        enter_kernel,
        [row_f32, row_f32, row_bf16],
        moved,
        modulation[0],
        kept=(1,),
        after=(attention_weights[0],),
        name="enter",
    )
    for layer in range(layers):
        mod = modulation[layer]
        more = layer + 1 < layers
        attn_rows = all_rows(attn_in)
        if more:
            own_block = gate(pack_block(layer + 1), attn_rows[3])
            pair_attention, pair_mlp = fetch_near(own_block, 4 * cols, 2 * units)
            parts_attention[layer + 1] = fetch_chips(gate(pair_attention, parts_mlp[layer][-1]))
            parts_mlp[layer + 1] = fetch_chips(gate(pair_mlp, parts_attention[layer + 1][-1]))
        if layer:
            attention_weights[layer] = join(parts_attention[layer])[0]
        attn_x, qkv, att, *partial = call(
            attention_kernel,
            [sds((full, D), BF16), sds((full, 3 * cols), BF16), sds((full, cols), BF16)] + keep_send,
            *attn_rows,
            attention_weights[layer],
            qkv_bias_all[layer],
            wide_bias[layer, :1],
            flops=attention_flops,
            stored=(4,),
            kept=(0, 1, 2),
            name="attention",
        )
        partial[2] = gate(partial[2], *parts_mlp[layer][1:3])
        branch, far_middle, middle, mlp_in = call(
            middle_kernel,
            [row_f32, row_f32, row_f32, row_bf16],
            residual,
            mod,
            *sum_rows(*partial),
            kept=(0, 1),
            name="middle",
        )
        mlp_rows = all_rows(mlp_in)
        mlp_weights[layer] = join(parts_mlp[layer])[0]
        mlp_x, hidden, act, *partial = call(
            mlp_kernel,
            [sds((full, D), BF16), sds((full, units), F32), sds((full, units), BF16)] + keep_send,
            *mlp_rows,
            mlp_weights[layer],
            up_bias_all[layer],
            wide_bias[layer, 1:],
            flops=mlp_flops,
            stored=(4,),
            kept=(0, 1, 2),
            name="mlp",
        )
        if more:
            partial[2] = gate(partial[2], *parts_attention[layer + 1][1:3])
        arrived = sum_rows(*partial)
        saved.append((far_residual, attn_x, qkv, att, branch, far_middle, mlp_x, hidden, act))
        if more:
            arrived = (gate(arrived[0], parts_attention[layer + 1][-1]),) + arrived[1:]
            mlp_out, far_residual, residual, attn_in = call(
                next_kernel,
                [row_f32, row_f32, row_f32, row_bf16],
                middle,
                mod,
                *arrived,
                modulation[layer + 1],
                kept=(0, 1),
                name="next",
            )
            saved[-1] += (mlp_out,)
        else:
            output, d_gate_two = call(
                last_kernel, [row_bf16, line], middle, mod, *arrived, cotan, stored=(5,), name="last"
            )

    output = move(output, swap_core_half)
    flow = cotan
    mod_lines = [None] * layers
    vecs = [None] * layers
    low = [None] * layers
    near_packs = [None] * layers
    given_attention = [None] * layers
    given_mlp = [None] * layers
    vec_shape = sds((n_dp, bias_len), F32)
    for layer in reversed(range(layers)):
        far_residual, attn_x, qkv, att, branch, far_middle, mlp_x, hidden, act = saved[layer][:9]
        mod = modulation[layer]
        more = layer + 1 < layers
        if more:
            d_mlp_rows = all_rows(d_mlp)
        mlp_y, d_hidden, *partial = call(
            mlp_back_kernel,
            [sds((full, D), BF16), sds((full, units), BF16)] + keep_send,
            *d_mlp_rows,
            mlp_weights[layer],
            hidden,
            flops=mlp_flops,
            stored=(4, 5),
            kept=(0, 1),
            name="mlp_back",
        )
        if more:
            partial[2] = gate(partial[2], *given_mlp[layer + 1][1:3])
        arrived = sum_rows(*partial)
        *grad_mlp, vec_mlp = call(
            mlp_grad_kernel,
            parts_of(2 * units) + [vec_shape],
            mlp_y,
            mlp_x,
            d_hidden,
            act,
            flops=mlp_flops,
            scalars=place,
            scratch=[pltpu.VMEM((D, 2 * units), BF16)],
            stored=(0, 1, 2, 3),
            kept=(0,),
            name="mlp_grad",
        )
        arrived = (gate(arrived[0], grad_mlp[0], *(given_mlp[layer + 1][3:] if more else ())),) + arrived[1:]
        if more:
            grad_mlp = [gate(part, *given_attention[layer + 1][1:]) for part in grad_mlp]
        given_mlp[layer] = give_chips(grad_mlp)
        d_middle, d_branch, sums_mid = call(
            middle_back_kernel,
            [row_f32, row_bf16, sds((3, D), F32)],
            flow,
            mod,
            *arrived,
            far_middle,
            branch,
            stored=(5, 6) if more else (0, 5, 6),
            name="middle_back",
        )
        if more:
            d_branch = gate(d_branch, *given_attention[layer + 1][1:])
            low[layer + 1] = sum_given(list(given_attention[layer + 1]) + list(given_mlp[layer + 1]), shard)
            near_packs[layer + 1] = give_near(low[layer + 1])
        d_branch_rows = all_rows(d_branch)
        attn_y, d_qkv, *partial = call(
            attention_back_kernel,
            [sds((full, D), BF16), sds((full, 3 * cols), BF16)] + keep_send,
            *d_branch_rows,
            attention_weights[layer],
            qkv,
            flops=attention_flops * 2,
            stored=(4, 5),
            kept=(0, 1),
            name="attention_back",
        )
        if more:
            partial[2] = gate(partial[2], *given_mlp[layer][1:3], near_packs[layer + 1][0])
        arrived = sum_rows(*partial)
        *grad_attention, vecs[layer] = call(
            functools.partial(
                attention_grad_kernel if layer or n_chips > 8 else attention_grad_last_kernel,
                1 if n_chips > 8 else n_chips,
            ),
            parts_of(4 * cols, 0 if layer else 16) + [vec_shape],
            attn_y,
            attn_x,
            d_qkv,
            att,
            vec_mlp,
            *(() if layer or n_chips > 8 else (vecs[1],)),
            flops=attention_flops,
            scalars=place,
            scratch=[pltpu.VMEM((D, 4 * cols), BF16)],
            stored=(0, 1, 2, 3),
            kept=(0,),
            name="attention_grad",
        )
        after = (grad_attention[0],)
        if layer == 0:
            after = after + (output,) + tuple(given_mlp[0][3:]) + tuple(near_packs[upper][1] for upper in range(1, layers))
        if layer == 0:
            height = 2 * shard + 16
            if n_chips > 8:
                rows_bias = jnp.concatenate([vecs[i] for i in range(layers)], axis=1).astype(BF16)
                rows_bias = jnp.pad(
                    rows_bias.reshape(n_chips, 2, -1), ((0, 0), (0, 14), (0, 4 * cols - layers * bias_len))
                )
                rows_all = jnp.concatenate(
                    [grad_attention[0].reshape(n_chips, 2 * shard, 4 * cols), rows_bias], axis=1
                )
                grad_attention = [rows_all.reshape(n_chips * height, 4 * cols)]
        given_attention[layer] = give_chips([gate(part, *given_mlp[layer][1:]) for part in grad_attention], True)
        if layer:
            flow, sums_in, d_mlp, gate_next = call(
                previous_kernel,
                [row_f32, sds((2, D), F32), row_bf16, line],
                d_middle,
                mod,
                *arrived,
                far_residual,
                modulation[layer - 1],
                saved[layer - 1][9],
                stored=(5, 7),
                after=after,
                name="previous",
            )
        else:
            flow, sums_in = call(
                enter_back_kernel,
                [row_f32, sds((2, D), F32)],
                d_middle,
                mod,
                *arrived,
                far_residual,
                stored=(5,),
                after=after,
                name="enter_back",
            )
            gate_next = None
        mod_lines[layer] = jnp.concatenate([sums_in, sums_mid, d_gate_two], axis=0)
        d_gate_two = gate_next

    d_mod = jnp.stack(mod_lines)
    d_mod = d_mod + xor(d_mod, CORE)
    d_mod = (d_mod + xor(d_mod, PARITY)).astype(BF16).reshape(layers * 6, 4, cols)
    d_mod = jnp.transpose(d_mod, (1, 0, 2))
    mine = pick(d_mod, z)
    far = xor(pick(d_mod, z ^ HALF), HALF)
    d_mod_pair = jnp.where(half == 0, jnp.stack([mine, far]), jnp.stack([far, mine]))
    low_attention = sum_given(list(given_attention[0]), shard + 16)
    near_attention = give_near(low_attention)
    near_mlp = give_near(sum_given(list(given_mlp[0]), shard))
    near_packs[0] = near_attention + near_mlp
    d_mod_pair = gate(d_mod_pair, *given_attention[0][1:])
    d_mod_every = gate(chip_gather(d_mod_pair), *near_mlp).reshape(n_dp, layers, 6, cols)
    grad_mod_w = jnp.einsum("ld,lykc->ykdc", cond_slice, d_mod_every, preferred_element_type=F32)
    grad_mod_w = jnp.transpose(grad_mod_w, (0, 2, 1, 3))
    grad_mod_b = jnp.sum(d_mod_every.astype(F32), axis=0).reshape(layers, 6, cols // HD, HD)
    grad_mod_b = lax.dynamic_slice_in_dim(grad_mod_b, dp * piece, piece, 3)
    cond_pieces = jnp.einsum("lykc,ydkc->ld", d_mod_every, mod_weight, preferred_element_type=F32)
    mixed = jnp.stack(chip_swap(cond_pieces.reshape(n_chips, 2, shard)))
    if n_chips <= 8:
        mixed = jnp.take(mixed, chip ^ jnp.arange(n_chips), axis=0)
    cond_pieces = jnp.transpose(mixed, (1, 0, 2))
    cond_pieces = gate(cond_pieces, *low_attention)
    cond_mine = pick(cond_pieces, core)
    cond_sent = xor(pick(cond_pieces, core ^ 1), CORE)
    cond_total = jnp.where(
        core == 0, jnp.stack([cond_mine, cond_sent], axis=1), jnp.stack([cond_sent, cond_mine], axis=1)
    ).reshape(1, D)
    cond_total = cond_total + xor(cond_total, PARITY)
    cond_total = gate(cond_total + xor(cond_total, HALF), *near_attention)
    sigmoid_cond = jax.nn.sigmoid(cond_full)
    grad_condition = cond_total * sigmoid_cond * (1.0 + cond_full * (1.0 - sigmoid_cond))

    grad_tokens = move(gate(flow, cond_mine), swap_core_half)
    output, grad_tokens, grad_qkv, grad_out, grad_up, grad_down, vec = call(
        finish_kernel,
        [
            row_bf16,
            row_f32,
            sds((layers, 3, shard, cols), F32),
            sds((layers, cols, shard), F32),
            sds((layers, shard, units), F32),
            sds((layers, shard, units), F32),
            sds((8, 4 * cols), F32),
        ],
        output,
        grad_tokens,
        *[part for layer in range(layers) for part in near_packs[layer]],
        kept=(0, 1, 2, 3, 4, 5),
        name="finish",
    )
    vec = vec[0, : layers * bias_len].reshape(layers, bias_len)
    vec_heads = vec[:, : 12 * piece].reshape(layers, 4, 3, piece)
    return (
        output[None],
        grad_tokens[None],
        grad_condition,
        grad_mod_w,
        grad_mod_b,
        jnp.transpose(grad_qkv, (0, 2, 1, 3)),
        vec_heads[:, :2],
        grad_out,
        vec_heads[:, 2],
        grad_up,
        vec[:, 12 * piece :].reshape(layers, 1, -1),
        jnp.transpose(grad_down, (0, 2, 1)),
        vec_heads[:, 3],
    )


def solution(mesh):
    in_specs = (
        P("dp", "tensor", None),
        P("dp", None),
        P("dp", "tensor", None),
        P(None, "dp", None, "tensor"),
        P(None, None, "tensor", "dp"),
        P(None, "dp", None, "tensor"),
        P(None, None, "tensor", "dp"),
        P(None, "tensor", "dp"),
        P(None, "tensor", "dp"),
        P(None, "dp", "tensor"),
        P(None, "tensor", "dp"),
        P(None, "tensor", "dp"),
        P(None, "tensor", "dp"),
    )
    out_specs = (
        P("dp", "tensor", None),
        P("dp", "tensor", None),
        P("dp", None),
        P(None, "dp", None, "tensor"),
        P(None, None, "tensor", "dp"),
        P(None, "dp", None, "tensor"),
        P(None, None, "tensor", "dp"),
        P(None, "tensor", "dp"),
        P(None, "tensor", "dp"),
        P(None, "dp", "tensor"),
        P(None, "tensor", "dp"),
        P(None, "tensor", "dp"),
        P(None, "tensor", "dp"),
    )
    return jax.shard_map(body, mesh=mesh, in_specs=in_specs, out_specs=out_specs, check_vma=False)
```
